32 devices in a mesh: dp: 8 (over z, y), tensor: 4 (over x, core).
Axes of the slice: x: 2, y: 2, z: 4, core: 2. Of those that a mesh axis runs over, the one named last changes fastest.
Arguments:
- h_in: bfloat16 [8192, 768], P(('dp', 'tensor')), may hold values from -6 to 6
- g_in: bfloat16 [8192, 768], P(('dp', 'tensor')), may hold values from -6 to 6
- lengths: int32 [16, 4], P('dp'), may hold values from 1 to 384, 512 in all within a row
- order: int32 [16, 512], P('dp'), may hold values from 0 to 511, each once within a row
- predicted: int32 [16, 512], P('dp'), may hold values 0 or 1
- w_query: bfloat16 [2, 768, 768], P(None, 'dp', 'tensor'), may hold values from -0.21875 to 0.21875
- w_key: bfloat16 [2, 768, 768], P(None, 'dp', 'tensor'), may hold values from -0.21875 to 0.21875
- w_value: bfloat16 [2, 768, 768], P(None, 'dp', 'tensor'), may hold values from -0.21875 to 0.21875
- w_out: bfloat16 [2, 768, 768], P(None, 'tensor', 'dp'), may hold values from -0.625 to 0.625
- w_up: bfloat16 [2, 768, 3072], P(None, 'dp', 'tensor'), may hold values from -0.21875 to 0.21875
- w_down: bfloat16 [2, 3072, 768], P(None, 'tensor', 'dp'), may hold values from -0.109375 to 0.109375
- q_bias: float32 [2, 768], P(None, 'tensor'), may hold values from -3 to 3
- v_bias: float32 [2, 768], P(None, 'tensor'), may hold values from -3 to 3
- up_bias: float32 [2, 3072], P(None, 'tensor'), may hold values from -3 to 3
- rel_table: float32 [2, 12, 32], P(None, 'tensor'), may hold values from -4 to 4
- norm_gain: float32 [2, 2, 768], replicated, may hold values from 0.5 to 1.5
- norm_shift: float32 [2, 2, 768], replicated, may hold values from -2 to 2
- out_bias: float32 [2, 2, 768], replicated, may hold values from -2 to 2
- h_cot: bfloat16 [8192, 768], P(('dp', 'tensor')), may hold values from -6 to 6
- g_cot: bfloat16 [8192, 768], P(('dp', 'tensor')), may hold values from -6 to 6
Outputs:
- h_out: bfloat16 [8192, 768], P(('dp', 'tensor'))
- g_out: bfloat16 [8192, 768], P(('dp', 'tensor'))
- h_grad: bfloat16 [8192, 768], P(('dp', 'tensor'))
- g_grad: bfloat16 [8192, 768], P(('dp', 'tensor'))
- w_query_grad: float32 [2, 768, 768], P(None, 'dp', 'tensor')
- w_key_grad: float32 [2, 768, 768], P(None, 'dp', 'tensor')
- w_value_grad: float32 [2, 768, 768], P(None, 'dp', 'tensor')
- w_out_grad: float32 [2, 768, 768], P(None, 'tensor', 'dp')
- w_up_grad: float32 [2, 768, 3072], P(None, 'dp', 'tensor')
- w_down_grad: float32 [2, 3072, 768], P(None, 'tensor', 'dp')
- q_bias_grad: float32 [2, 768], P(None, 'tensor')
- v_bias_grad: float32 [2, 768], P(None, 'tensor')
- up_bias_grad: float32 [2, 3072], P(None, 'tensor')
- rel_table_grad: float32 [2, 12, 32], P(None, 'tensor')
- norm_gain_grad: float32 [2, 2, 768], replicated
- norm_shift_grad: float32 [2, 2, 768], replicated
- out_bias_grad: float32 [2, 2, 768], replicated
The draws below stay inside these ranges and needn't reach their ends.
Inputs may be any that keep to these rules, and one draw needn't show every extreme that they name: Row s lists the lengths of the 3 documents of slot s in order and, last, the slot's padding; each row sums to 512. `order`: each row is a permutation of 0 to 511.
All inputs are finite; a program needn't handle non-finite values. No bound on the sum of `predicted` on one device may be relied on, other than what follows from the above.
Results may differ from the reference program's by a relative error of at most 0.03.
Values may be sent and summed in bfloat16 or wider, within the bound.
No kernel may reach another device: no remote copies, remote signals or barrier semaphores. Data moves between devices by JAX's collectives and lax.ppermute only.
A program may use at most 192 MiB of HBM per device.

```python
import math
import jax
import jax.numpy as jnp
import numpy as np
from jax import lax

HEADS = 12
HEAD = 64
D = 768
FF = 3072
BUCKETS = 32
LAYERS = 2
SEQ = 512
PIECES = 4
MOST = 384
SLOTS = 16
TOKENS = 8192


def plant(drawn, key, least, largest):
    dims = drawn.shape
    place = [jax.random.randint(jax.random.fold_in(key, axis), (), 0, dims[axis]) for axis in range(len(dims))]
    drawn = drawn.at[tuple(place)].set(least)
    longest = dims.index(max(dims))
    place[longest] = (place[longest] + 1) % dims[longest]
    return drawn.at[tuple(place)].set(largest)


def levels(rng, shape, cuts, smallest, top_value):
    level, own = 1.0, jax.random.fold_in(rng, 6)
    for dim, blocks in cuts:
        draws = jnp.exp(jax.random.uniform(jax.random.fold_in(own, dim), (blocks,), jnp.float32, smallest / len(cuts), top_value / len(cuts)))
        level = level * jnp.repeat(draws, shape[dim] // blocks).reshape([-1 if axis == dim else 1 for axis in range(len(shape))])
    return level


def profile(count, total, limit, slope):
    portions = [(1 << 20) // math.isqrt(grade ** slope) + 1 for grade in range(2, count + 1)]
    rest, given = total - limit - (count - 1), [1] * (count - 1)
    while rest > 0:
        movable = [i for i in range(count - 1) if given[i] < limit]
        mass, left = sum([portions[i] for i in movable]), rest
        for i in movable:
            more = min(limit - given[i], max(1, left * portions[i] // mass), rest)
            given[i] = given[i] + more
            rest = rest - more
    return np.array([limit] + given)


def uneven(key, number_of, total, most, slope):
    if number_of == 2:
        one = jax.random.randint(key, (), max(1, total - most), min(most, total - 1) + 1)
        return jnp.stack([one, total - one])
    sizes = jnp.asarray(profile(number_of, total, most, slope), jnp.int32)
    pairs = (number_of - 1) // 2
    source_of, receiver = sizes[1:1 + 2 * pairs:2], sizes[2:2 + 2 * pairs:2]
    margin = jnp.minimum(source_of - 1, most - receiver)
    passed = jax.random.randint(jax.random.fold_in(key, 1), (pairs,), 0, 1 << 20) % (margin + 1)
    sizes = sizes.at[1:1 + 2 * pairs:2].set(source_of - passed).at[2:2 + 2 * pairs:2].set(receiver + passed)
    return sizes[jax.random.permutation(jax.random.fold_in(key, 2), number_of)]


def normal_values(stream_key, shape, scale, reach, shards=(), held_as=jnp.bfloat16):
    loudness = levels(stream_key, shape, shards, -0.22, 0.18) if shards else 1.0
    result = jax.random.normal(stream_key, shape, jnp.float32) * scale * loudness
    return jnp.minimum(jnp.maximum(result, -reach), reach).astype(held_as)


def setup_inputs(seed: int = 0) -> dict:
    splits = jax.random.split(jax.random.key(seed), 21)
    return {
        "h_in": normal_values(splits[0], (TOKENS, D), 1.0, 6.0, ((0, 32),)),
        "g_in": normal_values(splits[1], (TOKENS, D), 1.0, 6.0, ((0, 32),)),
        "lengths": jax.vmap(lambda own: uneven(own, PIECES, SEQ, MOST, 2))(jax.random.split(splits[2], SLOTS)).reshape((SLOTS, PIECES)).astype(jnp.int32),
        "order": jax.vmap(lambda own: jax.random.permutation(own, SEQ))(jax.random.split(splits[3], SLOTS)).reshape((SLOTS, SEQ)).astype(jnp.int32),
        "predicted": plant((jax.random.randint(splits[4], (SLOTS, SEQ), 0, 20) < 3).astype(jnp.int32), jax.random.fold_in(splits[4], 1), 0, 1),
        "w_query": normal_values(splits[5], (LAYERS, D, D), D ** -0.5, 0.21875, ((1, 8), (2, 4))),
        "w_key": normal_values(splits[6], (LAYERS, D, D), D ** -0.5, 0.21875, ((1, 8), (2, 4))),
        "w_value": normal_values(splits[7], (LAYERS, D, D), D ** -0.5, 0.21875, ((1, 8), (2, 4))),
        "w_out": normal_values(splits[8], (LAYERS, D, D), (D // 8) ** -0.5, 0.625, ((1, 4), (2, 8))),
        "w_up": normal_values(splits[9], (LAYERS, D, FF), D ** -0.5, 0.21875, ((1, 8), (2, 4))),
        "w_down": normal_values(splits[10], (LAYERS, FF, D), FF ** -0.5, 0.109375, ((1, 4), (2, 8))),
        "q_bias": normal_values(splits[11], (LAYERS, D), 0.5, 3.0, ((1, 4),), jnp.float32),
        "v_bias": normal_values(splits[12], (LAYERS, D), 0.5, 3.0, ((1, 4),), jnp.float32),
        "up_bias": normal_values(splits[13], (LAYERS, FF), 0.5, 3.0, ((1, 4),), jnp.float32),
        "rel_table": normal_values(splits[14], (LAYERS, HEADS, BUCKETS), 1.0, 4.0, ((1, 4),), jnp.float32),
        "norm_gain": jnp.clip(1.0 + 0.1 * jax.random.normal(splits[15], (LAYERS, 2, D), jnp.float32), 0.5, 1.5),
        "norm_shift": normal_values(splits[16], (LAYERS, 2, D), 0.3, 2.0, (), jnp.float32),
        "out_bias": normal_values(splits[17], (LAYERS, 2, D), 0.3, 2.0, (), jnp.float32),
        "h_cot": normal_values(splits[18], (TOKENS, D), 1.0, 6.0, ((0, 32),)),
        "g_cot": normal_values(splits[19], (TOKENS, D), 1.0, 6.0, ((0, 32),)),
    }


@jax.custom_vjp
def low(v):
    return lax.optimization_barrier(v.astype(jnp.bfloat16)).astype(jnp.float32)

@jax.custom_vjp
def low_back(v):
    return v

def low_keep(v):
    return (low(v), None)

def low_pass(kept, grad):
    return (grad,)

def back_keep(v):
    return (v, None)

def back_low(kept, grad):
    return (low(grad),)
low.defvjp(low_keep, low_pass)
low_back.defvjp(back_keep, back_low)
epsilon = 1e-05
limits = (12, 16, 23, 32, 46, 64, 91)
highest = lax.Precision.HIGHEST

def product(left, right):
    return jnp.dot(left, right, precision=highest, preferred_element_type=jnp.float32)

def bucket_of(offset):
    distance = jnp.abs(offset)
    farther = 8 + sum(((distance >= border).astype(jnp.int32) for border in limits))
    return jnp.where(distance < 8, distance, farther) + 16 * (offset > 0).astype(jnp.int32)

def slot_masks(piece_lengths, ranks, chosen):
    places = jnp.arange(SEQ, dtype=jnp.int32)
    borders = jnp.cumsum(piece_lengths).astype(jnp.int32)[:-1]
    segment = lax.optimization_barrier(jnp.sum((places[:, None] >= borders[None, :]).astype(jnp.int32), axis=1)).astype(jnp.int32)
    starts = jnp.concatenate([jnp.zeros((1,), jnp.int32), borders])
    pieces = jnp.arange(starts.shape[0], dtype=jnp.int32)
    leading = lax.optimization_barrier(jnp.sum(jnp.where(segment[:, None] == pieces[None, :], starts[None, :], 0), axis=1))
    same_doc = segment[:, None] == segment[None, :]
    visible = chosen[None, :] == 0
    content_mask = same_doc & (visible | (ranks[None, :] <= ranks[:, None]))
    query_mask = same_doc & ((places[None, :] == leading[:, None]) | visible & (places[None, :] != places[:, None]) | (ranks[None, :] < ranks[:, None]))
    return (content_mask, query_mask)

def norm_rows(rows, gain, shift):
    center = rows - lax.optimization_barrier(jnp.mean(rows, axis=-1, keepdims=True))
    spread = lax.optimization_barrier(jnp.mean(center * center, axis=-1, keepdims=True))
    return center * lax.rsqrt(spread + epsilon) * gain + shift

def attend(queries, keys, values, allowed, bias):
    scores = jnp.einsum('qhe,khe->hqk', queries, keys, precision=highest) * 0.125 + bias
    scores = low_back(scores)
    scores = jnp.where(allowed[None], scores, -1e+30)
    maxima = lax.optimization_barrier(jnp.max(scores, axis=-1, keepdims=True))
    raised = jnp.exp(scores - maxima)
    probs = low(raised / lax.optimization_barrier(jnp.sum(raised, axis=-1, keepdims=True)))
    return jnp.einsum('hqk,khe->qhe', probs, values, precision=highest)

def slot_pair(bias):

    def inner(items):
        query_h, query_g, keys, values, content_mask, query_mask = items
        return (attend(query_h, keys, values, content_mask, bias), attend(query_g, keys, values, query_mask, bias))
    return jax.checkpoint(inner)

def layer_forward(current_h, current_g, weights, content_masks, query_masks, onehot):
    query_weight, key_weight, value_weight, out_weight, up_weight, down_weight, query_bias, value_bias, up_shift, table, gains, shifts, biases = weights
    slots = content_masks.shape[0]
    sent_h = low(current_h)
    sent_g = low(current_g)
    query_h = low_back(low(product(sent_h, query_weight) + query_bias))
    query_g = low_back(low(product(sent_g, query_weight) + query_bias))
    keys = low_back(low(product(sent_h, key_weight)))
    values = low_back(low(product(sent_h, value_weight) + value_bias))
    bias = jnp.einsum('bij,hb->hij', onehot, table, precision=highest)

    def to_heads(block):
        return block.reshape(slots, SEQ, HEADS, HEAD)
    mixed_h, mixed_g = lax.map(slot_pair(bias), (to_heads(query_h), to_heads(query_g), to_heads(keys), to_heads(values), content_masks, query_masks))
    mixed_h = low_back(low(mixed_h.reshape(-1, D)))
    mixed_g = low_back(low(mixed_g.reshape(-1, D)))
    before_h = current_h + low_back(product(mixed_h, out_weight)) + biases[0]
    before_g = current_g + low_back(product(mixed_g, out_weight)) + biases[0]
    normed_h = norm_rows(before_h, gains[0], shifts[0])
    normed_g = norm_rows(before_g, gains[0], shifts[0])
    inner_h = low_back(product(low(normed_h), up_weight) + up_shift)
    inner_g = low_back(product(low(normed_g), up_weight) + up_shift)
    act_h = low(jax.nn.gelu(inner_h, approximate=True))
    act_g = low(jax.nn.gelu(inner_g, approximate=True))
    after_h = normed_h + low_back(product(act_h, down_weight)) + biases[1]
    after_g = normed_g + low_back(product(act_g, down_weight)) + biases[1]
    return (norm_rows(after_h, gains[1], shifts[1]), norm_rows(after_g, gains[1], shifts[1]))

def reference(h_in, g_in, lengths, order, predicted, w_query, w_key, w_value, w_out, w_up, w_down, q_bias, v_bias, up_bias, rel_table, norm_gain, norm_shift, out_bias, h_cot, g_cot):
    content_masks, query_masks = jax.vmap(slot_masks)(lengths, order, predicted)
    places = jnp.arange(SEQ, dtype=jnp.int32)
    buckets = bucket_of(places[None, :] - places[:, None])
    onehot = (jnp.arange(BUCKETS, dtype=jnp.int32)[:, None, None] == buckets[None]).astype(jnp.float32)

    def forward(current_h, current_g, params):
        for layer in range(LAYERS):
            weights = tuple((member[layer] for member in params))
            current_h, current_g = layer_forward(current_h, current_g, weights, content_masks, query_masks, onehot)
        return (current_h, current_g)
    params = tuple((member.astype(jnp.float32) for member in (w_query, w_key, w_value, w_out, w_up, w_down, q_bias, v_bias, up_bias, rel_table, norm_gain, norm_shift, out_bias)))
    outputs, pull = jax.vjp(forward, h_in.astype(jnp.float32), g_in.astype(jnp.float32), params)
    grad_h, grad_g, grads = pull((h_cot.astype(jnp.float32), g_cot.astype(jnp.float32)))
    return (outputs[0].astype(jnp.bfloat16), outputs[1].astype(jnp.bfloat16), grad_h.astype(jnp.bfloat16), grad_g.astype(jnp.bfloat16), grads[0], grads[1], grads[2], grads[3], grads[4], grads[5], grads[6], grads[7], grads[8], grads[9], grads[10], grads[11], grads[12])
```

```python
import jax
import jax.numpy as jnp
from jax import lax
from jax.sharding import Mesh, PartitionSpec as P

HEAD = 64
BUCKETS = 32
LAYERS = 2
SEQ = 512

epsilon = 1e-05
limits = (12, 16, 23, 32, 46, 64, 91)
highest = lax.Precision.HIGHEST
f32 = jnp.float32
bf16 = jnp.bfloat16
SWAP = [(0, 1), (1, 0)]


def dot(left, right, numbers):
    return lax.dot_general(left, right, (numbers, ((), ())), preferred_element_type=f32)


def nn(left, right):
    return dot(left, right, ((1,), (0,)))


def nt(left, right):
    return dot(left, right, ((1,), (1,)))


def tn(left, right):
    return dot(left, right, ((0,), (0,)))


def bucket_of(offset):
    distance = jnp.abs(offset)
    farther = 8 + sum(((distance >= border).astype(jnp.int32) for border in limits))
    return jnp.where(distance < 8, distance, farther) + 16 * (offset > 0).astype(jnp.int32)


def slot_masks(piece_lengths, ranks, chosen):
    places = jnp.arange(SEQ, dtype=jnp.int32)
    first = piece_lengths[0]
    second = first + piece_lengths[1]
    third = second + piece_lengths[2]
    segment = (
        (places >= first).astype(jnp.int32)
        + (places >= second).astype(jnp.int32)
        + (places >= third).astype(jnp.int32)
    )
    leading = jnp.where(
        segment == 0,
        0,
        jnp.where(segment == 1, first, jnp.where(segment == 2, second, third)),
    )
    same_doc = segment[:, None] == segment[None, :]
    visible = chosen[None, :] == 0
    content_mask = same_doc & (visible | (ranks[None, :] <= ranks[:, None]))
    query_mask = same_doc & (
        (places[None, :] == leading[:, None])
        | visible & (places[None, :] != places[:, None])
        | (ranks[None, :] < ranks[:, None])
    )
    return (content_mask, query_mask)


class Links:
    def __init__(self, mesh):
        dp = mesh.shape["dp"]
        self.routed = dp == 8
        self.ny = 2
        self.nz = dp // 2
        self.nx = mesh.shape["tensor"] // 2
        self.mesh = Mesh(
            mesh.devices.reshape(self.nz, self.ny, self.nx, 2), ("z", "y", "x", "core")
        )
        self.ring = [(i, (i + 1) % self.nz) for i in range(self.nz)]

    def px(self, v):
        return lax.ppermute(v, "x", SWAP)

    def py(self, v):
        return lax.ppermute(v, "y", SWAP)

    def pz(self, v):
        return lax.ppermute(v, "z", self.ring)

    def pc(self, v):
        return lax.ppermute(v, "core", SWAP)

    def feature_order(self, width):
        count = self.nz * self.ny
        depth = width // count
        place = jnp.arange(width, dtype=jnp.int32)
        if not self.routed:
            return place
        block, rest = place // depth, place % depth
        ky, kz = block // self.nz, block % self.nz
        z = lax.rem(lax.axis_index("z") - kz + self.nz, self.nz)
        y = jnp.bitwise_xor(lax.axis_index("y"), ky)
        return (z * self.ny + y) * depth + rest

    def gather(self, block, route):
        if not self.routed:
            rows = lax.all_gather(block, ("z", "y"), axis=0, tiled=True)
            return lax.all_gather(rows, "x", axis=0)
        if route == "xzy":
            held = [jnp.stack([block, self.px(block)])]
            for _ in range(self.nz - 1):
                held.append(self.pz(held[-1]))
            return jnp.concatenate(held + [self.py(h) for h in held], axis=1)
        if route == "yzx":
            held = [jnp.concatenate([block, self.py(block)])]
            depth = block.shape[0]
            for _ in range(self.nz - 1):
                held.append(self.pz(held[-1]))
            other = [self.px(h) for h in held]
            return jnp.stack(
                [
                    jnp.concatenate([h[:depth] for h in s] + [h[depth:] for h in s])
                    for s in (held, other)
                ]
            )
        held = [block]
        for _ in range(self.nz - 1):
            held.append(self.pz(held[-1]))
        held = [jnp.stack([h, self.px(h)]) for h in held]
        return jnp.concatenate(held + [self.py(h) for h in held], axis=1)

    def scatter(self, grad, route):
        if not self.routed:
            mine = lax.psum_scatter(grad, "x", scatter_dimension=0, tiled=False)
            return lax.psum_scatter(
                mine, ("z", "y"), scatter_dimension=0, tiled=True
            ).astype(f32)
        depth = grad.shape[1] // (self.ny * self.nz)
        g = grad.reshape(2, self.ny, self.nz, depth, grad.shape[2])

        def ring(parts):
            acc = parts(1).astype(bf16)
            for k in range(2, self.nz):
                acc = (parts(k) + self.pz(acc).astype(f32)).astype(bf16)
            return parts(0) + self.pz(acc).astype(f32)

        def both(a, b):
            return a.astype(f32) + b.astype(f32)

        if route == "yzx":
            got = self.py(g[:, 1])
            done = ring(lambda k: both(g[:, 0, k], got[:, k]))
            return done[0] + self.px(done[1].astype(bf16)).astype(f32)
        if route == "xzy":
            got = self.px(g[1])
            done = ring(lambda k: both(g[0, :, k], got[:, k]))
            return done[0] + self.py(done[1].astype(bf16)).astype(f32)
        got = self.py(g[:, 1])
        more = self.px(both(g[1, 0], got[1]).astype(bf16))
        return ring(lambda k: both(g[0, 0, k], got[0, k]) + more[k].astype(f32))

    def pair(self, v):
        if not self.routed:
            return lax.all_gather(v, "x", axis=0)
        return jnp.stack([v, self.px(v)])

    def total(self, split, whole):
        if not self.routed:
            mine = lax.psum_scatter(split, "x", scatter_dimension=0, tiled=False)
            return lax.psum(mine, ("z", "y")), lax.psum(whole, ("z", "y", "x"))
        n = split.shape[1]
        count = n + whole.shape[0]
        filler = jnp.zeros((-count % 128,), f32)
        sent = jnp.concatenate([split[1], whole, filler]).reshape(-1, 128)
        kept = jnp.concatenate([split[0], whole, filler]).reshape(-1, 128)
        v = kept + self.px(sent)
        v = v + self.py(v)
        step = 1
        while step < self.nz:
            v = v + lax.ppermute(v, "z", [(i, i ^ step) for i in range(self.nz)])
            step *= 2
        v = v.reshape(-1)
        return v[:n], v[n:count]

    def both_rows(self, v):
        other = self.pc(v)
        first = lax.axis_index("core") == 0
        return jnp.concatenate([jnp.where(first, v, other), jnp.where(first, other, v)])


def norm_rows(rows, gain, shift):
    center = rows - jnp.mean(rows, axis=-1, keepdims=True)
    spread = jnp.mean(center * center, axis=-1, keepdims=True)
    return center * lax.rsqrt(spread + epsilon) * gain + shift


def norm_back(rows, gain, shift, grad):
    unused, pull = jax.vjp(norm_rows, rows, gain, shift)
    return pull(grad)


def smooth(inner):
    return jax.nn.gelu(inner, approximate=True)


def smooth_back(inner, grad):
    unused, pull = jax.vjp(smooth, inner)
    return pull(grad)[0]


def masked_scores(queries, keys, allowed, bias):
    scores = jnp.einsum("hqe,hke->hqk", queries, keys, preferred_element_type=f32) * 0.125 + bias
    return jnp.where(allowed[None], scores, -1e30)


def attend(queries, keys, values, allowed, bias):
    scores = masked_scores(queries, keys, allowed, bias)
    maxima = jnp.max(scores, axis=-1, keepdims=True)
    raised = jnp.exp(scores - maxima)
    total = jnp.sum(raised, axis=-1, keepdims=True)
    probs = (raised / total).astype(bf16)
    result = jnp.einsum("hqk,hke->hqe", probs, values, preferred_element_type=f32)
    return (result.astype(bf16), (maxima + jnp.log(total))[..., 0])


def attend_back(queries, keys, values, allowed, bias, logsum, grad_out):
    scores = masked_scores(queries, keys, allowed, bias)
    probs = jnp.where(allowed[None], jnp.exp(scores - logsum[..., None]), 0.0)
    grad_probs = jnp.einsum("hqe,hke->hqk", grad_out, values, preferred_element_type=f32)
    inner = jnp.sum(probs * grad_probs, axis=-1, keepdims=True)
    grad_scores = (probs * (grad_probs - inner)).astype(bf16)
    grad_query = jnp.einsum("hqk,hke->hqe", grad_scores, keys, preferred_element_type=f32) * 0.125
    grad_keys = jnp.einsum("hqk,hqe->hke", grad_scores, queries, preferred_element_type=f32) * 0.125
    grad_values = jnp.einsum(
        "hqk,hqe->hke", probs.astype(bf16), grad_out, preferred_element_type=f32
    )
    return (grad_query, grad_keys, grad_values, grad_scores)


def heads_of(block):
    rows, width = block.shape
    return block.reshape(rows, width // HEAD, HEAD).transpose(1, 0, 2)


def rows_of(block):
    heads, rows, head = block.shape
    return block.transpose(1, 0, 2).reshape(rows, heads * head)


def local(links, *arguments):
    (
        h_in,
        g_in,
        lengths,
        order,
        predicted,
        w_query,
        w_key,
        w_value,
        w_out,
        w_up,
        w_down,
        q_bias,
        v_bias,
        up_bias,
        rel_table,
        norm_gain,
        norm_shift,
        out_bias,
        h_cot,
        g_cot,
    ) = arguments
    rows_own, model = h_in.shape
    part = w_query.shape[2]
    units = w_up.shape[2]
    table_size = rel_table.shape[1] * BUCKETS
    slot = lax.axis_index("x")
    core = lax.axis_index("core")

    routes = (("zxy", "xzy", "yzx"), ("zxy", "xzy", "yzx"))
    blocks = []
    for layer in range(LAYERS):
        attn = jnp.concatenate(
            [w_query[layer], w_key[layer], w_value[layer], w_out[layer].T], axis=1
        )
        blocks.append((attn, w_up[layer], w_down[layer].T))
    gathered = [
        [links.gather(b, r) for b, r in zip(blocks[layer], routes[layer])]
        for layer in range(LAYERS)
    ]

    def pick(v):
        return lax.dynamic_index_in_dim(v, slot, 0, keepdims=False)

    content_mask, query_mask = slot_masks(pick(lengths), pick(order), pick(predicted))
    places = jnp.arange(SEQ, dtype=jnp.int32)
    buckets = bucket_of(places[None, :] - places[:, None])
    onehot = (jnp.arange(BUCKETS, dtype=jnp.int32)[:, None, None] == buckets[None]).astype(f32)

    small = links.pair(
        jnp.concatenate(
            [q_bias, v_bias, up_bias, rel_table.reshape(LAYERS, table_size)], axis=1
        )
    )
    features = links.feature_order(model)
    swapper = (jnp.arange(model, dtype=jnp.int32)[:, None] == features[None, :]).astype(bf16)
    swapper32 = swapper.astype(f32)

    entering = links.both_rows(jnp.concatenate([h_in, g_in], axis=1))
    leaving = links.both_rows(jnp.concatenate([h_cot, g_cot], axis=1))

    def ordered(rows):
        return nn(rows, swapper)

    params = jnp.dot(
        jnp.concatenate([norm_gain, norm_shift, out_bias], axis=1).reshape(-1, model),
        swapper32,
        precision=highest,
    ).reshape(LAYERS, 3, 2, model)

    current_h = ordered(entering[:, :model])
    current_g = ordered(entering[:, model:])
    kept = []
    for layer in range(LAYERS):
        attn, up, down = gathered[layer]
        own = small[:, layer]
        bias_q = own[:, :part].reshape(-1)
        bias_v = own[:, part : 2 * part].reshape(-1)
        bias_up = own[:, 2 * part : 2 * part + units].reshape(-1)
        table = own[:, 2 * part + units :].reshape(-1, BUCKETS)
        wq, wk, wv, wo = (
            jnp.concatenate([attn[i, :, part * n : part * (n + 1)] for i in range(2)], axis=1)
            for n in range(4)
        )
        wu = jnp.concatenate([up[0], up[1]], axis=1)
        wd = jnp.concatenate([down[0], down[1]], axis=1)
        gains, shifts, biases = params[layer]
        hs, gs = current_h.astype(bf16), current_g.astype(bf16)
        query_h = heads_of((nn(hs, wq) + bias_q).astype(bf16))
        query_g = heads_of((nn(gs, wq) + bias_q).astype(bf16))
        keys = heads_of(nn(hs, wk).astype(bf16))
        values = heads_of((nn(hs, wv) + bias_v).astype(bf16))
        bias = jnp.einsum("bij,hb->hij", onehot, table, precision=highest)
        mixed_h, logsum_h = attend(query_h, keys, values, content_mask, bias)
        mixed_g, logsum_g = attend(query_g, keys, values, query_mask, bias)
        mixed_h, mixed_g = rows_of(mixed_h), rows_of(mixed_g)
        part_h, part_g = nt(mixed_h, wo).astype(bf16), nt(mixed_g, wo).astype(bf16)
        before_h = current_h + part_h + links.pc(part_h).astype(f32) + biases[0]
        before_g = current_g + part_g + links.pc(part_g).astype(f32) + biases[0]
        normed_h = norm_rows(before_h, gains[0], shifts[0])
        normed_g = norm_rows(before_g, gains[0], shifts[0])
        fed_h, fed_g = normed_h.astype(bf16), normed_g.astype(bf16)
        inner_h, inner_g = nn(fed_h, wu) + bias_up, nn(fed_g, wu) + bias_up
        act_h, act_g = smooth(inner_h).astype(bf16), smooth(inner_g).astype(bf16)
        part_h, part_g = nt(act_h, wd).astype(bf16), nt(act_g, wd).astype(bf16)
        after_h = normed_h + part_h + links.pc(part_h).astype(f32) + biases[1]
        after_g = normed_g + part_g + links.pc(part_g).astype(f32) + biases[1]
        kept.append(
            (
                (hs, gs, query_h, query_g, keys, values, bias, logsum_h, logsum_g),
                (mixed_h, mixed_g, before_h, before_g, fed_h, fed_g, inner_h, inner_g),
                (act_h, act_g, after_h, after_g, wq, wk, wv, wo, wu, wd, gains, shifts),
            )
        )
        current_h = norm_rows(after_h, gains[1], shifts[1])
        current_g = norm_rows(after_g, gains[1], shifts[1])
    grad_h = ordered(leaving[:, :model])
    grad_g = ordered(leaving[:, model:])
    owned = [None] * LAYERS
    splits = [None] * LAYERS
    wholes = [None] * LAYERS
    for layer in range(LAYERS - 1, -1, -1):
        hs, gs, query_h, query_g, keys, values, bias, logsum_h, logsum_g = kept[layer][0]
        mixed_h, mixed_g, before_h, before_g, fed_h, fed_g, inner_h, inner_g = kept[layer][1]
        act_h, act_g, after_h, after_g, wq, wk, wv, wo, wu, wd, gains, shifts = kept[layer][2]
        back_h, gain2_h, shift2_h = norm_back(after_h, gains[1], shifts[1], grad_h)
        back_g, gain2_g, shift2_g = norm_back(after_g, gains[1], shifts[1], grad_g)
        dz_h, dz_g = back_h.astype(bf16), back_g.astype(bf16)
        du_h = smooth_back(inner_h, nn(dz_h, wd)).astype(bf16)
        du_g = smooth_back(inner_g, nn(dz_g, wd)).astype(bf16)
        down_grad = tn(dz_h, act_h) + tn(dz_g, act_g)
        up_grad = tn(fed_h, du_h) + tn(fed_g, du_g)
        up_bias_grad = jnp.sum(du_h.astype(f32), axis=0) + jnp.sum(du_g.astype(f32), axis=0)
        part_h, part_g = nt(du_h, wu).astype(bf16), nt(du_g, wu).astype(bf16)
        middle_h = back_h + part_h + links.pc(part_h).astype(f32)
        middle_g = back_g + part_g + links.pc(part_g).astype(f32)
        first_h, gain1_h, shift1_h = norm_back(before_h, gains[0], shifts[0], middle_h)
        first_g, gain1_g, shift1_g = norm_back(before_g, gains[0], shifts[0], middle_g)
        dy_h, dy_g = first_h.astype(bf16), first_g.astype(bf16)
        do_h = heads_of(nn(dy_h, wo).astype(bf16))
        do_g = heads_of(nn(dy_g, wo).astype(bf16))
        out_grad = tn(dy_h, mixed_h) + tn(dy_g, mixed_g)
        dq_h, dk_h, dv_h, ds_h = attend_back(
            query_h, keys, values, content_mask, bias, logsum_h, do_h
        )
        dq_g, dk_g, dv_g, ds_g = attend_back(
            query_g, keys, values, query_mask, bias, logsum_g, do_g
        )
        table_grad = jnp.einsum(
            "hij,bij->hb", ds_h.astype(f32) + ds_g.astype(f32), onehot, precision=highest
        )
        dq_h, dq_g = rows_of(dq_h).astype(bf16), rows_of(dq_g).astype(bf16)
        dk = rows_of(dk_h + dk_g).astype(bf16)
        dv = rows_of(dv_h + dv_g).astype(bf16)
        q_bias_grad = jnp.sum(dq_h.astype(f32), axis=0) + jnp.sum(dq_g.astype(f32), axis=0)
        v_bias_grad = jnp.sum(dv.astype(f32), axis=0)
        query_grad = tn(hs, dq_h) + tn(gs, dq_g)
        key_grad, value_grad = tn(hs, dk), tn(hs, dv)
        part_h = (nt(dq_h, wq) + nt(dk, wk) + nt(dv, wv)).astype(bf16)
        part_g = nt(dq_g, wq).astype(bf16)
        grad_h = first_h + part_h + links.pc(part_h).astype(f32)
        grad_g = first_g + part_g + links.pc(part_g).astype(f32)

        def by_x(v):
            return v.reshape(v.shape[0], 2, -1).transpose(1, 0, 2)

        attn_grad = jnp.concatenate(
            [by_x(query_grad), by_x(key_grad), by_x(value_grad), by_x(out_grad)], axis=2
        )
        owned[layer] = [
            links.scatter(g.astype(bf16), r)
            for g, r in zip((attn_grad, by_x(up_grad), by_x(down_grad)), routes[layer])
        ]
        splits[layer] = jnp.concatenate(
            [
                q_bias_grad.reshape(2, -1),
                v_bias_grad.reshape(2, -1),
                up_bias_grad.reshape(2, -1),
                table_grad.reshape(2, -1),
            ],
            axis=1,
        )
        wholes[layer] = jnp.stack(
            [
                gain1_h + gain1_g,
                gain2_h + gain2_g,
                shift1_h + shift1_g,
                shift2_h + shift2_g,
                jnp.sum(first_h + first_g, axis=0),
                jnp.sum(back_h + back_g, axis=0),
            ]
        )
    whole = jnp.dot(jnp.concatenate(wholes), swapper32.T, precision=highest)
    split_sum, whole_sum = links.total(jnp.concatenate(splits, axis=1), whole.reshape(-1))
    split_sum = split_sum.reshape(LAYERS, -1)
    whole_sum = whole_sum.reshape(LAYERS, 3, 2, model)

    def returned(rows):
        mine = lax.dynamic_slice_in_dim(rows.astype(bf16), core * rows_own, rows_own, 0)
        return nt(mine, swapper).astype(bf16)

    attn_sum = jnp.stack([owned[layer][0] for layer in range(LAYERS)])
    up_sum = jnp.stack([owned[layer][1] for layer in range(LAYERS)])
    down_sum = jnp.stack([owned[layer][2] for layer in range(LAYERS)])
    return (
        returned(current_h),
        returned(current_g),
        returned(grad_h),
        returned(grad_g),
        attn_sum[:, :, :part],
        attn_sum[:, :, part : 2 * part],
        attn_sum[:, :, 2 * part : 3 * part],
        attn_sum[:, :, 3 * part :].transpose(0, 2, 1),
        up_sum,
        down_sum.transpose(0, 2, 1),
        split_sum[:, :part],
        split_sum[:, part : 2 * part],
        split_sum[:, 2 * part : 2 * part + units],
        split_sum[:, 2 * part + units :].reshape(LAYERS, -1, BUCKETS),
        whole_sum[:, 0],
        whole_sum[:, 1],
        whole_sum[:, 2],
    )


def solution(mesh):
    links = Links(mesh)
    rows = P(("z", "y", "x", "core"), None)
    by_dp = P(("z", "y"), None)
    wide = P(None, ("z", "y"), ("x", "core"))
    tall = P(None, ("x", "core"), ("z", "y"))
    by_tensor = P(None, ("x", "core"))
    table = P(None, ("x", "core"), None)
    weights = (wide, wide, wide, tall, wide, tall)
    owned = (by_tensor, by_tensor, by_tensor, table, P(), P(), P())
    inner = jax.shard_map(
        lambda *arguments: local(links, *arguments),
        mesh=links.mesh,
        in_specs=(rows, rows, by_dp, by_dp, by_dp) + weights + owned + (rows, rows),
        out_specs=(rows, rows, rows, rows) + weights + owned,
        check_vma=False,
    )
    return inner
```

```python
import functools

import jax
import jax.numpy as jnp
from jax import lax
from jax.experimental import pallas as pl
from jax.experimental.pallas import tpu as pltpu
from jax.sharding import Mesh, PartitionSpec as P

HEAD = 64
BUCKETS = 32
LAYERS = 2
SEQ = 512
TILE = 128
NEAR = 5

epsilon = 1e-05
limits = (12, 16, 23, 32, 46, 64, 91)
highest = lax.Precision.HIGHEST
f32 = jnp.float32
bf16 = jnp.bfloat16
SWAP = [(0, 1), (1, 0)]
GATHER = (("zxy", "xzy", "yzx"), ("zyx", "xzy", "yzx"))
SCATTER = ("xyz", "yxz")
ANY = pl.BlockSpec(memory_space=pl.ANY)
VMEM = pl.BlockSpec(memory_space=pltpu.VMEM)


def dot(left, right, numbers):
    return lax.dot_general(left, right, (numbers, ((), ())), preferred_element_type=f32)


def nn(left, right):
    return dot(left, right, ((1,), (0,)))


def nt(left, right):
    return dot(left, right, ((1,), (1,)))


def tn(left, right):
    return dot(left, right, ((0,), (0,)))


def bucket_of(offset):
    distance = jnp.abs(offset)
    farther = 8 + sum(((distance >= border).astype(jnp.int32) for border in limits))
    return jnp.where(distance < 8, distance, farther) + 16 * (offset > 0).astype(jnp.int32)


def slot_masks(piece_lengths, ranks, chosen):
    places = jnp.arange(SEQ, dtype=jnp.int32)
    first = piece_lengths[0]
    second = first + piece_lengths[1]
    third = second + piece_lengths[2]
    segment = (
        (places >= first).astype(jnp.int32)
        + (places >= second).astype(jnp.int32)
        + (places >= third).astype(jnp.int32)
    )
    leading = jnp.where(
        segment == 0,
        0,
        jnp.where(segment == 1, first, jnp.where(segment == 2, second, third)),
    )
    same_doc = segment[:, None] == segment[None, :]
    visible = chosen[:, None] == 0
    content = same_doc & (visible | (ranks[:, None] <= ranks[None, :]))
    query = same_doc & (
        (places[:, None] == leading[None, :])
        | visible & (places[:, None] != places[None, :])
        | (ranks[:, None] < ranks[None, :])
    )
    return jnp.where(jnp.stack([content, query]), 0.0, -1e30).astype(f32)


def tile_buckets():
    near = jnp.arange(NEAR, dtype=jnp.int32)[:, None, None] - NEAR // 2
    key = jnp.arange(TILE, dtype=jnp.int32)[None, :, None]
    query = jnp.arange(TILE, dtype=jnp.int32)[None, None, :]
    return bucket_of(near * TILE + key - query)


class Links:
    def __init__(self, mesh):
        dp = mesh.shape["dp"]
        self.routed = dp == 8
        self.ny = 2
        self.nz = dp // 2
        self.nx = mesh.shape["tensor"] // 2
        self.mesh = Mesh(
            mesh.devices.reshape(self.nz, self.ny, self.nx, 2), ("z", "y", "x", "core")
        )
        self.ring = [(i, (i + 1) % self.nz) for i in range(self.nz)]

    def swap(self, v, axis):
        return lax.ppermute(v, axis, SWAP)

    def pz(self, v):
        return lax.ppermute(v, "z", self.ring)

    def pc(self, v):
        return lax.ppermute(v, "core", SWAP)

    def feature_order(self, width):
        count = self.nz * self.ny
        depth = width // count
        place = jnp.arange(width, dtype=jnp.int32)
        if not self.routed:
            return place
        block, rest = place // depth, place % depth
        ky, kz = block // self.nz, block % self.nz
        z = lax.rem(lax.axis_index("z") - kz + self.nz, self.nz)
        y = jnp.bitwise_xor(lax.axis_index("y"), ky)
        return (z * self.ny + y) * depth + rest

    def gather(self, block, route):
        if not self.routed:
            rows = lax.all_gather(block, ("z", "y"), axis=0, tiled=True)
            return Weight([lax.all_gather(rows, "x", axis=0)], (((0, 0), (1, 0)),))
        depth = block.shape[0]
        a, b = route.replace("z", "")
        held = [block if route[0] == "z" else jnp.stack([block, self.swap(block, a)])]
        for _ in range(self.nz - 1):
            held.append(self.pz(held[-1]))
        if route[0] == "z":
            held = [jnp.stack([h, self.swap(h, a)]) for h in held]
        pieces = held + [self.swap(h, b) for h in held]
        spots = []
        for other in range(2):
            for k in range(self.nz):
                pair = []
                for j in range(2):
                    x, y = (j, other) if a == "x" else (other, j)
                    pair.append((x, (y * self.nz + k) * depth))
                spots.append(tuple(pair))
        return Weight(pieces, tuple(spots))

    def scatter(self, keep, send, route):
        whole = jnp.concatenate([keep, send], axis=1)
        if route[0] == "x":
            whole = jnp.stack([keep.reshape(-1, keep.shape[2]), send.reshape(-1, send.shape[2])])
        mine = lax.psum_scatter(whole, "x", scatter_dimension=0, tiled=False)
        return lax.psum_scatter(mine, ("z", "y"), scatter_dimension=0, tiled=True).astype(f32)

    def pair(self, v):
        if not self.routed:
            return lax.all_gather(v, "x", axis=0)
        return jnp.stack([v, self.swap(v, "x")])

    def total(self, split, whole):
        if not self.routed:
            mine = lax.psum_scatter(split, "x", scatter_dimension=0, tiled=False)
            return lax.psum(mine, ("z", "y")), lax.psum(whole, ("z", "y", "x"))
        n = split.shape[1]
        count = n + whole.shape[0]
        filler = jnp.zeros((-count % 128,), f32)
        sent = jnp.concatenate([split[1], whole, filler]).reshape(-1, 128)
        kept = jnp.concatenate([split[0], whole, filler]).reshape(-1, 128)
        v = kept + self.swap(sent, "x")
        v = v + self.swap(v, "y")
        step = 1
        while step < self.nz:
            v = v + lax.ppermute(v, "z", [(i, i ^ step) for i in range(self.nz)])
            step *= 2
        v = v.reshape(-1)
        return v[:n], v[n:count]

    def both_rows(self, v):
        other = self.pc(v)
        first = lax.axis_index("core") == 0
        return jnp.concatenate([jnp.where(first, v, other), jnp.where(first, other, v)])


class Chain:
    last = ()

    def call(self, body, inputs, in_specs, outs, out_specs, flops, grid=(), scratch=(), after=()):
        waits = [*self.last, *after]
        count = len(inputs)

        def rest(*refs):
            body(*refs[:count], *refs[count + len(waits) :])

        made = pl.pallas_call(
            rest,
            out_shape=[jax.ShapeDtypeStruct(*o) for o in outs],
            grid=grid,
            in_specs=[*in_specs, *[ANY] * len(waits)],
            out_specs=out_specs,
            scratch_shapes=list(scratch),
            compiler_params=pltpu.CompilerParams(vmem_limit_bytes=48 << 20),
            cost_estimate=pl.CostEstimate(
                flops=4 * flops, bytes_accessed=0, transcendentals=0
            ),
        )(*inputs, *waits)
        self.last = (min(made, key=lambda v: v.size),)
        return made


class Weight:
    def __init__(self, arrays, spots):
        self.arrays = arrays
        self.spots = spots
        self.width = arrays[0].shape[2]

    def specs(self, grid):
        return [fixed(*v.shape) if grid else VMEM for v in self.arrays]

    def join(self, refs, target):
        for piece, places in zip(refs, self.spots):
            rows = piece.shape[1]
            for j, (x, row) in enumerate(places):
                target[x, row : row + rows] = piece[j]


def fold_sums(chain, arrays, wanted):
    inputs = [v for group in arrays for v in group]
    first = [sum(len(group) for group in arrays[:n]) for n in range(len(arrays))]
    outs = []
    for rows, dtype in wanted:
        which, index = rows[0]
        shape = jax.eval_shape(lambda v: v[index], arrays[which][0]).shape
        outs.append((shape if len(rows) == 1 else (len(rows), *shape), dtype))

    def body(*refs):
        for out, (rows, dtype) in zip(refs[len(inputs) :], wanted):
            for n, (which, index) in enumerate(rows):
                group = refs[first[which] : first[which] + len(arrays[which])]
                total = sum(ref[index].astype(f32) for ref in group).astype(dtype)
                if len(rows) == 1:
                    out[...] = total
                else:
                    out[n] = total

    return chain.call(
        body,
        inputs,
        [VMEM] * len(inputs),
        outs,
        [VMEM] * len(outs),
        flops=sum(v.size for v in inputs),
    )


class Scatter:
    def __init__(self, chain, links, parts):
        self.chain = chain
        self.links = links
        self.routes = [route for _, _, route in parts]
        self.depth = parts[0][0].shape[1] // links.nz
        if links.routed:
            self.sums = [[keep, links.swap(send, route[0])] for keep, send, route in parts]
        else:
            self.sums = [links.scatter(*part) for part in parts]

    def second(self):
        if not self.links.routed:
            return
        wanted = [([(n, (i,))], bf16 if i else f32) for n in range(len(self.routes)) for i in range(2)]
        made = fold_sums(self.chain, self.sums, wanted)
        self.sums = [
            [made[2 * n], self.links.swap(made[2 * n + 1], route[1])]
            for n, route in enumerate(self.routes)
        ]

    def third(self):
        links = self.links
        if not links.routed:
            return
        wanted = []
        for k in range(links.nz):
            at = (slice(k * self.depth, (k + 1) * self.depth),)
            wanted.append(([(n, at) for n in range(len(self.routes))], bf16 if k else f32))
        made = fold_sums(self.chain, self.sums, wanted)
        self.sums = [made[0]]
        for k in range(1, links.nz):
            to = [(i, (i - k) % links.nz) for i in range(links.nz)]
            self.sums.append(lax.ppermute(made[k], "z", to))

    def finish(self):
        if not self.links.routed:
            return self.sums
        wanted = [([(0, (n,))], f32) for n in range(len(self.routes))]
        return fold_sums(self.chain, [self.sums], wanted)


def centered(rows):
    center = rows - jnp.mean(rows, axis=-1, keepdims=True)
    scale = lax.rsqrt(jnp.mean(center * center, axis=-1, keepdims=True) + epsilon)
    return center * scale, scale


def norm_back(rows, gain, grad):
    unit, scale = centered(rows)
    inner = grad * gain
    first = jnp.mean(inner, axis=-1, keepdims=True)
    second = jnp.mean(inner * unit, axis=-1, keepdims=True)
    back = scale * (inner - first - unit * second)
    return back, jnp.sum(grad * unit, axis=0, keepdims=True), jnp.sum(grad, axis=0, keepdims=True)


def gelu_pair(u):
    root = 0.7978845608028654
    square = u * u
    t = jnp.tanh(root * u * (1.0 + 0.044715 * square))
    half = 0.5 * (1.0 + t)
    slope = half + (0.5 * root) * u * (1.0 - t * t) * (1.0 + (3 * 0.044715) * square)
    return u * half, slope


def bias_block(tiles, head, half):
    rows = []
    for key in range(SEQ // TILE):
        row = []
        for query in range(2 * half, 2 * half + 2):
            row.append(tiles[head, min(max(key - query, -2), 2) + 2])
        rows.append(jnp.concatenate(row, axis=1))
    return jnp.concatenate(rows, axis=0)


def split_heads(block, count):
    return [block[:, HEAD * n : HEAD * (n + 1)] for n in range(count)]


def attn_forward(weight, later, refs):
    n = len(weight.arrays)
    refs = list(refs)
    if later:
        h1_ref, own_ref, other_ref, prm_ref = refs[:4]
        refs = refs[4:]
    else:
        x_ref = refs.pop(0)
    pieces, refs = refs[:n], refs[n:]
    qv_ref, tiles_ref, mask_ref = refs[:3]
    refs = refs[3:]
    if later:
        h_ref, x_ref = refs[:2]
        refs = refs[2:]
    part_ref, q_ref, k_ref, v_ref, o_ref, lse_ref, w_ref, mixed_ref = refs
    rows = 2 * SEQ
    if later:
        gain, shift, bias = prm_ref[3:4], prm_ref[4:5], prm_ref[5:6]

        def norm(i, carry):
            at = pl.ds(pl.multiple_of(i * 128, 128), 128)
            value = h1_ref[at] + own_ref[at].astype(f32) + other_ref[at].astype(f32) + bias
            unit, scale = centered(value)
            result = unit * gain + shift
            h_ref[at] = result
            x_ref[at] = result.astype(bf16)
            return carry

        lax.fori_loop(0, rows // 128, norm, 0)
    weight.join(pieces, w_ref)
    heads = k_ref.shape[0]
    per = heads // 2
    part = per * HEAD
    for x in range(2):
        for stream in range(2):
            block = x_ref[stream * SEQ : (stream + 1) * SEQ]
            width = w_ref.shape[2] if stream == 0 else 256
            result = nn(block, w_ref[x, :, :width])
            query = (result[:, :part] + qv_ref[x, 0:1, :part]).astype(bf16).astype(f32) * 0.125
            for j, one in enumerate(split_heads(query.astype(bf16), per)):
                q_ref[stream * heads + x * per + j] = one
            if stream == 0:
                key = result[:, part : 2 * part].astype(bf16)
                value = (result[:, 2 * part : 3 * part] + qv_ref[x, 1:2, :part]).astype(bf16)
                for j, one in enumerate(split_heads(key, per)):
                    k_ref[x * per + j] = one
                for j, one in enumerate(split_heads(value, per)):
                    v_ref[x * per + j] = one

    def one_head(head, carry):
        key, value = k_ref[head], v_ref[head]
        for half in range(2):
            at = slice(half * 256, half * 256 + 256)
            bias = bias_block(tiles_ref, head, half)
            for stream in range(2):
                query = q_ref[stream * heads + head, at]
                score = nt(key, query) + (bias + mask_ref[stream, :, at])
                top = jnp.max(score, axis=0, keepdims=True)
                raised = jnp.exp(score - top)
                total = jnp.sum(raised, axis=0, keepdims=True)
                mixed = tn(value, raised.astype(bf16)) * (1.0 / total)
                mixed_ref[stream * heads + head, at] = mixed.T.astype(bf16)
                lse_ref[stream * heads + head, :, at] = top + jnp.log(total)
        return carry

    lax.fori_loop(0, heads, one_head, 0)
    for stream in range(2):
        total = None
        for x in range(2):
            blocks = [jnp.zeros((SEQ, HEAD), bf16)]
            blocks += [mixed_ref[stream * heads + x * per + j] for j in range(per)]
            block = jnp.concatenate(blocks, axis=1)
            o_ref[x, stream * SEQ : (stream + 1) * SEQ] = block
            term = nt(block, w_ref[x, :, 512:768])
            total = term if total is None else total + term
        part_ref[stream * SEQ : (stream + 1) * SEQ] = total.astype(bf16)


def run_attn_forward(chain, entering, weight, qv, tiles, mask, after):
    later = len(entering) == 4
    heads = tiles.shape[0]
    width = entering[0].shape[1]
    rows = entering[0].shape[0]
    columns = weight.width
    inputs = [*entering, *weight.arrays, qv, tiles, mask]
    specs = [VMEM] * len(entering) + weight.specs(False) + [VMEM] * 3
    outs = [((rows, width), f32), ((rows, width), bf16)] if later else []
    outs += [
        ((rows, width), bf16),
        ((2 * heads, SEQ, HEAD), bf16),
        ((heads, SEQ, HEAD), bf16),
        ((heads, SEQ, HEAD), bf16),
        ((2, rows, 256), bf16),
        ((2 * heads, 1, SEQ), f32),
    ]
    return chain.call(
        lambda *refs: attn_forward(weight, later, refs),
        inputs,
        specs,
        outs,
        [VMEM] * len(outs),
        flops=14 * 10**9,
        scratch=[
            pltpu.VMEM((2, width, weight.width), bf16),
            pltpu.VMEM((2 * heads, SEQ, HEAD), bf16),
        ],
        after=after,
    )


def ffn_forward(up, down, refs):
    h_ref, own_ref, other_ref, prm_ref, bias_ref = refs[:5]
    refs = refs[5:]
    up_pieces, refs = refs[: len(up.arrays)], refs[len(up.arrays) :]
    down_pieces, refs = refs[: len(down.arrays)], refs[len(down.arrays) :]
    ah_ref, h1_ref, fed_ref, act_ref, slope_ref, part_ref = refs[:6]
    up_ref, down_ref = refs[6:]

    @pl.when(pl.program_id(0) == 0)
    def _():
        up.join(up_pieces, up_ref)
        down.join(down_pieces, down_ref)

    gain, shift, bias = prm_ref[0:1], prm_ref[1:2], prm_ref[2:3]
    before = h_ref[...].astype(f32) + own_ref[...].astype(f32) + other_ref[...].astype(f32) + bias
    ah_ref[...] = before
    unit, scale = centered(before)
    normed = unit * gain + shift
    h1_ref[...] = normed
    fed = normed.astype(bf16)
    fed_ref[...] = fed

    total = None
    for x in range(2):
        inner = nn(fed, up_ref[x]) + bias_ref[x]
        act, slope = gelu_pair(inner)
        act = act.astype(bf16)
        act_ref[x] = act
        slope_ref[x] = slope.astype(bf16)
        term = nt(act, down_ref[x])
        total = term if total is None else total + term
    part_ref[...] = total.astype(bf16)


def by_rows(rows, width):
    return pl.BlockSpec((rows, width), lambda i: (i, 0))


def by_rows_pair(rows, width):
    return pl.BlockSpec((2, rows, width), lambda i: (0, i, 0))


def fixed(*shape):
    return pl.BlockSpec(shape, lambda i: (0,) * len(shape))


def run_ffn_forward(chain, entering, params, bias, up, down):
    rows, width = entering[0].shape
    step = 256
    units = up.width
    inputs = [*entering, params, bias, *up.arrays, *down.arrays]
    specs = [by_rows(step, width)] * 3 + [fixed(8, width), fixed(2, 1, units)]
    specs += up.specs(True) + down.specs(True)
    outs = [
        ((rows, width), f32),
        ((rows, width), f32),
        ((rows, width), bf16),
        ((2, rows, units), bf16),
        ((2, rows, units), bf16),
        ((rows, width), bf16),
    ]
    out_specs = [by_rows(step, width)] * 3 + [by_rows_pair(step, units)] * 2
    out_specs += [by_rows(step, width)]
    return chain.call(
        lambda *refs: ffn_forward(up, down, refs),
        inputs,
        specs,
        outs,
        out_specs,
        flops=8 * rows * width * units,
        grid=(rows // step,),
        scratch=[
            pltpu.VMEM((2, width, units), bf16),
            pltpu.VMEM((2, width, units), bf16),
        ],
    )


def ffn_backward(up, down, grads, last, refs):
    grad_refs, refs = refs[:grads], refs[grads:]
    h1_ref, own_ref, other_ref, prm_ref, slope_ref = refs[:5]
    refs = refs[5:]
    up_pieces, refs = refs[: len(up.arrays)], refs[len(up.arrays) :]
    down_pieces, refs = refs[: len(down.arrays)], refs[len(down.arrays) :]
    dz_ref, dbh_ref, du_ref, part_ref, sums_ref, up_sums_ref = refs[:6]
    refs = refs[6:]
    if last:
        out_ref, refs = refs[0], refs[1:]
    up_ref, down_ref = refs

    @pl.when(pl.program_id(0) == 0)
    def _():
        up.join(up_pieces, up_ref)
        down.join(down_pieces, down_ref)
        sums_ref[...] = jnp.zeros_like(sums_ref)
        up_sums_ref[...] = jnp.zeros_like(up_sums_ref)

    gain, shift, bias = prm_ref[3:4], prm_ref[4:5], prm_ref[5:6]
    grad = sum(ref[...].astype(f32) for ref in grad_refs)
    after = h1_ref[...] + own_ref[...].astype(f32) + other_ref[...].astype(f32) + bias
    if last:
        unit, scale = centered(after)
        out_ref[...] = (unit * gain + shift).astype(bf16)
    back, gain_sum, shift_sum = norm_back(after, gain, grad)
    dbh_ref[...] = back
    sums_ref[0:1] += gain_sum
    sums_ref[1:2] += shift_sum
    sums_ref[2:3] += jnp.sum(back, axis=0, keepdims=True)
    dz = back.astype(bf16)
    dz_ref[...] = dz

    total = None
    for x in range(2):
        du = (nn(dz, down_ref[x]) * slope_ref[x].astype(f32)).astype(bf16)
        du_ref[x] = du
        up_sums_ref[x] += jnp.sum(du.astype(f32), axis=0, keepdims=True)
        term = nt(du, up_ref[x])
        total = term if total is None else total + term
    part_ref[...] = total.astype(bf16)


def run_ffn_backward(chain, grads, entering, params, slope, up, down, last):
    rows, width = entering[0].shape
    step = 256
    units = up.width
    inputs = [*grads, *entering, params, slope, *up.arrays, *down.arrays]
    specs = [by_rows(step, width)] * (len(grads) + 3)
    specs += [fixed(8, width), by_rows_pair(step, units)]
    specs += up.specs(True) + down.specs(True)
    outs = [
        ((rows, width), bf16),
        ((rows, width), f32),
        ((2, rows, units), bf16),
        ((rows, width), bf16),
        ((8, width), f32),
        ((2, 1, units), f32),
    ]
    out_specs = [by_rows(step, width)] * 2 + [by_rows_pair(step, units), by_rows(step, width)]
    out_specs += [fixed(8, width), fixed(2, 1, units)]
    if last:
        outs.append(((rows, width), bf16))
        out_specs.append(by_rows(step, width))
    return chain.call(
        lambda *refs: ffn_backward(up, down, len(grads), last, refs),
        inputs,
        specs,
        outs,
        out_specs,
        flops=8 * rows * width * units,
        grid=(rows // step,),
        scratch=[
            pltpu.VMEM((2, width, units), bf16),
            pltpu.VMEM((2, width, units), bf16),
        ],
    )


def fold(near):
    within = lax.broadcasted_iota(jnp.int32, (8, TILE), 0)
    lane = lax.broadcasted_iota(jnp.int32, (8, TILE), 1)
    zero = jnp.zeros((8, TILE), f32)

    def aligned(rows, at):
        rows = pltpu.roll(rows, (TILE - at) % TILE, 1)
        for bit in (1, 2, 4):
            rows = jnp.where((within & bit) != 0, pltpu.roll(rows, TILE - bit, 1), rows)
        return rows

    same = after = far_before = far_after = zero
    for at in range(0, TILE, 8):
        upper = within + lane < TILE - at
        one, two, three = (aligned(near[i][at : at + 8], at) for i in (1, 2, 3))
        same += jnp.where(upper, two, one)
        after += jnp.where(upper, three, two)
        far_before += near[0][at : at + 8] + jnp.where(upper, one, zero)
        far_after += near[4][at : at + 8] + jnp.where(upper, zero, three)
    sums = [jnp.sum(v, axis=0, keepdims=True) for v in (same, after, far_before, far_after)]
    return jnp.concatenate([*sums, jnp.zeros((4, TILE), f32)])


def attn_backward(weight, refs):
    n = len(weight.arrays)
    dbh_ref, own_ref, other_ref, ah_ref, prm_ref = refs[:5]
    pieces, refs = refs[5 : 5 + n], refs[5 + n :]
    q_ref, k_ref, v_ref, lse_ref, tiles_ref, mask_ref = refs[:6]
    refs = refs[6:]
    dah_ref, dy_ref, dcat_ref, dqg_ref, part_ref, near_ref, sums_ref, col_ref = refs[:8]
    w_ref, do_ref, dq_ref, dk_ref, dv_ref = refs[8:]
    rows = 2 * SEQ
    gain = prm_ref[0:1]
    sums_ref[...] = jnp.zeros_like(sums_ref)

    def norm(i, carry):
        at = pl.ds(pl.multiple_of(i * 128, 128), 128)
        grad = dbh_ref[at] + own_ref[at].astype(f32) + other_ref[at].astype(f32)
        back, gain_sum, shift_sum = norm_back(ah_ref[at], gain, grad)
        dah_ref[at] = back
        dy_ref[at] = back.astype(bf16)
        sums_ref[0:1] += gain_sum
        sums_ref[1:2] += shift_sum
        sums_ref[2:3] += jnp.sum(back, axis=0, keepdims=True)
        return carry

    lax.fori_loop(0, rows // 128, norm, 0)
    weight.join(pieces, w_ref)
    heads = k_ref.shape[0]
    per = heads // 2
    for stream in range(2):
        at = slice(stream * SEQ, (stream + 1) * SEQ)
        for x in range(2):
            block = nn(dy_ref[at], w_ref[x, :, 512:768]).astype(bf16)
            for j in range(per):
                do_ref[stream * heads + x * per + j] = block[:, HEAD * (1 + j) : HEAD * (2 + j)]

    def one_head(head, carry):
        key, value = k_ref[head], v_ref[head]
        grad_key = jnp.zeros((SEQ, HEAD), f32)
        grad_value = jnp.zeros((SEQ, HEAD), f32)
        near = [jnp.zeros((TILE, TILE), f32) for _ in range(NEAR)]
        for half in range(2):
            at = slice(half * 256, half * 256 + 256)
            bias = bias_block(tiles_ref, head, half)
            for stream in range(2):
                spot = stream * heads + head
                query, grad_out = q_ref[spot, at], do_ref[spot, at]
                score = nt(key, query) + (bias + mask_ref[stream, :, at])
                prob = jnp.exp(score - lse_ref[spot, :, at])
                both = prob * nt(value, grad_out)
                inner = jnp.sum(both, axis=0, keepdims=True)
                grad_score = (both - prob * inner).astype(bf16)
                grad_value += nn(prob.astype(bf16), grad_out)
                grad_key += nn(grad_score, query)
                dq_ref[spot, at] = (tn(key, grad_score) * 0.125).T.astype(bf16)
                wide = grad_score.astype(f32)
                for k in range(SEQ // TILE):
                    for q in range(2):
                        which = min(max(k - (2 * half + q), -2), 2) + 2
                        near[which] += wide[
                            k * TILE : (k + 1) * TILE, q * TILE : (q + 1) * TILE
                        ]
        near_ref[head] = fold(near)
        dk_ref[head] = grad_key.astype(bf16)
        dv_ref[head] = grad_value.astype(bf16)
        return carry

    lax.fori_loop(0, heads, one_head, 0)
    total_h = total_g = None
    for x in range(2):
        near = range(x * per, (x + 1) * per)
        blocks = [dq_ref[j] for j in near] + [dk_ref[j] for j in near] + [dv_ref[j] for j in near]
        blocks += [jnp.zeros((SEQ, HEAD), bf16)] * per
        block = jnp.concatenate(blocks, axis=1)
        dcat_ref[x] = block
        term = nt(block, w_ref[x])
        total_h = term if total_h is None else total_h + term
        col_ref[x, 0:1] = jnp.sum(block.astype(f32), axis=0, keepdims=True)
        blocks = [dq_ref[heads + j] for j in near] + [jnp.zeros((SEQ, HEAD), bf16)]
        block = jnp.concatenate(blocks, axis=1)
        dqg_ref[x] = block
        term = nt(block, w_ref[x, :, :256])
        total_g = term if total_g is None else total_g + term
        col_ref[x, 1:2, :256] = jnp.sum(block.astype(f32), axis=0, keepdims=True)
    part_ref[:SEQ] = total_h.astype(bf16)
    part_ref[SEQ:] = total_g.astype(bf16)


def run_attn_backward(chain, entering, params, weight, saved, tiles, mask):
    rows, width = entering[0].shape
    heads = tiles.shape[0]
    columns = weight.width
    q, k, v, _, lse = saved
    inputs = [*entering, params, *weight.arrays, q, k, v, lse, tiles, mask]
    specs = [VMEM] * 5 + weight.specs(False) + [VMEM] * 6
    outs = [
        ((rows, width), f32),
        ((rows, width), bf16),
        ((2, SEQ, columns), bf16),
        ((2, SEQ, 256), bf16),
        ((rows, width), bf16),
        ((heads, 8, TILE), f32),
        ((8, width), f32),
        ((2, 8, columns), f32),
    ]
    return chain.call(
        lambda *refs: attn_backward(weight, refs),
        inputs,
        specs,
        outs,
        [VMEM] * len(outs),
        flops=20 * 10**9,
        scratch=[
            pltpu.VMEM((2, width, weight.width), bf16),
            pltpu.VMEM((2 * heads, SEQ, HEAD), bf16),
            pltpu.VMEM((2 * heads, SEQ, HEAD), bf16),
            pltpu.VMEM((heads, SEQ, HEAD), bf16),
            pltpu.VMEM((heads, SEQ, HEAD), bf16),
        ],
    )


def quarters(part, first):
    return [(part, x) for x in range(2)] if first == "y" else [(y, part) for y in range(2)]


def ffn_grads(chain, fed, du, dz, act, part, up_first, down_first):
    rows, width = fed.shape
    units = du.shape[2]
    half = width // 2

    def body(fed_ref, du_ref, dz_ref, act_ref, up_ref, down_ref):
        for left, right, out, first in (
            (fed_ref, du_ref, up_ref, up_first),
            (dz_ref, act_ref, down_ref, down_first),
        ):
            for n, (y, x) in enumerate(quarters(part, first)):
                out[n] = tn(left[:, y * half : (y + 1) * half], right[x]).astype(bf16)

    return chain.call(
        body,
        [fed, du, dz, act],
        [VMEM] * 4,
        [((2, half, units), bf16)] * 2,
        [VMEM] * 2,
        flops=8 * rows * half * units,
    )


def attn_grads(chain, x, dcat, dqg, dy, o, part, firsts):
    rows, width = x.shape
    half = width // 2
    columns = dcat.shape[2]
    span = columns // len(firsts)

    def body(x_ref, dcat_ref, dqg_ref, dy_ref, o_ref, *outs):
        for y in range(2):
            at = slice(y * half, (y + 1) * half)
            for n, first in enumerate(firsts):
                for place, (want, other) in enumerate(quarters(part, first)):
                    if want != y:
                        continue
                    low, high = n * span, (n + 1) * span
                    total = tn(x_ref[:SEQ, at], dcat_ref[other, :, low:high])
                    outs[n][place] = total.astype(bf16)
                    if n == 0:
                        query = total[:, :256] + tn(x_ref[SEQ:, at], dqg_ref[other])
                        outs[n][place, :, :256] = query.astype(bf16)
                    if n == len(firsts) - 1:
                        out = total[:, span - 256 :] + tn(dy_ref[:, at], o_ref[other])
                        outs[n][place, :, span - 256 :] = out.astype(bf16)

    return chain.call(
        body,
        [x, dcat, dqg, dy, o],
        [VMEM] * 5,
        [((2, half, span), bf16)] * len(firsts),
        [VMEM] * len(firsts),
        flops=6 * rows * half * columns,
    )


def local(links, *arguments):
    (
        h_in,
        g_in,
        lengths,
        order,
        predicted,
        w_query,
        w_key,
        w_value,
        w_out,
        w_up,
        w_down,
        q_bias,
        v_bias,
        up_bias,
        rel_table,
        norm_gain,
        norm_shift,
        out_bias,
        h_cot,
        g_cot,
    ) = arguments
    rows_own, model = h_in.shape
    part = w_query.shape[2]
    units = w_up.shape[2]
    heads = 2 * rel_table.shape[1]
    table_size = rel_table.shape[1] * BUCKETS
    slot = lax.axis_index("x")
    core = lax.axis_index("core")

    chain = Chain()
    gathered = []
    for layer in range(LAYERS):
        attn = jnp.concatenate(
            [w_query[layer], w_key[layer], w_value[layer], w_out[layer].T], axis=1
        )
        blocks = (attn, w_up[layer], w_down[layer].T)
        gathered.append([links.gather(b, r) for b, r in zip(blocks, GATHER[layer])])

    def pick(v):
        return lax.dynamic_index_in_dim(v, slot, 0, keepdims=False)

    mask = slot_masks(pick(lengths), pick(order), pick(predicted))
    onehot = (
        jnp.arange(BUCKETS, dtype=jnp.int32)[:, None] == tile_buckets().reshape(1, -1)
    ).astype(f32)

    lanes = jnp.arange(TILE, dtype=jnp.int32)
    edge = jnp.full_like(lanes, TILE)
    fold_buckets = bucket_of(jnp.concatenate([-lanes, TILE - lanes, -edge, edge]))
    fold_hot = (fold_buckets[:, None] == jnp.arange(BUCKETS, dtype=jnp.int32)[None, :]).astype(f32)

    small = links.pair(
        jnp.concatenate(
            [q_bias, v_bias, up_bias, rel_table.reshape(LAYERS, table_size)], axis=1
        )
    )
    tables = small[:, :, 2 * part + units :].transpose(1, 0, 2).reshape(LAYERS * heads, BUCKETS)
    tiles = jnp.dot(tables, onehot, precision=highest).reshape(LAYERS, heads, NEAR, TILE, TILE)
    qv = jnp.stack([small[:, :, :part], small[:, :, part : 2 * part]], axis=2)
    qv = jnp.pad(qv, ((0, 0), (0, 0), (0, 6), (0, 256 - part)))
    bias_up = small[:, :, None, 2 * part : 2 * part + units]

    features = links.feature_order(model)
    swapper = (jnp.arange(model, dtype=jnp.int32)[:, None] == features[None, :]).astype(bf16)
    swapper32 = swapper.astype(f32)
    params = jnp.dot(
        jnp.stack([norm_gain, norm_shift, out_bias], axis=2).reshape(-1, model),
        swapper32,
        precision=highest,
    ).reshape(LAYERS, 6, model)
    params = jnp.pad(params, ((0, 0), (0, 2), (0, 0)))

    def ordered(first, second):
        rows = links.both_rows(jnp.concatenate([first, second], axis=1))
        both = jnp.concatenate([rows[:, :model], rows[:, model:]], axis=0)
        return nn(both, swapper).astype(bf16)

    entering = ordered(h_in, g_in)
    kept = []
    for layer in range(LAYERS):
        attn, up, down = gathered[layer]
        if layer == 0:
            x = stream = entering
            before = (entering,)
            after = []
            if links.routed:
                after = [v for w in (up, down, *gathered[1]) for v in w.arrays]
        else:
            before = (h1, part_own, part_other, params[layer - 1])
            after = []
        made = run_attn_forward(chain, before, attn, qv[:, layer], tiles[layer], mask, after)
        if layer > 0:
            stream, x = made[:2]
            made = made[2:]
        mixed_own, q, k, v, o, lse = made
        ah, h1, fed, act, slope, part_own = run_ffn_forward(
            chain, (stream, mixed_own, links.pc(mixed_own)), params[layer], bias_up[:, layer], up, down
        )
        part_other = links.pc(part_own)
        kept.append((x, (q, k, v, o, lse), ah, (h1, part_own, part_other), fed, act, slope))
    grads = (ordered(h_cot, g_cot),)
    owned = [None] * LAYERS
    splits = [None] * LAYERS
    wholes = [None] * LAYERS
    for layer in range(LAYERS - 1, -1, -1):
        attn, up, down = gathered[layer]
        firsts = [r[0] for r in SCATTER]
        x, saved, ah, second, fed, act, slope = kept[layer]
        last = layer == LAYERS - 1
        made = run_ffn_backward(chain, grads, second, params[layer], slope, up, down, last)
        dz, dbh, du, part_own, sums_two, up_sums = made[:6]
        if last:
            result = made[6]
        part_other = links.pc(part_own)
        if not last:
            ffn_way.third()
            attn_way.second()
        sent = ffn_grads(chain, fed, du, dz, act, 1, *firsts)
        held = ffn_grads(chain, fed, du, dz, act, 0, *firsts)
        if not last:
            attn_way.third()
            done_ffn = ffn_way.finish()
            old_attn = attn_way
        ffn_way = Scatter(chain, links, list(zip(held, sent, SCATTER)))
        dah, dy, dcat, dqg, part_own, near, sums_one, cols = run_attn_backward(
            chain, (dbh, part_own, part_other, ah), params[layer], attn, saved, tiles[layer], mask
        )
        part_other = links.pc(part_own)
        ffn_way.second()
        sent = attn_grads(chain, x, dcat, dqg, dy, saved[3], 1, firsts)
        held = attn_grads(chain, x, dcat, dqg, dy, saved[3], 0, firsts)
        attn_way = Scatter(chain, links, list(zip(held, sent, SCATTER)))
        if not last:
            owned[layer + 1] = (old_attn.finish(), done_ffn)
            ffn_way.third()
            attn_way.second()
            attn_way.third()
            owned[layer] = (attn_way.finish(), ffn_way.finish())
        grads = (dah, part_own, part_other)
        table = jnp.dot(near[:, :4].reshape(heads, -1), fold_hot, precision=highest)
        splits[layer] = jnp.concatenate(
            [
                cols[:, 0, :part] + cols[:, 1, :part],
                cols[:, 0, 2 * part : 3 * part],
                up_sums[:, 0],
                table.reshape(2, table_size),
            ],
            axis=1,
        )
        wholes[layer] = jnp.stack(
            [sums_one[0], sums_two[0], sums_one[1], sums_two[1], sums_one[2], sums_two[2]]
        )
    whole = jnp.dot(jnp.concatenate(wholes), swapper32.T, precision=highest)
    split_sum, whole_sum = links.total(jnp.concatenate(splits, axis=1), whole.reshape(-1))
    split_sum = split_sum.reshape(LAYERS, -1)
    whole_sum = whole_sum.reshape(LAYERS, 3, 2, model)

    def returned(parts):
        mine = []
        for stream in range(2):
            at = stream * SEQ + core * rows_own
            rows = [lax.dynamic_slice_in_dim(p, at, rows_own, 0) for p in parts]
            mine.append(sum(r.astype(f32) for r in rows).astype(bf16))
        back = nt(jnp.concatenate(mine), swapper).astype(bf16)
        return back[:rows_own], back[rows_own:]

    h_out, g_out = returned((result,))
    h_grad, g_grad = returned(grads)
    attn_sum = jnp.stack([jnp.concatenate(owned[layer][0], axis=1) for layer in range(LAYERS)])
    up_sum = jnp.stack([owned[layer][1][0] for layer in range(LAYERS)])
    down_sum = jnp.stack([owned[layer][1][1] for layer in range(LAYERS)])
    return (
        h_out,
        g_out,
        h_grad,
        g_grad,
        attn_sum[:, :, :part],
        attn_sum[:, :, part : 2 * part],
        attn_sum[:, :, 2 * part : 3 * part],
        attn_sum[:, :, 3 * part :].transpose(0, 2, 1),
        up_sum,
        down_sum.transpose(0, 2, 1),
        split_sum[:, :part],
        split_sum[:, part : 2 * part],
        split_sum[:, 2 * part : 2 * part + units],
        split_sum[:, 2 * part + units :].reshape(LAYERS, -1, BUCKETS),
        whole_sum[:, 0],
        whole_sum[:, 1],
        whole_sum[:, 2],
    )


def solution(mesh):
    links = Links(mesh)
    rows = P(("z", "y", "x", "core"), None)
    by_dp = P(("z", "y"), None)
    wide = P(None, ("z", "y"), ("x", "core"))
    tall = P(None, ("x", "core"), ("z", "y"))
    by_tensor = P(None, ("x", "core"))
    table = P(None, ("x", "core"), None)
    weights = (wide, wide, wide, tall, wide, tall)
    owned = (by_tensor, by_tensor, by_tensor, table, P(), P(), P())
    return jax.shard_map(
        functools.partial(local, links),
        mesh=links.mesh,
        in_specs=(rows, rows, by_dp, by_dp, by_dp) + weights + owned + (rows, rows),
        out_specs=(rows, rows, rows, rows) + weights + owned,
        check_vma=False,
    )
```

```python
import functools

import jax
import jax.numpy as jnp
from jax import lax
from jax.experimental import pallas as pl
from jax.experimental.pallas import tpu as pltpu
from jax.sharding import Mesh, PartitionSpec as P

HEAD = 64
BUCKETS = 32
LAYERS = 2
SEQ = 512
TILE = 128
NEAR = 5

epsilon = 1e-05
limits = (12, 16, 23, 32, 46, 64, 91)
highest = lax.Precision.HIGHEST
f32 = jnp.float32
bf16 = jnp.bfloat16
SWAP = [(0, 1), (1, 0)]
GATHER = (("zxy", "xzy", "yzx"), ("zyx", "xzy", "yzx"))
SCATTER = ("xyz", "yxz")
ANY = pl.BlockSpec(memory_space=pl.ANY)
VMEM = pl.BlockSpec(memory_space=pltpu.VMEM)


def dot(left, right, numbers):
    return lax.dot_general(left, right, (numbers, ((), ())), preferred_element_type=f32)


def nn(left, right):
    return dot(left, right, ((1,), (0,)))


def nt(left, right):
    return dot(left, right, ((1,), (1,)))


def tn(left, right):
    return dot(left, right, ((0,), (0,)))


def bucket_of(offset):
    distance = jnp.abs(offset)
    farther = 8 + sum(((distance >= border).astype(jnp.int32) for border in limits))
    return jnp.where(distance < 8, distance, farther) + 16 * (offset > 0).astype(jnp.int32)


def slot_masks(piece_lengths, ranks, chosen):
    places = jnp.arange(SEQ, dtype=jnp.int32)
    first = piece_lengths[0]
    second = first + piece_lengths[1]
    third = second + piece_lengths[2]
    segment = (
        (places >= first).astype(jnp.int32)
        + (places >= second).astype(jnp.int32)
        + (places >= third).astype(jnp.int32)
    )
    leading = jnp.where(
        segment == 0,
        0,
        jnp.where(segment == 1, first, jnp.where(segment == 2, second, third)),
    )
    same_doc = segment[:, None] == segment[None, :]
    visible = chosen[:, None] == 0
    content = same_doc & (visible | (ranks[:, None] <= ranks[None, :]))
    query = same_doc & (
        (places[:, None] == leading[None, :])
        | visible & (places[:, None] != places[None, :])
        | (ranks[:, None] < ranks[None, :])
    )
    return jnp.where(jnp.stack([content, query]), 0.0, -1e30).astype(f32)


def tile_buckets():
    near = jnp.arange(NEAR, dtype=jnp.int32)[:, None, None] - NEAR // 2
    key = jnp.arange(TILE, dtype=jnp.int32)[None, :, None]
    query = jnp.arange(TILE, dtype=jnp.int32)[None, None, :]
    return bucket_of(near * TILE + key - query)


class Links:
    def __init__(self, mesh):
        dp = mesh.shape["dp"]
        self.routed = dp == 8
        self.ny = 2
        self.nz = dp // 2
        self.nx = mesh.shape["tensor"] // 2
        self.mesh = Mesh(
            mesh.devices.reshape(self.nz, self.ny, self.nx, 2), ("z", "y", "x", "core")
        )
        self.ring = [(i, (i + 1) % self.nz) for i in range(self.nz)]

    def swap(self, v, axis):
        return lax.ppermute(v, axis, SWAP)

    def pz(self, v):
        return lax.ppermute(v, "z", self.ring)

    def pc(self, v):
        return lax.ppermute(v, "core", SWAP)

    def feature_order(self, width):
        count = self.nz * self.ny
        depth = width // count
        place = jnp.arange(width, dtype=jnp.int32)
        if not self.routed:
            return place
        block, rest = place // depth, place % depth
        ky, kz = block // self.nz, block % self.nz
        z = lax.rem(lax.axis_index("z") - kz + self.nz, self.nz)
        y = jnp.bitwise_xor(lax.axis_index("y"), ky)
        return (z * self.ny + y) * depth + rest

    def gather(self, block, route):
        if not self.routed:
            rows = lax.all_gather(block, ("z", "y"), axis=0, tiled=True)
            return Weight([lax.all_gather(rows, "x", axis=0)], (((0, 0), (1, 0)),))
        depth = block.shape[0]
        a, b = route.replace("z", "")
        held = [block if route[0] == "z" else jnp.stack([block, self.swap(block, a)])]
        for _ in range(self.nz - 1):
            held.append(self.pz(held[-1]))
        if route[0] == "z":
            held = [jnp.stack([h, self.swap(h, a)]) for h in held]
        pieces = held + [self.swap(h, b) for h in held]
        spots = []
        for other in range(2):
            for k in range(self.nz):
                pair = []
                for j in range(2):
                    x, y = (j, other) if a == "x" else (other, j)
                    pair.append((x, (y * self.nz + k) * depth))
                spots.append(tuple(pair))
        return Weight(pieces, tuple(spots))

    def scatter(self, keep, send, route):
        whole = jnp.concatenate([keep, send], axis=1)
        if route[0] == "x":
            whole = jnp.stack([keep.reshape(-1, keep.shape[2]), send.reshape(-1, send.shape[2])])
        mine = lax.psum_scatter(whole, "x", scatter_dimension=0, tiled=False)
        return lax.psum_scatter(mine, ("z", "y"), scatter_dimension=0, tiled=True).astype(f32)

    def pair(self, v):
        if not self.routed:
            return lax.all_gather(v, "x", axis=0)
        return jnp.stack([v, self.swap(v, "x")])

    def both_rows(self, v):
        other = self.pc(v)
        first = lax.axis_index("core") == 0
        return jnp.concatenate([jnp.where(first, v, other), jnp.where(first, other, v)])


class Chain:
    last = ()

    def call(self, body, inputs, in_specs, outs, out_specs, flops, vmem, grid=(), scratch=(), after=()):
        waits = [*self.last, *after]
        count = len(inputs)

        def rest(*refs):
            body(*refs[:count], *refs[count + len(waits) :])

        made = pl.pallas_call(
            rest,
            out_shape=[jax.ShapeDtypeStruct(*o) for o in outs],
            grid=grid,
            in_specs=[*in_specs, *[ANY] * len(waits)],
            out_specs=out_specs,
            scratch_shapes=list(scratch),
            compiler_params=pltpu.CompilerParams(vmem_limit_bytes=vmem << 20),
            cost_estimate=pl.CostEstimate(
                flops=4 * flops, bytes_accessed=0, transcendentals=0
            ),
        )(*inputs, *waits)
        self.last = (min(made, key=lambda v: v.size),)
        return made


class Weight:
    def __init__(self, arrays, spots):
        self.arrays = arrays
        self.spots = spots
        self.width = arrays[0].shape[2]

    def specs(self, grid):
        return [fixed(*v.shape) if grid else VMEM for v in self.arrays]

    def join(self, refs, target):
        for piece, places in zip(refs, self.spots):
            rows = piece.shape[1]
            for j, (x, row) in enumerate(places):
                target[x, row : row + rows] = piece[j]


def fold_sums(chain, arrays, wanted):
    inputs = [v for group in arrays for v in group]
    first = [sum(len(group) for group in arrays[:n]) for n in range(len(arrays))]
    outs = []
    for rows, dtype in wanted:
        which, index = rows[0]
        shape = jax.eval_shape(lambda v: v[index], arrays[which][0]).shape
        outs.append((shape if len(rows) == 1 else (len(rows), *shape), dtype))

    def body(*refs):
        for out, (rows, dtype) in zip(refs[len(inputs) :], wanted):
            for n, (which, index) in enumerate(rows):
                group = refs[first[which] : first[which] + len(arrays[which])]
                total = sum(ref[index].astype(f32) for ref in group).astype(dtype)
                if len(rows) == 1:
                    out[...] = total
                else:
                    out[n] = total

    return chain.call(
        body,
        inputs,
        [VMEM] * len(inputs),
        outs,
        [VMEM] * len(outs),
        flops=sum(v.size for v in inputs),
        vmem=12,
    )


class Scatter:
    def __init__(self, chain, links, parts):
        self.chain = chain
        self.links = links
        self.routes = [route for _, _, route in parts]
        self.depth = parts[0][0].shape[1] // links.nz
        if links.routed:
            self.sums = [[keep, links.swap(send, route[0])] for keep, send, route in parts]
        else:
            self.sums = [links.scatter(*part) for part in parts]

    def second(self):
        if not self.links.routed:
            return
        wanted = [([(n, (i,))], bf16 if i else f32) for n in range(len(self.routes)) for i in range(2)]
        made = fold_sums(self.chain, self.sums, wanted)
        self.sums = [
            [made[2 * n], self.links.swap(made[2 * n + 1], route[1])]
            for n, route in enumerate(self.routes)
        ]

    def third(self):
        links = self.links
        if not links.routed:
            return
        wanted = []
        for k in range(links.nz):
            at = (slice(k * self.depth, (k + 1) * self.depth),)
            wanted.append(([(n, at) for n in range(len(self.routes))], bf16 if k else f32))
        made = fold_sums(self.chain, self.sums, wanted)
        self.sums = [made[0]]
        for k in range(1, links.nz):
            to = [(i, (i - k) % links.nz) for i in range(links.nz)]
            self.sums.append(lax.ppermute(made[k], "z", to))

    def finish(self):
        if not self.links.routed:
            return self.sums
        wanted = [([(0, (n,))], f32) for n in range(len(self.routes))]
        return fold_sums(self.chain, [self.sums], wanted)


def centered(rows):
    center = rows - jnp.mean(rows, axis=-1, keepdims=True)
    scale = lax.rsqrt(jnp.mean(center * center, axis=-1, keepdims=True) + epsilon)
    return center * scale, scale


def norm_back(rows, gain, grad):
    unit, scale = centered(rows)
    inner = grad * gain
    first = jnp.mean(inner, axis=-1, keepdims=True)
    second = jnp.mean(inner * unit, axis=-1, keepdims=True)
    back = scale * (inner - first - unit * second)
    return back, jnp.sum(grad * unit, axis=0, keepdims=True), jnp.sum(grad, axis=0, keepdims=True)


def gelu_pair(u):
    root = 0.7978845608028654
    square = u * u
    t = jnp.tanh(root * u * (1.0 + 0.044715 * square))
    half = 0.5 * (1.0 + t)
    slope = half + (0.5 * root) * u * (1.0 - t * t) * (1.0 + (3 * 0.044715) * square)
    return u * half, slope


def bias_block(tiles, head, half):
    rows = []
    for key in range(SEQ // TILE):
        row = []
        for query in range(2 * half, 2 * half + 2):
            row.append(tiles[head, min(max(key - query, -2), 2) + 2])
        rows.append(jnp.concatenate(row, axis=1))
    return jnp.concatenate(rows, axis=0)


def split_heads(block, count):
    return [block[:, HEAD * n : HEAD * (n + 1)] for n in range(count)]


def attn_forward(weight, later, refs):
    n = len(weight.arrays)
    refs = list(refs)
    if later:
        h1_ref, own_ref, other_ref, prm_ref = refs[:4]
        refs = refs[4:]
    else:
        x_ref = refs.pop(0)
    pieces, refs = refs[:n], refs[n:]
    qv_ref, tiles_ref, mask_ref = refs[:3]
    refs = refs[3:]
    if later:
        h_ref, x_ref = refs[:2]
        refs = refs[2:]
    part_ref, q_ref, k_ref, v_ref, o_ref, lse_ref, w_ref, mixed_ref = refs
    rows = 2 * SEQ
    if later:
        gain, shift, bias = prm_ref[3:4], prm_ref[4:5], prm_ref[5:6]

        def norm(i, carry):
            at = pl.ds(pl.multiple_of(i * 128, 128), 128)
            value = h1_ref[at] + own_ref[at].astype(f32) + other_ref[at].astype(f32) + bias
            unit, scale = centered(value)
            result = unit * gain + shift
            h_ref[at] = result
            x_ref[at] = result.astype(bf16)
            return carry

        lax.fori_loop(0, rows // 128, norm, 0)
    weight.join(pieces, w_ref)
    heads = k_ref.shape[0]
    per = heads // 2
    part = per * HEAD
    for x in range(2):
        for stream in range(2):
            block = x_ref[stream * SEQ : (stream + 1) * SEQ]
            width = w_ref.shape[2] if stream == 0 else 256
            result = nn(block, w_ref[x, :, :width])
            query = (result[:, :part] + qv_ref[x, 0:1, :part]).astype(bf16).astype(f32) * 0.125
            for j, one in enumerate(split_heads(query.astype(bf16), per)):
                q_ref[stream * heads + x * per + j] = one
            if stream == 0:
                key = result[:, part : 2 * part].astype(bf16)
                value = (result[:, 2 * part : 3 * part] + qv_ref[x, 1:2, :part]).astype(bf16)
                for j, one in enumerate(split_heads(key, per)):
                    k_ref[x * per + j] = one
                for j, one in enumerate(split_heads(value, per)):
                    v_ref[x * per + j] = one

    def one_head(head, carry):
        key, value = k_ref[head], v_ref[head]
        for half in range(2):
            at = slice(half * 256, half * 256 + 256)
            bias = bias_block(tiles_ref, head, half)
            for stream in range(2):
                query = q_ref[stream * heads + head, at]
                score = nt(key, query) + (bias + mask_ref[stream, :, at])
                top = jnp.max(score, axis=0, keepdims=True)
                raised = jnp.exp(score - top)
                total = jnp.sum(raised, axis=0, keepdims=True)
                mixed = tn(value, raised.astype(bf16)) * (1.0 / total)
                mixed_ref[stream * heads + head, at] = mixed.T.astype(bf16)
                lse_ref[stream * heads + head, :, at] = top + jnp.log(total)
        return carry

    lax.fori_loop(0, heads, one_head, 0)
    for stream in range(2):
        total = None
        for x in range(2):
            blocks = [jnp.zeros((SEQ, HEAD), bf16)]
            blocks += [mixed_ref[stream * heads + x * per + j] for j in range(per)]
            block = jnp.concatenate(blocks, axis=1)
            o_ref[x, stream * SEQ : (stream + 1) * SEQ] = block
            term = nt(block, w_ref[x, :, 512:768])
            total = term if total is None else total + term
        part_ref[stream * SEQ : (stream + 1) * SEQ] = total.astype(bf16)


def run_attn_forward(chain, entering, weight, qv, tiles, mask, after):
    later = len(entering) == 4
    heads = tiles.shape[0]
    width = entering[0].shape[1]
    rows = entering[0].shape[0]
    columns = weight.width
    inputs = [*entering, *weight.arrays, qv, tiles, mask]
    specs = [VMEM] * len(entering) + weight.specs(False) + [VMEM] * 3
    outs = [((rows, width), f32), ((rows, width), bf16)] if later else []
    outs += [
        ((rows, width), bf16),
        ((2 * heads, SEQ, HEAD), bf16),
        ((heads, SEQ, HEAD), bf16),
        ((heads, SEQ, HEAD), bf16),
        ((2, rows, 256), bf16),
        ((2 * heads, 1, SEQ), f32),
    ]
    return chain.call(
        lambda *refs: attn_forward(weight, later, refs),
        inputs,
        specs,
        outs,
        [VMEM] * len(outs),
        flops=14 * 10**9,
        vmem=36,
        scratch=[
            pltpu.VMEM((2, width, weight.width), bf16),
            pltpu.VMEM((2 * heads, SEQ, HEAD), bf16),
        ],
        after=after,
    )


def ffn_forward(up, down, refs):
    h_ref, own_ref, other_ref, prm_ref, bias_ref = refs[:5]
    refs = refs[5:]
    up_pieces, refs = refs[: len(up.arrays)], refs[len(up.arrays) :]
    down_pieces, refs = refs[: len(down.arrays)], refs[len(down.arrays) :]
    ah_ref, h1_ref, fed_ref, act_ref, slope_ref, part_ref = refs[:6]
    up_ref, down_ref = refs[6:]

    @pl.when(pl.program_id(0) == 0)
    def _():
        up.join(up_pieces, up_ref)
        down.join(down_pieces, down_ref)

    gain, shift, bias = prm_ref[0:1], prm_ref[1:2], prm_ref[2:3]
    before = h_ref[...].astype(f32) + own_ref[...].astype(f32) + other_ref[...].astype(f32) + bias
    ah_ref[...] = before
    unit, scale = centered(before)
    normed = unit * gain + shift
    h1_ref[...] = normed
    fed = normed.astype(bf16)
    fed_ref[...] = fed

    total = None
    for x in range(2):
        inner = nn(fed, up_ref[x]) + bias_ref[x]
        act, slope = gelu_pair(inner)
        act = act.astype(bf16)
        act_ref[x] = act
        slope_ref[x] = slope.astype(bf16)
        term = nt(act, down_ref[x])
        total = term if total is None else total + term
    part_ref[...] = total.astype(bf16)


def by_rows(rows, width):
    return pl.BlockSpec((rows, width), lambda i: (i, 0))


def by_rows_pair(rows, width):
    return pl.BlockSpec((2, rows, width), lambda i: (0, i, 0))


def fixed(*shape):
    return pl.BlockSpec(shape, lambda i: (0,) * len(shape))


def run_ffn_forward(chain, entering, params, bias, up, down):
    rows, width = entering[0].shape
    step = 256
    units = up.width
    inputs = [*entering, params, bias, *up.arrays, *down.arrays]
    specs = [by_rows(step, width)] * 3 + [fixed(8, width), fixed(2, 1, units)]
    specs += up.specs(True) + down.specs(True)
    outs = [
        ((rows, width), f32),
        ((rows, width), f32),
        ((rows, width), bf16),
        ((2, rows, units), bf16),
        ((2, rows, units), bf16),
        ((rows, width), bf16),
    ]
    out_specs = [by_rows(step, width)] * 3 + [by_rows_pair(step, units)] * 2
    out_specs += [by_rows(step, width)]
    return chain.call(
        lambda *refs: ffn_forward(up, down, refs),
        inputs,
        specs,
        outs,
        out_specs,
        flops=8 * rows * width * units,
        vmem=30,
        grid=(rows // step,),
        scratch=[
            pltpu.VMEM((2, width, units), bf16),
            pltpu.VMEM((2, width, units), bf16),
        ],
    )


def ffn_backward(up, down, grads, last, refs):
    grad_refs, refs = refs[:grads], refs[grads:]
    h1_ref, own_ref, other_ref, prm_ref, slope_ref = refs[:5]
    refs = refs[5:]
    up_pieces, refs = refs[: len(up.arrays)], refs[len(up.arrays) :]
    down_pieces, refs = refs[: len(down.arrays)], refs[len(down.arrays) :]
    dz_ref, dbh_ref, du_ref, part_ref, sums_ref, up_sums_ref = refs[:6]
    refs = refs[6:]
    if last:
        out_ref, refs = refs[0], refs[1:]
    up_ref, down_ref = refs

    @pl.when(pl.program_id(0) == 0)
    def _():
        up.join(up_pieces, up_ref)
        down.join(down_pieces, down_ref)
        sums_ref[...] = jnp.zeros_like(sums_ref)
        up_sums_ref[...] = jnp.zeros_like(up_sums_ref)

    gain, shift, bias = prm_ref[3:4], prm_ref[4:5], prm_ref[5:6]
    grad = sum(ref[...].astype(f32) for ref in grad_refs)
    after = h1_ref[...] + own_ref[...].astype(f32) + other_ref[...].astype(f32) + bias
    if last:
        unit, scale = centered(after)
        out_ref[...] = (unit * gain + shift).astype(bf16)
    back, gain_sum, shift_sum = norm_back(after, gain, grad)
    dbh_ref[...] = back
    sums_ref[0:1] += gain_sum
    sums_ref[1:2] += shift_sum
    sums_ref[2:3] += jnp.sum(back, axis=0, keepdims=True)
    dz = back.astype(bf16)
    dz_ref[...] = dz

    total = None
    for x in range(2):
        du = (nn(dz, down_ref[x]) * slope_ref[x].astype(f32)).astype(bf16)
        du_ref[x] = du
        up_sums_ref[x] += jnp.sum(du.astype(f32), axis=0, keepdims=True)
        term = nt(du, up_ref[x])
        total = term if total is None else total + term
    part_ref[...] = total.astype(bf16)


def run_ffn_backward(chain, grads, entering, params, slope, up, down, last):
    rows, width = entering[0].shape
    step = 256
    units = up.width
    inputs = [*grads, *entering, params, slope, *up.arrays, *down.arrays]
    specs = [by_rows(step, width)] * (len(grads) + 3)
    specs += [fixed(8, width), by_rows_pair(step, units)]
    specs += up.specs(True) + down.specs(True)
    outs = [
        ((rows, width), bf16),
        ((rows, width), f32),
        ((2, rows, units), bf16),
        ((rows, width), bf16),
        ((8, width), f32),
        ((2, 1, units), f32),
    ]
    out_specs = [by_rows(step, width)] * 2 + [by_rows_pair(step, units), by_rows(step, width)]
    out_specs += [fixed(8, width), fixed(2, 1, units)]
    if last:
        outs.append(((rows, width), bf16))
        out_specs.append(by_rows(step, width))
    return chain.call(
        lambda *refs: ffn_backward(up, down, len(grads), last, refs),
        inputs,
        specs,
        outs,
        out_specs,
        flops=8 * rows * width * units,
        vmem=30,
        grid=(rows // step,),
        scratch=[
            pltpu.VMEM((2, width, units), bf16),
            pltpu.VMEM((2, width, units), bf16),
        ],
    )


def fold(near):
    within = lax.broadcasted_iota(jnp.int32, (8, TILE), 0)
    lane = lax.broadcasted_iota(jnp.int32, (8, TILE), 1)
    zero = jnp.zeros((8, TILE), f32)

    def aligned(rows, at):
        rows = pltpu.roll(rows, (TILE - at) % TILE, 1)
        for bit in (1, 2, 4):
            rows = jnp.where((within & bit) != 0, pltpu.roll(rows, TILE - bit, 1), rows)
        return rows

    same = after = far_before = far_after = zero
    for at in range(0, TILE, 8):
        upper = within + lane < TILE - at
        one, two, three = (aligned(near[i][at : at + 8], at) for i in (1, 2, 3))
        same += jnp.where(upper, two, one)
        after += jnp.where(upper, three, two)
        far_before += near[0][at : at + 8] + jnp.where(upper, one, zero)
        far_after += near[4][at : at + 8] + jnp.where(upper, zero, three)
    sums = [jnp.sum(v, axis=0, keepdims=True) for v in (same, after, far_before, far_after)]
    return jnp.concatenate([*sums, jnp.zeros((4, TILE), f32)])


def attn_backward(weight, refs):
    n = len(weight.arrays)
    dbh_ref, own_ref, other_ref, ah_ref, prm_ref = refs[:5]
    pieces, refs = refs[5 : 5 + n], refs[5 + n :]
    q_ref, k_ref, v_ref, lse_ref, tiles_ref, mask_ref = refs[:6]
    refs = refs[6:]
    dah_ref, dy_ref, dcat_ref, dqg_ref, part_ref, near_ref, sums_ref, col_ref = refs[:8]
    w_ref, do_ref, dq_ref, dk_ref, dv_ref = refs[8:]
    rows = 2 * SEQ
    gain = prm_ref[0:1]
    sums_ref[...] = jnp.zeros_like(sums_ref)

    def norm(i, carry):
        at = pl.ds(pl.multiple_of(i * 128, 128), 128)
        grad = dbh_ref[at] + own_ref[at].astype(f32) + other_ref[at].astype(f32)
        back, gain_sum, shift_sum = norm_back(ah_ref[at], gain, grad)
        dah_ref[at] = back
        dy_ref[at] = back.astype(bf16)
        sums_ref[0:1] += gain_sum
        sums_ref[1:2] += shift_sum
        sums_ref[2:3] += jnp.sum(back, axis=0, keepdims=True)
        return carry

    lax.fori_loop(0, rows // 128, norm, 0)
    weight.join(pieces, w_ref)
    heads = k_ref.shape[0]
    per = heads // 2
    for stream in range(2):
        at = slice(stream * SEQ, (stream + 1) * SEQ)
        for x in range(2):
            block = nn(dy_ref[at], w_ref[x, :, 512:768]).astype(bf16)
            for j in range(per):
                do_ref[stream * heads + x * per + j] = block[:, HEAD * (1 + j) : HEAD * (2 + j)]

    def one_head(head, carry):
        key, value = k_ref[head], v_ref[head]
        grad_key = jnp.zeros((SEQ, HEAD), f32)
        grad_value = jnp.zeros((SEQ, HEAD), f32)
        near = [jnp.zeros((TILE, TILE), f32) for _ in range(NEAR)]
        for half in range(2):
            at = slice(half * 256, half * 256 + 256)
            bias = bias_block(tiles_ref, head, half)
            for stream in range(2):
                spot = stream * heads + head
                query, grad_out = q_ref[spot, at], do_ref[spot, at]
                score = nt(key, query) + (bias + mask_ref[stream, :, at])
                prob = jnp.exp(score - lse_ref[spot, :, at])
                both = prob * nt(value, grad_out)
                inner = jnp.sum(both, axis=0, keepdims=True)
                grad_score = (both - prob * inner).astype(bf16)
                grad_value += nn(prob.astype(bf16), grad_out)
                grad_key += nn(grad_score, query)
                dq_ref[spot, at] = (tn(key, grad_score) * 0.125).T.astype(bf16)
                wide = grad_score.astype(f32)
                for k in range(SEQ // TILE):
                    for q in range(2):
                        which = min(max(k - (2 * half + q), -2), 2) + 2
                        near[which] += wide[
                            k * TILE : (k + 1) * TILE, q * TILE : (q + 1) * TILE
                        ]
        near_ref[head] = fold(near)
        dk_ref[head] = grad_key.astype(bf16)
        dv_ref[head] = grad_value.astype(bf16)
        return carry

    lax.fori_loop(0, heads, one_head, 0)
    total_h = total_g = None
    for x in range(2):
        near = range(x * per, (x + 1) * per)
        blocks = [dq_ref[j] for j in near] + [dk_ref[j] for j in near] + [dv_ref[j] for j in near]
        blocks += [jnp.zeros((SEQ, HEAD), bf16)] * per
        block = jnp.concatenate(blocks, axis=1)
        dcat_ref[x] = block
        term = nt(block, w_ref[x])
        total_h = term if total_h is None else total_h + term
        col_ref[x, 0:1] = jnp.sum(block.astype(f32), axis=0, keepdims=True)
        blocks = [dq_ref[heads + j] for j in near] + [jnp.zeros((SEQ, HEAD), bf16)]
        block = jnp.concatenate(blocks, axis=1)
        dqg_ref[x] = block
        term = nt(block, w_ref[x, :, :256])
        total_g = term if total_g is None else total_g + term
        col_ref[x, 1:2, :256] = jnp.sum(block.astype(f32), axis=0, keepdims=True)
    part_ref[:SEQ] = total_h.astype(bf16)
    part_ref[SEQ:] = total_g.astype(bf16)


def run_attn_backward(chain, entering, params, weight, saved, tiles, mask):
    rows, width = entering[0].shape
    heads = tiles.shape[0]
    columns = weight.width
    q, k, v, _, lse = saved
    inputs = [*entering, params, *weight.arrays, q, k, v, lse, tiles, mask]
    specs = [VMEM] * 5 + weight.specs(False) + [VMEM] * 6
    outs = [
        ((rows, width), f32),
        ((rows, width), bf16),
        ((2, SEQ, columns), bf16),
        ((2, SEQ, 256), bf16),
        ((rows, width), bf16),
        ((heads, 8, TILE), f32),
        ((8, width), f32),
        ((2, 8, columns), f32),
    ]
    return chain.call(
        lambda *refs: attn_backward(weight, refs),
        inputs,
        specs,
        outs,
        [VMEM] * len(outs),
        flops=20 * 10**9,
        vmem=40,
        scratch=[
            pltpu.VMEM((2, width, weight.width), bf16),
            pltpu.VMEM((2 * heads, SEQ, HEAD), bf16),
            pltpu.VMEM((2 * heads, SEQ, HEAD), bf16),
            pltpu.VMEM((heads, SEQ, HEAD), bf16),
            pltpu.VMEM((heads, SEQ, HEAD), bf16),
        ],
    )


def quarters(part, first):
    return [(part, x) for x in range(2)] if first == "y" else [(y, part) for y in range(2)]


def ffn_grads(chain, fed, du, dz, act, part, up_first, down_first):
    rows, width = fed.shape
    units = du.shape[2]
    half = width // 2

    def body(fed_ref, du_ref, dz_ref, act_ref, up_ref, down_ref):
        for left, right, out, first in (
            (fed_ref, du_ref, up_ref, up_first),
            (dz_ref, act_ref, down_ref, down_first),
        ):
            for n, (y, x) in enumerate(quarters(part, first)):
                out[n] = tn(left[:, y * half : (y + 1) * half], right[x]).astype(bf16)

    return chain.call(
        body,
        [fed, du, dz, act],
        [VMEM] * 4,
        [((2, half, units), bf16)] * 2,
        [VMEM] * 2,
        flops=8 * rows * half * units,
        vmem=20,
    )


def attn_grads(chain, x, dcat, dqg, dy, o, part, firsts):
    rows, width = x.shape
    half = width // 2
    columns = dcat.shape[2]
    span = columns // len(firsts)

    def body(x_ref, dcat_ref, dqg_ref, dy_ref, o_ref, *outs):
        for y in range(2):
            at = slice(y * half, (y + 1) * half)
            for n, first in enumerate(firsts):
                for place, (want, other) in enumerate(quarters(part, first)):
                    if want != y:
                        continue
                    low, high = n * span, (n + 1) * span
                    total = tn(x_ref[:SEQ, at], dcat_ref[other, :, low:high])
                    outs[n][place] = total.astype(bf16)
                    if n == 0:
                        query = total[:, :256] + tn(x_ref[SEQ:, at], dqg_ref[other])
                        outs[n][place, :, :256] = query.astype(bf16)
                    if n == len(firsts) - 1:
                        out = total[:, span - 256 :] + tn(dy_ref[:, at], o_ref[other])
                        outs[n][place, :, span - 256 :] = out.astype(bf16)

    return chain.call(
        body,
        [x, dcat, dqg, dy, o],
        [VMEM] * 5,
        [((2, half, span), bf16)] * len(firsts),
        [VMEM] * len(firsts),
        flops=6 * rows * half * columns,
        vmem=20,
    )


def exact(rows, right, product):
    total = None
    for _ in range(3):
        top = rows.astype(bf16)
        rows = rows - top.astype(f32)
        term = product(top, right)
        total = term if total is None else total + term
    return total


SMALL = 8


def finish_rows(chain, core, swapper, fold_hot, groups, smalls):
    rows, width = groups[0][0].shape
    own = rows // 4
    flat = [v for group in groups for v in group]
    counts = [len(group) for group in groups]
    layers = len(smalls) // 5
    heads = smalls[0].shape[0]
    per = heads // 2

    def body(core_ref, swapper_ref, hot_ref, *refs):
        ins, small_ins = refs[: len(flat)], refs[len(flat) : len(flat) + len(smalls)]
        outs = refs[len(flat) + len(smalls) :]
        at = pl.multiple_of(core_ref[0] * own, own)
        first = 0
        for count, out in zip(counts, outs):
            for stream in range(2):
                total = sum(
                    ref[pl.ds(at + stream * SEQ, own)].astype(f32)
                    for ref in ins[first : first + count]
                )
                out[stream] = nt(total.astype(bf16), swapper_ref[...]).astype(bf16)
            first += count
        sides = outs[len(counts) :]
        edge = layers * SMALL
        for layer in range(layers):
            near, cols, one, two, up = small_ins[5 * layer : 5 * layer + 5]
            for x, side in enumerate(sides):
                base = layer * SMALL
                side[base : base + SMALL] = jnp.zeros((SMALL, width), f32)
                side[base : base + 1] = cols[x, 0:1]
                side[base : base + 1, :256] = cols[x, 0:1, :256] + cols[x, 1:2, :256]
                side[base + 1 : base + 2] = up[x]
                for j in range(per):
                    table = None
                    for n in range(4):
                        hot = hot_ref[n * TILE : (n + 1) * TILE]
                        term = exact(near[x * per + j], hot, nn)[n : n + 1]
                        table = term if table is None else table + term
                    side[base + 2 + j : base + 3 + j, :TILE] = table
            sums = jnp.concatenate([one[...], two[...]])
            back = exact(sums, swapper_ref[...], nt)
            for side in sides:
                base = edge + layer * SMALL
                for n in range(3):
                    side[base + 2 * n : base + 2 * n + 1] = back[n : n + 1]
                    side[base + 2 * n + 1 : base + 2 * n + 2] = back[SMALL + n : SMALL + n + 1]
                side[base + 6 : base + 8] = jnp.zeros((2, width), f32)

    shape = ((2 * layers * SMALL, width), f32)
    made = chain.call(
        body,
        [core, swapper, fold_hot, *flat, *smalls],
        [pl.BlockSpec(memory_space=pltpu.SMEM)] + [VMEM] * (2 + len(flat) + len(smalls)),
        [((2, own, width), bf16)] * len(groups) + [shape] * 2,
        [VMEM] * (len(groups) + 2),
        flops=4 * own * width * width * len(groups),
        vmem=24,
    )
    return made[: len(groups)], made[len(groups)], made[len(groups) + 1]


def small_grads(value, part, per):
    layers = value.shape[0] // (2 * SMALL)
    base = [layer * SMALL for layer in range(layers)]
    far = [layers * SMALL + b for b in base]
    return [
        [value[b : b + 1, :part] for b in base],
        [value[b : b + 1, 2 * part : 3 * part] for b in base],
        [value[b + 1 : b + 2] for b in base],
        [value[b + 2 : b + 2 + per, :BUCKETS] for b in base],
        *[[value[b + 2 * n : b + 2 * n + 2] for b in far] for n in range(3)],
    ]


def add_pair(chain, a, b):
    def body(one, two, out):
        out[...] = one[...] + two[...]

    return chain.call(body, [a, b], [VMEM] * 2, [(a.shape, f32)], [VMEM], flops=10**5, vmem=4)[0]


def all_grads(chain, part, per, attn_sums, attn_old, ffn_sums, ffn_old, small):
    groups = [*attn_sums, *ffn_sums]
    depth, units = ffn_old[0].shape
    width = small[0].shape[1]
    layers = 2

    def body(*refs):
        ins, outs = refs[: len(groups) + 6], refs[len(groups) + 6 :]
        attn_refs, rest = ins[: len(attn_sums)], ins[len(attn_sums) :]
        ffn_refs, (low, high, up, down, one, two) = rest[: len(ffn_sums)], rest[len(ffn_sums) :]

        def total(of, n):
            return sum(ref[n].astype(f32) for ref in of)

        for layer in range(layers):
            if layer == 0:
                attn = [total(attn_refs, n) for n in range(2)]
                ffn = [total(ffn_refs, n) for n in range(2)]
            else:
                attn, ffn = [low[...], high[...]], [up[...], down[...]]
            outs[0][layer] = attn[0][:, :part]
            outs[1][layer] = attn[0][:, part:]
            outs[2][layer] = attn[1][:, :part]
            outs[3][layer] = attn[1][:, part:].T
            outs[4][layer] = ffn[0]
            outs[5][layer] = ffn[1].T
        made = small_grads(one[...] + two[...], part, per)
        for n, values in enumerate(made):
            for layer in range(layers):
                if n < 3:
                    outs[6 + n][layer : layer + 1] = values[layer]
                else:
                    outs[6 + n][layer] = values[layer]

    shapes = [(layers, depth, part)] * 3 + [(layers, part, depth), (layers, depth, units)]
    shapes += [(layers, units, depth), (layers, part), (layers, part), (layers, units)]
    shapes += [(layers, per, BUCKETS)] + [(layers, 2, width)] * 3
    return chain.call(
        body,
        [*groups, *attn_old, *ffn_old, *small],
        [VMEM] * (len(groups) + 6),
        [(shape, f32) for shape in shapes],
        [VMEM] * len(shapes),
        flops=10**6,
        vmem=16,
    )


def local(links, *arguments):
    (
        h_in,
        g_in,
        lengths,
        order,
        predicted,
        w_query,
        w_key,
        w_value,
        w_out,
        w_up,
        w_down,
        q_bias,
        v_bias,
        up_bias,
        rel_table,
        norm_gain,
        norm_shift,
        out_bias,
        h_cot,
        g_cot,
    ) = arguments
    rows_own, model = h_in.shape
    part = w_query.shape[2]
    units = w_up.shape[2]
    heads = 2 * rel_table.shape[1]
    table_size = rel_table.shape[1] * BUCKETS
    slot = lax.axis_index("x")
    core = lax.axis_index("core")

    chain = Chain()
    gathered = []
    for layer in range(LAYERS):
        attn = jnp.concatenate(
            [w_query[layer], w_key[layer], w_value[layer], w_out[layer].T], axis=1
        )
        blocks = (attn, w_up[layer], w_down[layer].T)
        gathered.append([links.gather(b, r) for b, r in zip(blocks, GATHER[layer])])

    def pick(v):
        return lax.dynamic_index_in_dim(v, slot, 0, keepdims=False)

    mask = slot_masks(pick(lengths), pick(order), pick(predicted))
    onehot = (
        jnp.arange(BUCKETS, dtype=jnp.int32)[:, None] == tile_buckets().reshape(1, -1)
    ).astype(f32)

    lanes = jnp.arange(TILE, dtype=jnp.int32)
    edge = jnp.full_like(lanes, TILE)
    fold_buckets = bucket_of(jnp.concatenate([-lanes, TILE - lanes, -edge, edge]))
    fold_hot = (fold_buckets[:, None] == lanes[None, :]).astype(bf16)

    small = links.pair(
        jnp.concatenate(
            [q_bias, v_bias, up_bias, rel_table.reshape(LAYERS, table_size)], axis=1
        )
    )
    tables = small[:, :, 2 * part + units :].transpose(1, 0, 2).reshape(LAYERS * heads, BUCKETS)
    tiles = jnp.dot(tables, onehot, precision=highest).reshape(LAYERS, heads, NEAR, TILE, TILE)
    qv = jnp.stack([small[:, :, :part], small[:, :, part : 2 * part]], axis=2)
    qv = jnp.pad(qv, ((0, 0), (0, 0), (0, 6), (0, 256 - part)))
    bias_up = small[:, :, None, 2 * part : 2 * part + units]

    features = links.feature_order(model)
    swapper = (jnp.arange(model, dtype=jnp.int32)[:, None] == features[None, :]).astype(bf16)
    swapper32 = swapper.astype(f32)
    params = jnp.dot(
        jnp.stack([norm_gain, norm_shift, out_bias], axis=2).reshape(-1, model),
        swapper32,
        precision=highest,
    ).reshape(LAYERS, 6, model)
    params = jnp.pad(params, ((0, 0), (0, 2), (0, 0)))

    def ordered(first, second):
        rows = links.both_rows(jnp.concatenate([first, second], axis=1))
        both = jnp.concatenate([rows[:, :model], rows[:, model:]], axis=0)
        return nn(both, swapper).astype(bf16)

    entering = ordered(h_in, g_in)
    kept = []
    for layer in range(LAYERS):
        attn, up, down = gathered[layer]
        if layer == 0:
            x = stream = entering
            before = (entering,)
            after = []
            if links.routed:
                after = [v for w in (up, down, *gathered[1]) for v in w.arrays]
        else:
            before = (h1, part_own, part_other, params[layer - 1])
            after = []
        made = run_attn_forward(chain, before, attn, qv[:, layer], tiles[layer], mask, after)
        if layer > 0:
            stream, x = made[:2]
            made = made[2:]
        mixed_own, q, k, v, o, lse = made
        ah, h1, fed, act, slope, part_own = run_ffn_forward(
            chain, (stream, mixed_own, links.pc(mixed_own)), params[layer], bias_up[:, layer], up, down
        )
        part_other = links.pc(part_own)
        kept.append((x, (q, k, v, o, lse), ah, (h1, part_own, part_other), fed, act, slope))
    grads = (ordered(h_cot, g_cot),)
    smalls = []
    for layer in range(LAYERS - 1, -1, -1):
        attn, up, down = gathered[layer]
        firsts = [r[0] for r in SCATTER]
        x, saved, ah, second, fed, act, slope = kept[layer]
        last = layer == LAYERS - 1
        made = run_ffn_backward(chain, grads, second, params[layer], slope, up, down, last)
        dz, dbh, du, part_own, sums_two, up_sums = made[:6]
        if last:
            result = made[6]
        part_other = links.pc(part_own)
        if not last:
            attn_way.second()
        sent = ffn_grads(chain, fed, du, dz, act, 1, *firsts)
        held = ffn_grads(chain, fed, du, dz, act, 0, *firsts)
        if not last:
            attn_way.third()
            done_ffn = ffn_way.finish()
            old_attn = attn_way
        ffn_way = Scatter(chain, links, list(zip(held, sent, SCATTER)))
        dah, dy, dcat, dqg, part_own, near, sums_one, cols = run_attn_backward(
            chain, (dbh, part_own, part_other, ah), params[layer], attn, saved, tiles[layer], mask
        )
        part_other = links.pc(part_own)
        if not last:
            done_attn = old_attn.finish()
        ffn_way.second()
        sent = attn_grads(chain, x, dcat, dqg, dy, saved[3], 1, firsts)
        held = attn_grads(chain, x, dcat, dqg, dy, saved[3], 0, firsts)
        attn_way = Scatter(chain, links, list(zip(held, sent, SCATTER)))
        if last:
            ffn_way.third()
        smalls += [near, cols, sums_one, sums_two, up_sums]
        grads = (dah, part_own, part_other)
    smalls = smalls[5:] + smalls[:5]
    final, kept_small, sent_small = finish_rows(
        chain, jnp.full((1,), core, jnp.int32), swapper, fold_hot, [(result,), grads], smalls
    )
    per = heads // 2
    if links.routed:
        other = links.swap(sent_small, "x")
        ffn_way.third()
        attn_way.second()
        value = add_pair(chain, kept_small, other)
        other = links.swap(value, "y")
        attn_way.third()
        value = add_pair(chain, value, other)
        step = 1
        while step < links.nz // 2:
            value = value + lax.ppermute(value, "z", [(i, i ^ step) for i in range(links.nz)])
            step *= 2
        other = lax.ppermute(value, "z", [(i, i ^ step) for i in range(links.nz)])
        small = (value, other)
        owned = all_grads(chain, part, per, attn_way.sums, done_attn, ffn_way.sums, done_ffn, small)
    else:
        attn_sum = jnp.stack([jnp.concatenate(v, axis=1) for v in (attn_way.sums, done_attn)])
        up_sum, down_sum = (jnp.stack([ffn_way.sums[n], done_ffn[n]]) for n in range(2))
        owned = [attn_sum[:, :, n * part : (n + 1) * part] for n in range(4)] + [up_sum, down_sum]
        owned[3] = owned[3].transpose(0, 2, 1)
        owned[5] = owned[5].transpose(0, 2, 1)
        edge = LAYERS * SMALL
        split = lax.psum_scatter(jnp.stack([kept_small[:edge], sent_small[:edge]]), "x")
        value = jnp.concatenate(
            [lax.psum(split, ("z", "y")), lax.psum(kept_small[edge:], ("z", "y", "x"))]
        )
        for n, values in enumerate(small_grads(value, part, per)):
            owned.append(jnp.concatenate(values) if n < 3 else jnp.stack(values))
    return (
        final[0][0],
        final[0][1],
        final[1][0],
        final[1][1],
        *owned,
    )


def solution(mesh):
    links = Links(mesh)
    rows = P(("z", "y", "x", "core"), None)
    by_dp = P(("z", "y"), None)
    wide = P(None, ("z", "y"), ("x", "core"))
    tall = P(None, ("x", "core"), ("z", "y"))
    by_tensor = P(None, ("x", "core"))
    table = P(None, ("x", "core"), None)
    weights = (wide, wide, wide, tall, wide, tall)
    owned = (by_tensor, by_tensor, by_tensor, table, P(), P(), P())
    return jax.shard_map(
        functools.partial(local, links),
        mesh=links.mesh,
        in_specs=(rows, rows, by_dp, by_dp, by_dp) + weights + owned + (rows, rows),
        out_specs=(rows, rows, rows, rows) + weights + owned,
        check_vma=False,
    )
```

```python
import functools

import jax
import jax.numpy as jnp
from jax import lax
from jax.experimental import pallas as pl
from jax.experimental.pallas import tpu as pltpu
from jax.sharding import Mesh, PartitionSpec as P

HEAD = 64
BUCKETS = 32
LAYERS = 2
SEQ = 512
TILE = 128
NEAR = 5

epsilon = 1e-05
limits = (12, 16, 23, 32, 46, 64, 91)
highest = lax.Precision.HIGHEST
f32 = jnp.float32
bf16 = jnp.bfloat16
SWAP = [(0, 1), (1, 0)]
GATHER = ("zxy", "xzy", "yzx")
SCATTER = ("xyz", "yxz")
ANY = pl.BlockSpec(memory_space=pl.ANY)
VMEM = pl.BlockSpec(memory_space=pltpu.VMEM)


def dot(left, right, numbers):
    return lax.dot_general(left, right, (numbers, ((), ())), preferred_element_type=f32)


def nn(left, right):
    return dot(left, right, ((1,), (0,)))


def nt(left, right):
    return dot(left, right, ((1,), (1,)))


def tn(left, right):
    return dot(left, right, ((0,), (0,)))


def bucket_of(offset):
    distance = jnp.abs(offset)
    farther = 8 + sum(((distance >= border).astype(jnp.int32) for border in limits))
    return jnp.where(distance < 8, distance, farther) + 16 * (offset > 0).astype(jnp.int32)


def slot_masks(piece_lengths, ranks, chosen):
    places = jnp.arange(SEQ, dtype=jnp.int32)
    first = piece_lengths[0]
    second = first + piece_lengths[1]
    third = second + piece_lengths[2]
    segment = (
        (places >= first).astype(jnp.int32)
        + (places >= second).astype(jnp.int32)
        + (places >= third).astype(jnp.int32)
    )
    leading = jnp.where(
        segment == 0,
        0,
        jnp.where(segment == 1, first, jnp.where(segment == 2, second, third)),
    )
    same_doc = segment[:, None] == segment[None, :]
    visible = chosen[:, None] == 0
    content = same_doc & (visible | (ranks[:, None] <= ranks[None, :]))
    query = same_doc & (
        (places[:, None] == leading[None, :])
        | visible & (places[:, None] != places[None, :])
        | (ranks[:, None] < ranks[None, :])
    )
    return jnp.where(jnp.stack([content, query]), 0.0, -1e30).astype(f32)


def tile_buckets():
    near = jnp.arange(NEAR, dtype=jnp.int32)[:, None, None] - NEAR // 2
    key = jnp.arange(TILE, dtype=jnp.int32)[None, :, None]
    query = jnp.arange(TILE, dtype=jnp.int32)[None, None, :]
    return bucket_of(near * TILE + key - query)


class Links:
    def __init__(self, mesh):
        dp = mesh.shape["dp"]
        self.routed = dp == 8
        self.ny = 2
        self.nz = dp // 2
        self.nx = mesh.shape["tensor"] // 2
        self.mesh = Mesh(
            mesh.devices.reshape(self.nz, self.ny, self.nx, 2), ("z", "y", "x", "core")
        )
        self.ring = [(i, (i + 1) % self.nz) for i in range(self.nz)]

    def swap(self, v, axis):
        return lax.ppermute(v, axis, SWAP)

    def pz(self, v):
        return lax.ppermute(v, "z", self.ring)

    def across(self, v, step):
        return lax.ppermute(v, "z", [(i, i ^ step) for i in range(self.nz)])

    def turn(self):
        z = lax.axis_index("z")
        far = [jnp.bitwise_xor(z, k) for k in (1, 3)]
        return jnp.stack([lax.rem(z - f + self.nz, self.nz) for f in far]).astype(jnp.int32)

    def pc(self, v):
        return lax.ppermute(v, "core", SWAP)

    def feature_order(self, width):
        count = self.nz * self.ny
        depth = width // count
        place = jnp.arange(width, dtype=jnp.int32)
        if not self.routed:
            return place
        block, rest = place // depth, place % depth
        ky, kz = block // self.nz, block % self.nz
        z = lax.rem(lax.axis_index("z") - kz + self.nz, self.nz)
        y = jnp.bitwise_xor(lax.axis_index("y"), ky)
        return (z * self.ny + y) * depth + rest

    def gather(self, block, route):
        if not self.routed:
            rows = lax.all_gather(block, ("z", "y"), axis=0, tiled=True)
            return Weight([lax.all_gather(rows, "x", axis=0)], (((0, 0), (1, 0)),))
        depth = block.shape[0]
        a, b = route.replace("z", "")
        held = [block if route[0] == "z" else jnp.stack([block, self.swap(block, a)])]
        for _ in range(self.nz - 1):
            held.append(self.pz(held[-1]))
        if route[0] == "z":
            held = [jnp.stack([h, self.swap(h, a)]) for h in held]
        pieces = held + [self.swap(h, b) for h in held]
        spots = []
        for other in range(2):
            for k in range(self.nz):
                pair = []
                for j in range(2):
                    x, y = (j, other) if a == "x" else (other, j)
                    pair.append((x, (y * self.nz + k) * depth))
                spots.append(tuple(pair))
        return Weight(pieces, tuple(spots))

    def gather_far(self, blocks):
        if not self.routed:
            return [self.gather(block, "") for block in blocks]
        depth, width = blocks[0].shape
        whole = lax.all_gather(jnp.concatenate(blocks, axis=1), ("z", "y", "x"), axis=0)
        places, spots = [], []
        z, y, x = (lax.axis_index(name) for name in ("z", "y", "x"))
        for other in range(self.nx):
            for ky in range(self.ny):
                for kz in range(self.nz):
                    far = lax.rem(z - kz + self.nz, self.nz) * self.ny + jnp.bitwise_xor(y, ky)
                    places.append(far * self.nx + jnp.bitwise_xor(x, other))
                    spots.append((other, (ky * self.nz + kz) * depth))
        places = jnp.stack(places).astype(jnp.int32)
        return [FarWeight(whole, places, spots, n, width) for n in range(len(blocks))]

    def scatter(self, keep, send, route):
        whole = jnp.concatenate([keep, send], axis=1)
        if route[0] == "x":
            whole = jnp.stack([keep.reshape(-1, keep.shape[2]), send.reshape(-1, send.shape[2])])
        mine = lax.psum_scatter(whole, "x", scatter_dimension=0, tiled=False)
        return lax.psum_scatter(mine, ("z", "y"), scatter_dimension=0, tiled=True).astype(f32)

    def pair(self, v):
        if not self.routed:
            return lax.all_gather(v, "x", axis=0)
        return jnp.stack([v, self.swap(v, "x")])

    def both_rows(self, v):
        other = self.pc(v)
        first = lax.axis_index("core") == 0
        return jnp.concatenate([jnp.where(first, v, other), jnp.where(first, other, v)])


class Chain:
    last = ()

    def call(self, body, inputs, in_specs, outs, out_specs, flops, vmem, grid=(), scratch=(), after=()):
        waits = [*self.last, *after]
        count = len(inputs)

        def rest(*refs):
            body(*refs[:count], *refs[count + len(waits) :])

        made = pl.pallas_call(
            rest,
            out_shape=[jax.ShapeDtypeStruct(*o) for o in outs],
            grid=grid,
            in_specs=[*in_specs, *[ANY] * len(waits)],
            out_specs=out_specs,
            scratch_shapes=list(scratch),
            compiler_params=pltpu.CompilerParams(vmem_limit_bytes=vmem << 20),
            cost_estimate=pl.CostEstimate(
                flops=4 * flops, bytes_accessed=0, transcendentals=0
            ),
        )(*inputs, *waits)
        self.last = (min(made, key=lambda v: v.size),)
        return made


class Weight:
    def __init__(self, arrays, spots):
        self.arrays = arrays
        self.spots = spots
        self.width = arrays[0].shape[2]

    def specs(self, grid):
        return [fixed(*v.shape) if grid else VMEM for v in self.arrays]

    def start(self, refs, target, sems):
        for piece, places in zip(refs, self.spots):
            rows = piece.shape[1]
            for j, (x, row) in enumerate(places):
                target[x, row : row + rows] = piece[j]

    def finish(self, refs, target, sems):
        pass


class FarWeight:
    def __init__(self, whole, places, spots, number, width):
        self.arrays = [whole, places]
        self.spots = spots
        self.number = number
        self.width = width

    def specs(self, grid):
        return [
            pl.BlockSpec(memory_space=pltpu.HBM),
            pl.BlockSpec(memory_space=pltpu.SMEM),
        ]

    def copies(self, refs, target, sems):
        whole, places = refs
        rows = whole.shape[1]
        columns = pl.ds(self.number * self.width, self.width)
        return [
            pltpu.make_async_copy(
                whole.at[places[n], :, columns], target.at[x, pl.ds(row, rows), :], sems.at[n]
            )
            for n, (x, row) in enumerate(self.spots)
        ]

    def start(self, refs, target, sems):
        for c in self.copies(refs, target, sems):
            c.start()

    def finish(self, refs, target, sems):
        for c in self.copies(refs, target, sems):
            c.wait()


def fold_sums(chain, arrays, wanted):
    inputs = [v for group in arrays for v in group]
    first = [sum(len(group) for group in arrays[:n]) for n in range(len(arrays))]
    outs = []
    for rows, dtype in wanted:
        which, index = rows[0]
        shape = jax.eval_shape(lambda v: v[index], arrays[which][0]).shape
        outs.append((shape if len(rows) == 1 else (len(rows), *shape), dtype))

    def body(*refs):
        for out, (rows, dtype) in zip(refs[len(inputs) :], wanted):
            for n, (which, index) in enumerate(rows):
                group = refs[first[which] : first[which] + len(arrays[which])]
                total = sum(ref[index].astype(f32) for ref in group).astype(dtype)
                if len(rows) == 1:
                    out[...] = total
                else:
                    out[n] = total

    return chain.call(
        body,
        inputs,
        [VMEM] * len(inputs),
        outs,
        [VMEM] * len(outs),
        flops=sum(v.size for v in inputs),
        vmem=12,
    )


class Scatter:
    def __init__(self, chain, links, parts):
        self.chain = chain
        self.links = links
        self.routes = [route for _, _, route in parts]
        self.depth = parts[0][0].shape[1] // links.nz
        if links.routed:
            self.sums = [[keep, links.swap(send, route[0])] for keep, send, route in parts]
        else:
            self.sums = [links.scatter(*part) for part in parts]

    def second(self):
        if not self.links.routed:
            return
        wanted = [([(n, (i,))], bf16 if i else f32) for n in range(len(self.routes)) for i in range(2)]
        made = fold_sums(self.chain, self.sums, wanted)
        self.sums = [
            [made[2 * n], self.links.swap(made[2 * n + 1], route[1])]
            for n, route in enumerate(self.routes)
        ]

    def third(self):
        links = self.links
        if not links.routed:
            return
        depth = self.depth
        count = len(self.sums)
        columns = self.sums[0][0].shape[1]

        def body(turn, *refs):
            ins, (keep, send) = refs[: 2 * count], refs[2 * count :]
            for n in range(count):
                held, got = ins[2 * n : 2 * n + 2]
                for i in range(2):
                    at = slice(2 * i * depth, (2 * i + 1) * depth)
                    keep[i, n] = held[at].astype(f32) + got[at].astype(f32)
                    at = pl.ds(pl.multiple_of(turn[i] * depth, 32), depth)
                    send[i, n] = (held[at].astype(f32) + got[at].astype(f32)).astype(bf16)

        shape = (2, count, depth, columns)
        keep, send = self.chain.call(
            body,
            [links.turn(), *self.sums[0], *self.sums[1]],
            [pl.BlockSpec(memory_space=pltpu.SMEM)] + [VMEM] * (2 * count),
            [(shape, f32), (shape, bf16)],
            [VMEM] * 2,
            flops=10**6,
            vmem=12,
        )
        self.sums = [keep, links.across(send, 1)]

    def fourth(self):
        if not self.links.routed:
            return
        wanted = [([(0, (i,))], bf16 if i else f32) for i in range(2)]
        keep, send = fold_sums(self.chain, [self.sums], wanted)
        self.sums = [keep, self.links.across(send, 2)]

    def finish(self):
        if not self.links.routed:
            return self.sums
        wanted = [([(0, (n,))], f32) for n in range(len(self.routes))]
        return fold_sums(self.chain, [self.sums], wanted)


def centered(rows):
    center = rows - jnp.mean(rows, axis=-1, keepdims=True)
    scale = lax.rsqrt(jnp.mean(center * center, axis=-1, keepdims=True) + epsilon)
    return center * scale, scale


def norm_back(rows, gain, grad):
    unit, scale = centered(rows)
    inner = grad * gain
    first = jnp.mean(inner, axis=-1, keepdims=True)
    second = jnp.mean(inner * unit, axis=-1, keepdims=True)
    back = scale * (inner - first - unit * second)
    return back, jnp.sum(grad * unit, axis=0, keepdims=True), jnp.sum(grad, axis=0, keepdims=True)


def gelu_pair(u):
    root = 0.7978845608028654
    square = u * u
    t = jnp.tanh(root * u * (1.0 + 0.044715 * square))
    half = 0.5 * (1.0 + t)
    slope = half + (0.5 * root) * u * (1.0 - t * t) * (1.0 + (3 * 0.044715) * square)
    return u * half, slope


def bias_block(tiles, head, half):
    rows = []
    for key in range(SEQ // TILE):
        row = []
        for query in range(2 * half, 2 * half + 2):
            row.append(tiles[head, min(max(key - query, -2), 2) + 2])
        rows.append(jnp.concatenate(row, axis=1))
    return jnp.concatenate(rows, axis=0)


def split_heads(block, count):
    return [block[:, HEAD * n : HEAD * (n + 1)] for n in range(count)]


def attn_forward(weight, later, refs):
    n = len(weight.arrays)
    refs = list(refs)
    if later:
        h1_ref, own_ref, other_ref, prm_ref = refs[:4]
        refs = refs[4:]
    else:
        x_ref = refs.pop(0)
    pieces, refs = refs[:n], refs[n:]
    qv_ref, tiles_ref, mask_ref = refs[:3]
    refs = refs[3:]
    if later:
        h_ref, x_ref = refs[:2]
        refs = refs[2:]
    part_ref, q_ref, k_ref, v_ref, o_ref, lse_ref, w_ref, mixed_ref = refs
    rows = 2 * SEQ
    if later:
        gain, shift, bias = prm_ref[3:4], prm_ref[4:5], prm_ref[5:6]

        def norm(i, carry):
            at = pl.ds(pl.multiple_of(i * 128, 128), 128)
            value = h1_ref[at] + own_ref[at].astype(f32) + other_ref[at].astype(f32) + bias
            unit, scale = centered(value)
            result = unit * gain + shift
            h_ref[at] = result
            x_ref[at] = result.astype(bf16)
            return carry

        lax.fori_loop(0, rows // 128, norm, 0)
    weight.start(pieces, w_ref, None)
    heads = k_ref.shape[0]
    per = heads // 2
    part = per * HEAD
    for x in range(2):
        for stream in range(2):
            block = x_ref[stream * SEQ : (stream + 1) * SEQ]
            width = w_ref.shape[2] if stream == 0 else 256
            result = nn(block, w_ref[x, :, :width])
            query = (result[:, :part] + qv_ref[x, 0:1, :part]).astype(bf16).astype(f32) * 0.125
            for j, one in enumerate(split_heads(query.astype(bf16), per)):
                q_ref[stream * heads + x * per + j] = one
            if stream == 0:
                key = result[:, part : 2 * part].astype(bf16)
                value = (result[:, 2 * part : 3 * part] + qv_ref[x, 1:2, :part]).astype(bf16)
                for j, one in enumerate(split_heads(key, per)):
                    k_ref[x * per + j] = one
                for j, one in enumerate(split_heads(value, per)):
                    v_ref[x * per + j] = one

    def one_head(head, carry):
        key, value = k_ref[head], v_ref[head]
        for half in range(2):
            at = slice(half * 256, half * 256 + 256)
            bias = bias_block(tiles_ref, head, half)
            for stream in range(2):
                query = q_ref[stream * heads + head, at]
                score = nt(key, query) + (bias + mask_ref[stream, :, at])
                top = jnp.max(score, axis=0, keepdims=True)
                raised = jnp.exp(score - top)
                total = jnp.sum(raised, axis=0, keepdims=True)
                mixed = tn(value, raised.astype(bf16)) * (1.0 / total)
                mixed_ref[stream * heads + head, at] = mixed.T.astype(bf16)
                lse_ref[stream * heads + head, :, at] = top + jnp.log(total)
        return carry

    lax.fori_loop(0, heads, one_head, 0)
    for stream in range(2):
        total = None
        for x in range(2):
            blocks = [jnp.zeros((SEQ, HEAD), bf16)]
            blocks += [mixed_ref[stream * heads + x * per + j] for j in range(per)]
            block = jnp.concatenate(blocks, axis=1)
            o_ref[x, stream * SEQ : (stream + 1) * SEQ] = block
            term = nt(block, w_ref[x, :, 512:768])
            total = term if total is None else total + term
        part_ref[stream * SEQ : (stream + 1) * SEQ] = total.astype(bf16)


def run_attn_forward(chain, entering, weight, qv, tiles, mask, after):
    later = len(entering) == 4
    heads = tiles.shape[0]
    width = entering[0].shape[1]
    rows = entering[0].shape[0]
    columns = weight.width
    inputs = [*entering, *weight.arrays, qv, tiles, mask]
    specs = [VMEM] * len(entering) + weight.specs(False) + [VMEM] * 3
    outs = [((rows, width), f32), ((rows, width), bf16)] if later else []
    outs += [
        ((rows, width), bf16),
        ((2 * heads, SEQ, HEAD), bf16),
        ((heads, SEQ, HEAD), bf16),
        ((heads, SEQ, HEAD), bf16),
        ((2, rows, 256), bf16),
        ((2 * heads, 1, SEQ), f32),
    ]
    return chain.call(
        lambda *refs: attn_forward(weight, later, refs),
        inputs,
        specs,
        outs,
        [VMEM] * len(outs),
        flops=14 * 10**9,
        vmem=36,
        scratch=[
            pltpu.VMEM((2, width, weight.width), bf16),
            pltpu.VMEM((2 * heads, SEQ, HEAD), bf16),
        ],
        after=after,
    )


def ffn_forward(up, down, refs):
    h_ref, own_ref, other_ref, prm_ref, bias_ref = refs[:5]
    refs = refs[5:]
    up_pieces, refs = refs[: len(up.arrays)], refs[len(up.arrays) :]
    down_pieces, refs = refs[: len(down.arrays)], refs[len(down.arrays) :]
    ah_ref, h1_ref, fed_ref, act_ref, slope_ref, part_ref = refs[:6]
    up_ref, down_ref, up_sems, down_sems = refs[6:]

    @pl.when(pl.program_id(0) == 0)
    def _():
        up.start(up_pieces, up_ref, up_sems)
        down.start(down_pieces, down_ref, down_sems)

    gain, shift, bias = prm_ref[0:1], prm_ref[1:2], prm_ref[2:3]
    before = h_ref[...].astype(f32) + own_ref[...].astype(f32) + other_ref[...].astype(f32) + bias
    ah_ref[...] = before
    unit, scale = centered(before)
    normed = unit * gain + shift
    h1_ref[...] = normed
    fed = normed.astype(bf16)
    fed_ref[...] = fed

    @pl.when(pl.program_id(0) == 0)
    def _():
        up.finish(up_pieces, up_ref, up_sems)
        down.finish(down_pieces, down_ref, down_sems)

    total = None
    for x in range(2):
        inner = nn(fed, up_ref[x]) + bias_ref[x]
        act, slope = gelu_pair(inner)
        act = act.astype(bf16)
        act_ref[x] = act
        slope_ref[x] = slope.astype(bf16)
        term = nt(act, down_ref[x])
        total = term if total is None else total + term
    part_ref[...] = total.astype(bf16)


def by_rows(rows, width):
    return pl.BlockSpec((rows, width), lambda i: (i, 0))


def by_rows_pair(rows, width):
    return pl.BlockSpec((2, rows, width), lambda i: (0, i, 0))


def fixed(*shape):
    return pl.BlockSpec(shape, lambda i: (0,) * len(shape))


def run_ffn_forward(chain, entering, params, bias, up, down):
    rows, width = entering[0].shape
    step = 256
    units = up.width
    inputs = [*entering, params, bias, *up.arrays, *down.arrays]
    specs = [by_rows(step, width)] * 3 + [fixed(8, width), fixed(2, 1, units)]
    specs += up.specs(True) + down.specs(True)
    outs = [
        ((rows, width), f32),
        ((rows, width), f32),
        ((rows, width), bf16),
        ((2, rows, units), bf16),
        ((2, rows, units), bf16),
        ((rows, width), bf16),
    ]
    out_specs = [by_rows(step, width)] * 3 + [by_rows_pair(step, units)] * 2
    out_specs += [by_rows(step, width)]
    return chain.call(
        lambda *refs: ffn_forward(up, down, refs),
        inputs,
        specs,
        outs,
        out_specs,
        flops=8 * rows * width * units,
        vmem=30,
        grid=(rows // step,),
        scratch=[
            pltpu.VMEM((2, width, units), bf16),
            pltpu.VMEM((2, width, units), bf16),
            pltpu.SemaphoreType.DMA((16,)),
            pltpu.SemaphoreType.DMA((16,)),
        ],
    )


def ffn_backward(up, down, grads, last, refs):
    grad_refs, refs = refs[:grads], refs[grads:]
    h1_ref, own_ref, other_ref, prm_ref, slope_ref = refs[:5]
    refs = refs[5:]
    up_pieces, refs = refs[: len(up.arrays)], refs[len(up.arrays) :]
    down_pieces, refs = refs[: len(down.arrays)], refs[len(down.arrays) :]
    dz_ref, dbh_ref, du_ref, part_ref, sums_ref, up_sums_ref = refs[:6]
    refs = refs[6:]
    if last:
        out_ref, refs = refs[0], refs[1:]
    up_ref, down_ref, up_sems, down_sems = refs

    @pl.when(pl.program_id(0) == 0)
    def _():
        up.start(up_pieces, up_ref, up_sems)
        down.start(down_pieces, down_ref, down_sems)
        sums_ref[...] = jnp.zeros_like(sums_ref)
        up_sums_ref[...] = jnp.zeros_like(up_sums_ref)

    gain, shift, bias = prm_ref[3:4], prm_ref[4:5], prm_ref[5:6]
    grad = sum(ref[...].astype(f32) for ref in grad_refs)
    after = h1_ref[...] + own_ref[...].astype(f32) + other_ref[...].astype(f32) + bias
    if last:
        unit, scale = centered(after)
        out_ref[...] = (unit * gain + shift).astype(bf16)
    back, gain_sum, shift_sum = norm_back(after, gain, grad)
    dbh_ref[...] = back
    sums_ref[0:1] += gain_sum
    sums_ref[1:2] += shift_sum
    sums_ref[2:3] += jnp.sum(back, axis=0, keepdims=True)
    dz = back.astype(bf16)
    dz_ref[...] = dz

    @pl.when(pl.program_id(0) == 0)
    def _():
        up.finish(up_pieces, up_ref, up_sems)
        down.finish(down_pieces, down_ref, down_sems)

    total = None
    for x in range(2):
        du = (nn(dz, down_ref[x]) * slope_ref[x].astype(f32)).astype(bf16)
        du_ref[x] = du
        up_sums_ref[x] += jnp.sum(du.astype(f32), axis=0, keepdims=True)
        term = nt(du, up_ref[x])
        total = term if total is None else total + term
    part_ref[...] = total.astype(bf16)


def run_ffn_backward(chain, grads, entering, params, slope, up, down, last):
    rows, width = entering[0].shape
    step = 256
    units = up.width
    inputs = [*grads, *entering, params, slope, *up.arrays, *down.arrays]
    specs = [by_rows(step, width)] * (len(grads) + 3)
    specs += [fixed(8, width), by_rows_pair(step, units)]
    specs += up.specs(True) + down.specs(True)
    outs = [
        ((rows, width), bf16),
        ((rows, width), f32),
        ((2, rows, units), bf16),
        ((rows, width), bf16),
        ((8, width), f32),
        ((2, 1, units), f32),
    ]
    out_specs = [by_rows(step, width)] * 2 + [by_rows_pair(step, units), by_rows(step, width)]
    out_specs += [fixed(8, width), fixed(2, 1, units)]
    if last:
        outs.append(((rows, width), bf16))
        out_specs.append(by_rows(step, width))
    return chain.call(
        lambda *refs: ffn_backward(up, down, len(grads), last, refs),
        inputs,
        specs,
        outs,
        out_specs,
        flops=8 * rows * width * units,
        vmem=30,
        grid=(rows // step,),
        scratch=[
            pltpu.VMEM((2, width, units), bf16),
            pltpu.VMEM((2, width, units), bf16),
            pltpu.SemaphoreType.DMA((16,)),
            pltpu.SemaphoreType.DMA((16,)),
        ],
    )


def fold(near):
    within = lax.broadcasted_iota(jnp.int32, (8, TILE), 0)
    lane = lax.broadcasted_iota(jnp.int32, (8, TILE), 1)
    zero = jnp.zeros((8, TILE), f32)

    def aligned(rows, at):
        rows = pltpu.roll(rows, (TILE - at) % TILE, 1)
        for bit in (1, 2, 4):
            rows = jnp.where((within & bit) != 0, pltpu.roll(rows, TILE - bit, 1), rows)
        return rows

    same = after = far_before = far_after = zero
    for at in range(0, TILE, 8):
        upper = within + lane < TILE - at
        one, two, three = (aligned(near[i][at : at + 8], at) for i in (1, 2, 3))
        same += jnp.where(upper, two, one)
        after += jnp.where(upper, three, two)
        far_before += near[0][at : at + 8] + jnp.where(upper, one, zero)
        far_after += near[4][at : at + 8] + jnp.where(upper, zero, three)
    sums = [jnp.sum(v, axis=0, keepdims=True) for v in (same, after, far_before, far_after)]
    return jnp.concatenate([*sums, jnp.zeros((4, TILE), f32)])


def attn_backward(weight, refs):
    n = len(weight.arrays)
    dbh_ref, own_ref, other_ref, ah_ref, prm_ref = refs[:5]
    pieces, refs = refs[5 : 5 + n], refs[5 + n :]
    q_ref, k_ref, v_ref, lse_ref, tiles_ref, mask_ref = refs[:6]
    refs = refs[6:]
    dah_ref, dy_ref, dcat_ref, dqg_ref, part_ref, near_ref, sums_ref, col_ref = refs[:8]
    w_ref, do_ref, dq_ref, dk_ref, dv_ref = refs[8:]
    rows = 2 * SEQ
    gain = prm_ref[0:1]
    sums_ref[...] = jnp.zeros_like(sums_ref)

    def norm(i, carry):
        at = pl.ds(pl.multiple_of(i * 128, 128), 128)
        grad = dbh_ref[at] + own_ref[at].astype(f32) + other_ref[at].astype(f32)
        back, gain_sum, shift_sum = norm_back(ah_ref[at], gain, grad)
        dah_ref[at] = back
        dy_ref[at] = back.astype(bf16)
        sums_ref[0:1] += gain_sum
        sums_ref[1:2] += shift_sum
        sums_ref[2:3] += jnp.sum(back, axis=0, keepdims=True)
        return carry

    lax.fori_loop(0, rows // 128, norm, 0)
    weight.start(pieces, w_ref, None)
    heads = k_ref.shape[0]
    per = heads // 2
    for stream in range(2):
        at = slice(stream * SEQ, (stream + 1) * SEQ)
        for x in range(2):
            block = nn(dy_ref[at], w_ref[x, :, 512:768]).astype(bf16)
            for j in range(per):
                do_ref[stream * heads + x * per + j] = block[:, HEAD * (1 + j) : HEAD * (2 + j)]

    def one_head(head, carry):
        key, value = k_ref[head], v_ref[head]
        grad_key = jnp.zeros((SEQ, HEAD), f32)
        grad_value = jnp.zeros((SEQ, HEAD), f32)
        near = [jnp.zeros((TILE, TILE), f32) for _ in range(NEAR)]
        for half in range(2):
            at = slice(half * 256, half * 256 + 256)
            bias = bias_block(tiles_ref, head, half)
            for stream in range(2):
                spot = stream * heads + head
                query, grad_out = q_ref[spot, at], do_ref[spot, at]
                score = nt(key, query) + (bias + mask_ref[stream, :, at])
                prob = jnp.exp(score - lse_ref[spot, :, at])
                both = prob * nt(value, grad_out)
                inner = jnp.sum(both, axis=0, keepdims=True)
                grad_score = (both - prob * inner).astype(bf16)
                grad_value += nn(prob.astype(bf16), grad_out)
                grad_key += nn(grad_score, query)
                dq_ref[spot, at] = (tn(key, grad_score) * 0.125).T.astype(bf16)
                wide = grad_score.astype(f32)
                for k in range(SEQ // TILE):
                    for q in range(2):
                        which = min(max(k - (2 * half + q), -2), 2) + 2
                        near[which] += wide[
                            k * TILE : (k + 1) * TILE, q * TILE : (q + 1) * TILE
                        ]
        near_ref[head] = fold(near)
        dk_ref[head] = grad_key.astype(bf16)
        dv_ref[head] = grad_value.astype(bf16)
        return carry

    lax.fori_loop(0, heads, one_head, 0)
    total_h = total_g = None
    for x in range(2):
        near = range(x * per, (x + 1) * per)
        blocks = [dq_ref[j] for j in near] + [dk_ref[j] for j in near] + [dv_ref[j] for j in near]
        blocks += [jnp.zeros((SEQ, HEAD), bf16)] * per
        block = jnp.concatenate(blocks, axis=1)
        dcat_ref[x] = block
        term = nt(block, w_ref[x])
        total_h = term if total_h is None else total_h + term
        col_ref[x, 0:1] = jnp.sum(block.astype(f32), axis=0, keepdims=True)
        blocks = [dq_ref[heads + j] for j in near] + [jnp.zeros((SEQ, HEAD), bf16)]
        block = jnp.concatenate(blocks, axis=1)
        dqg_ref[x] = block
        term = nt(block, w_ref[x, :, :256])
        total_g = term if total_g is None else total_g + term
        col_ref[x, 1:2, :256] = jnp.sum(block.astype(f32), axis=0, keepdims=True)
    part_ref[:SEQ] = total_h.astype(bf16)
    part_ref[SEQ:] = total_g.astype(bf16)


def run_attn_backward(chain, entering, params, weight, saved, tiles, mask):
    rows, width = entering[0].shape
    heads = tiles.shape[0]
    columns = weight.width
    q, k, v, _, lse = saved
    inputs = [*entering, params, *weight.arrays, q, k, v, lse, tiles, mask]
    specs = [VMEM] * 5 + weight.specs(False) + [VMEM] * 6
    outs = [
        ((rows, width), f32),
        ((rows, width), bf16),
        ((2, SEQ, columns), bf16),
        ((2, SEQ, 256), bf16),
        ((rows, width), bf16),
        ((heads, 8, TILE), f32),
        ((8, width), f32),
        ((2, 8, columns), f32),
    ]
    return chain.call(
        lambda *refs: attn_backward(weight, refs),
        inputs,
        specs,
        outs,
        [VMEM] * len(outs),
        flops=20 * 10**9,
        vmem=40,
        scratch=[
            pltpu.VMEM((2, width, weight.width), bf16),
            pltpu.VMEM((2 * heads, SEQ, HEAD), bf16),
            pltpu.VMEM((2 * heads, SEQ, HEAD), bf16),
            pltpu.VMEM((heads, SEQ, HEAD), bf16),
            pltpu.VMEM((heads, SEQ, HEAD), bf16),
        ],
    )


def quarters(part, first):
    return [(part, x) for x in range(2)] if first == "y" else [(y, part) for y in range(2)]


def ffn_grads(chain, fed, du, dz, act, part, up_first, down_first):
    rows, width = fed.shape
    units = du.shape[2]
    half = width // 2

    def body(fed_ref, du_ref, dz_ref, act_ref, up_ref, down_ref):
        for left, right, out, first in (
            (fed_ref, du_ref, up_ref, up_first),
            (dz_ref, act_ref, down_ref, down_first),
        ):
            for n, (y, x) in enumerate(quarters(part, first)):
                out[n] = tn(left[:, y * half : (y + 1) * half], right[x]).astype(bf16)

    return chain.call(
        body,
        [fed, du, dz, act],
        [VMEM] * 4,
        [((2, half, units), bf16)] * 2,
        [VMEM] * 2,
        flops=8 * rows * half * units,
        vmem=20,
    )


def attn_grads(chain, x, dcat, dqg, dy, o, part, firsts):
    rows, width = x.shape
    half = width // 2
    columns = dcat.shape[2]
    span = columns // len(firsts)

    def body(x_ref, dcat_ref, dqg_ref, dy_ref, o_ref, *outs):
        for y in range(2):
            at = slice(y * half, (y + 1) * half)
            for n, first in enumerate(firsts):
                for place, (want, other) in enumerate(quarters(part, first)):
                    if want != y:
                        continue
                    low, high = n * span, (n + 1) * span
                    total = tn(x_ref[:SEQ, at], dcat_ref[other, :, low:high])
                    outs[n][place] = total.astype(bf16)
                    if n == 0:
                        query = total[:, :256] + tn(x_ref[SEQ:, at], dqg_ref[other])
                        outs[n][place, :, :256] = query.astype(bf16)
                    if n == len(firsts) - 1:
                        out = total[:, span - 256 :] + tn(dy_ref[:, at], o_ref[other])
                        outs[n][place, :, span - 256 :] = out.astype(bf16)

    return chain.call(
        body,
        [x, dcat, dqg, dy, o],
        [VMEM] * 5,
        [((2, half, span), bf16)] * len(firsts),
        [VMEM] * len(firsts),
        flops=6 * rows * half * columns,
        vmem=20,
    )


def exact(rows, right, product):
    total = None
    for _ in range(3):
        top = rows.astype(bf16)
        rows = rows - top.astype(f32)
        term = product(top, right)
        total = term if total is None else total + term
    return total


SMALL = 8


def finish_rows(chain, core, swapper, fold_hot, groups, smalls):
    rows, width = groups[0][0].shape
    own = rows // 4
    flat = [v for group in groups for v in group]
    counts = [len(group) for group in groups]
    layers = len(smalls) // 5
    heads = smalls[0].shape[0]
    per = heads // 2

    def body(core_ref, swapper_ref, hot_ref, *refs):
        ins, small_ins = refs[: len(flat)], refs[len(flat) : len(flat) + len(smalls)]
        outs = refs[len(flat) + len(smalls) :]
        at = pl.multiple_of(core_ref[0] * own, own)
        first = 0
        for count, out in zip(counts, outs):
            for stream in range(2):
                total = sum(
                    ref[pl.ds(at + stream * SEQ, own)].astype(f32)
                    for ref in ins[first : first + count]
                )
                out[stream] = nt(total.astype(bf16), swapper_ref[...]).astype(bf16)
            first += count
        sides = outs[len(counts) :]
        edge = layers * SMALL
        for layer in range(layers):
            near, cols, one, two, up = small_ins[5 * layer : 5 * layer + 5]
            for x, side in enumerate(sides):
                base = layer * SMALL
                side[base : base + SMALL] = jnp.zeros((SMALL, width), f32)
                side[base : base + 1] = cols[x, 0:1]
                side[base : base + 1, :256] = cols[x, 0:1, :256] + cols[x, 1:2, :256]
                side[base + 1 : base + 2] = up[x]
                for j in range(per):
                    table = None
                    for n in range(4):
                        hot = hot_ref[n * TILE : (n + 1) * TILE]
                        term = exact(near[x * per + j], hot, nn)[n : n + 1]
                        table = term if table is None else table + term
                    side[base + 2 + j : base + 3 + j, :TILE] = table
            sums = jnp.concatenate([one[...], two[...]])
            back = exact(sums, swapper_ref[...], nt)
            for side in sides:
                base = edge + layer * SMALL
                for n in range(3):
                    side[base + 2 * n : base + 2 * n + 1] = back[n : n + 1]
                    side[base + 2 * n + 1 : base + 2 * n + 2] = back[SMALL + n : SMALL + n + 1]
                side[base + 6 : base + 8] = jnp.zeros((2, width), f32)

    shape = ((2 * layers * SMALL, width), f32)
    made = chain.call(
        body,
        [core, swapper, fold_hot, *flat, *smalls],
        [pl.BlockSpec(memory_space=pltpu.SMEM)] + [VMEM] * (2 + len(flat) + len(smalls)),
        [((2, own, width), bf16)] * len(groups) + [shape] * 2,
        [VMEM] * (len(groups) + 2),
        flops=4 * own * width * width * len(groups),
        vmem=24,
    )
    return made[: len(groups)], made[len(groups)], made[len(groups) + 1]


def small_grads(value, part, per):
    layers = value.shape[0] // (2 * SMALL)
    base = [layer * SMALL for layer in range(layers)]
    far = [layers * SMALL + b for b in base]
    return [
        [value[b : b + 1, :part] for b in base],
        [value[b : b + 1, 2 * part : 3 * part] for b in base],
        [value[b + 1 : b + 2] for b in base],
        [value[b + 2 : b + 2 + per, :BUCKETS] for b in base],
        *[[value[b + 2 * n : b + 2 * n + 2] for b in far] for n in range(3)],
    ]


def add_pair(chain, a, b):
    def body(one, two, out):
        out[...] = one[...] + two[...]

    return chain.call(body, [a, b], [VMEM] * 2, [(a.shape, f32)], [VMEM], flops=10**5, vmem=4)[0]


def all_grads(chain, part, per, attn_sums, attn_old, ffn_sums, ffn_old, small):
    groups = [*attn_sums, *ffn_sums]
    depth, units = ffn_old[0].shape
    width = small[0].shape[1]
    layers = 2

    def body(*refs):
        ins, outs = refs[: len(groups) + 6], refs[len(groups) + 6 :]
        attn_refs, rest = ins[: len(attn_sums)], ins[len(attn_sums) :]
        ffn_refs, (low, high, up, down, *more) = rest[: len(ffn_sums)], rest[len(ffn_sums) :]

        def total(of, n):
            return sum(ref[n].astype(f32) for ref in of)

        for layer in range(layers):
            if layer == 0:
                attn = [total(attn_refs, n) for n in range(2)]
                ffn = [total(ffn_refs, n) for n in range(2)]
            else:
                attn, ffn = [low[...], high[...]], [up[...], down[...]]
            outs[0][layer] = attn[0][:, :part]
            outs[1][layer] = attn[0][:, part:]
            outs[2][layer] = attn[1][:, :part]
            outs[3][layer] = attn[1][:, part:].T
            outs[4][layer] = ffn[0]
            outs[5][layer] = ffn[1].T
        one, two = more
        made = small_grads(one[...] + two[...], part, per)
        for n, values in enumerate(made):
            for layer in range(layers):
                if n < 3:
                    outs[6 + n][layer : layer + 1] = values[layer]
                else:
                    outs[6 + n][layer] = values[layer]

    shapes = [(layers, depth, part)] * 3 + [(layers, part, depth), (layers, depth, units)]
    shapes += [(layers, units, depth), (layers, part), (layers, part), (layers, units)]
    shapes += [(layers, per, BUCKETS)] + [(layers, 2, width)] * 3
    return chain.call(
        body,
        [*groups, *attn_old, *ffn_old, *small],
        [VMEM] * (len(groups) + 6),
        [(shape, f32) for shape in shapes],
        [VMEM] * len(shapes),
        flops=10**6,
        vmem=16,
    )


def local(links, *arguments):
    (
        h_in,
        g_in,
        lengths,
        order,
        predicted,
        w_query,
        w_key,
        w_value,
        w_out,
        w_up,
        w_down,
        q_bias,
        v_bias,
        up_bias,
        rel_table,
        norm_gain,
        norm_shift,
        out_bias,
        h_cot,
        g_cot,
    ) = arguments
    rows_own, model = h_in.shape
    part = w_query.shape[2]
    units = w_up.shape[2]
    heads = 2 * rel_table.shape[1]
    table_size = rel_table.shape[1] * BUCKETS
    slot = lax.axis_index("x")
    core = lax.axis_index("core")

    chain = Chain()
    gathered = []
    for layer in range(LAYERS):
        attn = jnp.concatenate(
            [w_query[layer], w_key[layer], w_value[layer], w_out[layer].T], axis=1
        )
        blocks = (attn, w_up[layer], w_down[layer].T)
        if layer < LAYERS - 1:
            gathered.append([links.gather(b, r) for b, r in zip(blocks, GATHER)])
            continue
        gathered.append([links.gather(attn, "zyx"), *links.gather_far(blocks[1:])])

    def pick(v):
        return lax.dynamic_index_in_dim(v, slot, 0, keepdims=False)

    mask = slot_masks(pick(lengths), pick(order), pick(predicted))
    onehot = (
        jnp.arange(BUCKETS, dtype=jnp.int32)[:, None] == tile_buckets().reshape(1, -1)
    ).astype(f32)

    lanes = jnp.arange(TILE, dtype=jnp.int32)
    edge = jnp.full_like(lanes, TILE)
    fold_buckets = bucket_of(jnp.concatenate([-lanes, TILE - lanes, -edge, edge]))
    fold_hot = (fold_buckets[:, None] == lanes[None, :]).astype(bf16)

    small = links.pair(
        jnp.concatenate(
            [q_bias, v_bias, up_bias, rel_table.reshape(LAYERS, table_size)], axis=1
        )
    )
    tables = small[:, :, 2 * part + units :].transpose(1, 0, 2).reshape(LAYERS * heads, BUCKETS)
    tiles = jnp.dot(tables, onehot, precision=highest).reshape(LAYERS, heads, NEAR, TILE, TILE)
    qv = jnp.stack([small[:, :, :part], small[:, :, part : 2 * part]], axis=2)
    qv = jnp.pad(qv, ((0, 0), (0, 0), (0, 6), (0, 256 - part)))
    bias_up = small[:, :, None, 2 * part : 2 * part + units]

    features = links.feature_order(model)
    swapper = (jnp.arange(model, dtype=jnp.int32)[:, None] == features[None, :]).astype(bf16)
    swapper32 = swapper.astype(f32)
    params = jnp.dot(
        jnp.stack([norm_gain, norm_shift, out_bias], axis=2).reshape(-1, model),
        swapper32,
        precision=highest,
    ).reshape(LAYERS, 6, model)
    params = jnp.pad(params, ((0, 0), (0, 2), (0, 0)))

    def ordered(first, second):
        rows = links.both_rows(jnp.concatenate([first, second], axis=1))
        both = jnp.concatenate([rows[:, :model], rows[:, model:]], axis=0)
        return nn(both, swapper).astype(bf16)

    entering = ordered(h_in, g_in)
    kept = []
    for layer in range(LAYERS):
        attn, up, down = gathered[layer]
        if layer == 0:
            x = stream = entering
            before = (entering,)
            after = []
            if links.routed:
                after = [v for w in (up, down, gathered[1][0]) for v in w.arrays]
        else:
            before = (h1, part_own, part_other, params[layer - 1])
            after = []
        made = run_attn_forward(chain, before, attn, qv[:, layer], tiles[layer], mask, after)
        if layer > 0:
            stream, x = made[:2]
            made = made[2:]
        mixed_own, q, k, v, o, lse = made
        ah, h1, fed, act, slope, part_own = run_ffn_forward(
            chain, (stream, mixed_own, links.pc(mixed_own)), params[layer], bias_up[:, layer], up, down
        )
        part_other = links.pc(part_own)
        kept.append((x, (q, k, v, o, lse), ah, (h1, part_own, part_other), fed, act, slope))
    grads = (ordered(h_cot, g_cot),)
    smalls = []
    for layer in range(LAYERS - 1, -1, -1):
        attn, up, down = gathered[layer]
        firsts = [r[0] for r in SCATTER]
        x, saved, ah, second, fed, act, slope = kept[layer]
        last = layer == LAYERS - 1
        made = run_ffn_backward(chain, grads, second, params[layer], slope, up, down, last)
        dz, dbh, du, part_own, sums_two, up_sums = made[:6]
        if last:
            result = made[6]
        part_other = links.pc(part_own)
        if not last:
            ffn_way.third()
            attn_way.second()
        sent = ffn_grads(chain, fed, du, dz, act, 1, *firsts)
        held = ffn_grads(chain, fed, du, dz, act, 0, *firsts)
        if not last:
            ffn_way.fourth()
            attn_way.third()
            old_ffn, old_attn = ffn_way, attn_way
        ffn_way = Scatter(chain, links, list(zip(held, sent, SCATTER)))
        dah, dy, dcat, dqg, part_own, near, sums_one, cols = run_attn_backward(
            chain, (dbh, part_own, part_other, ah), params[layer], attn, saved, tiles[layer], mask
        )
        part_other = links.pc(part_own)
        if not last:
            done_ffn = old_ffn.finish()
            old_attn.fourth()
        ffn_way.second()
        sent = attn_grads(chain, x, dcat, dqg, dy, saved[3], 1, firsts)
        held = attn_grads(chain, x, dcat, dqg, dy, saved[3], 0, firsts)
        attn_way = Scatter(chain, links, list(zip(held, sent, SCATTER)))
        smalls += [near, cols, sums_one, sums_two, up_sums]
        grads = (dah, part_own, part_other)
    smalls = smalls[5:] + smalls[:5]
    final, kept_small, sent_small = finish_rows(
        chain, jnp.full((1,), core, jnp.int32), swapper, fold_hot, [(result,), grads], smalls
    )
    per = heads // 2
    if links.routed:
        other = links.swap(sent_small, "x")
        ffn_way.third()
        attn_way.second()
        value = add_pair(chain, kept_small, other)
        other = links.swap(value, "y")
        ffn_way.fourth()
        attn_way.third()
        value = add_pair(chain, value, other)
        other = links.across(value, 1)
        done_attn = old_attn.finish()
        attn_way.fourth()
        value = add_pair(chain, value, other)
        small = (value, links.across(value, 2))
        owned = all_grads(chain, part, per, attn_way.sums, done_attn, ffn_way.sums, done_ffn, small)
    else:
        done_attn = old_attn.finish()
        attn_sum = jnp.stack([jnp.concatenate(v, axis=1) for v in (attn_way.sums, done_attn)])
        up_sum, down_sum = (jnp.stack([ffn_way.sums[n], done_ffn[n]]) for n in range(2))
        owned = [attn_sum[:, :, n * part : (n + 1) * part] for n in range(4)] + [up_sum, down_sum]
        owned[3] = owned[3].transpose(0, 2, 1)
        owned[5] = owned[5].transpose(0, 2, 1)
        edge = LAYERS * SMALL
        split = lax.psum_scatter(jnp.stack([kept_small[:edge], sent_small[:edge]]), "x")
        value = jnp.concatenate(
            [lax.psum(split, ("z", "y")), lax.psum(kept_small[edge:], ("z", "y", "x"))]
        )
        for n, values in enumerate(small_grads(value, part, per)):
            owned.append(jnp.concatenate(values) if n < 3 else jnp.stack(values))
    return (
        final[0][0],
        final[0][1],
        final[1][0],
        final[1][1],
        *owned,
    )


def solution(mesh):
    links = Links(mesh)
    rows = P(("z", "y", "x", "core"), None)
    by_dp = P(("z", "y"), None)
    wide = P(None, ("z", "y"), ("x", "core"))
    tall = P(None, ("x", "core"), ("z", "y"))
    by_tensor = P(None, ("x", "core"))
    table = P(None, ("x", "core"), None)
    weights = (wide, wide, wide, tall, wide, tall)
    owned = (by_tensor, by_tensor, by_tensor, table, P(), P(), P())
    return jax.shard_map(
        functools.partial(local, links),
        mesh=links.mesh,
        in_specs=(rows, rows, by_dp, by_dp, by_dp) + weights + owned + (rows, rows),
        out_specs=(rows, rows, rows, rows) + weights + owned,
        check_vma=False,
    )
```

```python
import functools

import jax
import jax.numpy as jnp
from jax import lax
from jax.experimental import pallas as pl
from jax.experimental.pallas import tpu as pltpu
from jax.sharding import Mesh, PartitionSpec as P

HEAD = 64
BUCKETS = 32
LAYERS = 2
SEQ = 512
TILE = 128
NEAR = 5

epsilon = 1e-05
limits = (12, 16, 23, 32, 46, 64, 91)
highest = lax.Precision.HIGHEST
f32 = jnp.float32
bf16 = jnp.bfloat16
SWAP = [(0, 1), (1, 0)]
GATHER = ("zxy", "xzy", "yzx")
SCATTER = ("xyz", "yxz")
ANY = pl.BlockSpec(memory_space=pl.ANY)
VMEM = pl.BlockSpec(memory_space=pltpu.VMEM)


def dot(left, right, numbers):
    return lax.dot_general(left, right, (numbers, ((), ())), preferred_element_type=f32)


def nn(left, right):
    return dot(left, right, ((1,), (0,)))


def nt(left, right):
    return dot(left, right, ((1,), (1,)))


def tn(left, right):
    return dot(left, right, ((0,), (0,)))


def bucket_of(offset):
    distance = jnp.abs(offset)
    farther = 8 + sum(((distance >= border).astype(jnp.int32) for border in limits))
    return jnp.where(distance < 8, distance, farther) + 16 * (offset > 0).astype(jnp.int32)


def slot_masks(piece_lengths, ranks, chosen):
    places = jnp.arange(SEQ, dtype=jnp.int32)
    first = piece_lengths[0]
    second = first + piece_lengths[1]
    third = second + piece_lengths[2]
    segment = (
        (places >= first).astype(jnp.int32)
        + (places >= second).astype(jnp.int32)
        + (places >= third).astype(jnp.int32)
    )
    leading = jnp.where(
        segment == 0,
        0,
        jnp.where(segment == 1, first, jnp.where(segment == 2, second, third)),
    )
    same_doc = segment[:, None] == segment[None, :]
    visible = chosen[:, None] == 0
    content = same_doc & (visible | (ranks[:, None] <= ranks[None, :]))
    query = same_doc & (
        (places[:, None] == leading[None, :])
        | visible & (places[:, None] != places[None, :])
        | (ranks[:, None] < ranks[None, :])
    )
    return jnp.where(jnp.stack([content, query]), 0.0, -1e30).astype(f32)


def tile_buckets():
    near = jnp.arange(NEAR, dtype=jnp.int32)[:, None, None] - NEAR // 2
    key = jnp.arange(TILE, dtype=jnp.int32)[None, :, None]
    query = jnp.arange(TILE, dtype=jnp.int32)[None, None, :]
    return bucket_of(near * TILE + key - query)


class Links:
    def __init__(self, mesh):
        dp = mesh.shape["dp"]
        self.routed = dp == 8
        self.ny = 2
        self.nz = dp // 2
        self.nx = mesh.shape["tensor"] // 2
        self.mesh = Mesh(
            mesh.devices.reshape(self.nz, self.ny, self.nx, 2), ("z", "y", "x", "core")
        )
        self.ring = [(i, (i + 1) % self.nz) for i in range(self.nz)]

    def swap(self, v, axis):
        return lax.ppermute(v, axis, SWAP)

    def pz(self, v):
        return lax.ppermute(v, "z", self.ring)

    def across(self, v, step):
        return lax.ppermute(v, "z", [(i, i ^ step) for i in range(self.nz)])

    def turn(self):
        z = lax.axis_index("z")
        far = [jnp.bitwise_xor(z, k) for k in (1, 3)]
        return jnp.stack([lax.rem(z - f + self.nz, self.nz) for f in far]).astype(jnp.int32)

    def pc(self, v):
        return lax.ppermute(v, "core", SWAP)

    def feature_order(self, width):
        count = self.nz * self.ny
        depth = width // count
        place = jnp.arange(width, dtype=jnp.int32)
        if not self.routed:
            return place
        block, rest = place // depth, place % depth
        ky, kz = block // self.nz, block % self.nz
        z = lax.rem(lax.axis_index("z") - kz + self.nz, self.nz)
        y = jnp.bitwise_xor(lax.axis_index("y"), ky)
        return (z * self.ny + y) * depth + rest

    def gather(self, block, route):
        if not self.routed:
            rows = lax.all_gather(block, ("z", "y"), axis=0, tiled=True)
            return Weight([lax.all_gather(rows, "x", axis=0)], (((0, 0), (1, 0)),))
        depth = block.shape[0]
        a, b = route.replace("z", "")
        held = [block if route[0] == "z" else jnp.stack([block, self.swap(block, a)])]
        for _ in range(self.nz - 1):
            held.append(self.pz(held[-1]))
        if route[0] == "z":
            held = [jnp.stack([h, self.swap(h, a)]) for h in held]
        pieces = held + [self.swap(h, b) for h in held]
        spots = []
        for other in range(2):
            for k in range(self.nz):
                pair = []
                for j in range(2):
                    x, y = (j, other) if a == "x" else (other, j)
                    pair.append((x, (y * self.nz + k) * depth))
                spots.append(tuple(pair))
        return Weight(pieces, tuple(spots))

    def gather_far(self, blocks):
        if not self.routed:
            return [self.gather(block, "") for block in blocks]
        depth, width = blocks[0].shape
        whole = lax.all_gather(jnp.concatenate(blocks, axis=1), ("z", "y", "x"), axis=0)
        places, spots = [], []
        z, y, x = (lax.axis_index(name) for name in ("z", "y", "x"))
        for other in range(self.nx):
            for ky in range(self.ny):
                for kz in range(self.nz):
                    far = lax.rem(z - kz + self.nz, self.nz) * self.ny + jnp.bitwise_xor(y, ky)
                    places.append(far * self.nx + jnp.bitwise_xor(x, other))
                    spots.append((other, (ky * self.nz + kz) * depth))
        places = jnp.stack(places).astype(jnp.int32)
        return [FarWeight(whole, places, spots, n, width) for n in range(len(blocks))]

    def scatter(self, keep, send, route):
        whole = jnp.concatenate([keep, send], axis=1)
        if route[0] == "x":
            whole = jnp.stack([keep.reshape(-1, keep.shape[2]), send.reshape(-1, send.shape[2])])
        mine = lax.psum_scatter(whole, "x", scatter_dimension=0, tiled=False)
        return lax.psum_scatter(mine, ("z", "y"), scatter_dimension=0, tiled=True).astype(f32)

    def pair(self, v):
        if not self.routed:
            return lax.all_gather(v, "x", axis=0)
        return jnp.stack([v, self.swap(v, "x")])

    def both_rows(self, v):
        other = self.pc(v)
        first = lax.axis_index("core") == 0
        return jnp.concatenate([jnp.where(first, v, other), jnp.where(first, other, v)])


class Chain:
    last = ()

    def call(self, body, inputs, in_specs, outs, out_specs, flops, vmem, grid=(), scratch=(), after=()):
        waits = [*self.last, *after]
        count = len(inputs)

        def rest(*refs):
            body(*refs[:count], *refs[count + len(waits) :])

        made = pl.pallas_call(
            rest,
            out_shape=[jax.ShapeDtypeStruct(*o) for o in outs],
            grid=grid,
            in_specs=[*in_specs, *[ANY] * len(waits)],
            out_specs=out_specs,
            scratch_shapes=list(scratch),
            compiler_params=pltpu.CompilerParams(vmem_limit_bytes=vmem << 20),
            cost_estimate=pl.CostEstimate(
                flops=4 * flops, bytes_accessed=0, transcendentals=0
            ),
        )(*inputs, *waits)
        self.last = (min(made, key=lambda v: v.size),)
        return made


class Weight:
    def __init__(self, arrays, spots):
        self.arrays = arrays
        self.spots = spots
        self.width = arrays[0].shape[2]

    def specs(self, grid):
        return [fixed(*v.shape) if grid else VMEM for v in self.arrays]

    def start(self, refs, target, sems):
        for piece, places in zip(refs, self.spots):
            rows = piece.shape[1]
            for j, (x, row) in enumerate(places):
                target[x, row : row + rows] = piece[j]

    def finish(self, refs, target, sems, x):
        pass


class FarWeight:
    def __init__(self, whole, places, spots, number, width):
        self.arrays = [whole, places]
        self.spots = spots
        self.number = number
        self.width = width

    def specs(self, grid):
        return [
            pl.BlockSpec(memory_space=pltpu.HBM),
            pl.BlockSpec(memory_space=pltpu.SMEM),
        ]

    def copies(self, refs, target, sems):
        whole, places = refs
        rows = whole.shape[1]
        columns = pl.ds(self.number * self.width, self.width)
        return [
            pltpu.make_async_copy(
                whole.at[places[n], :, columns], target.at[x, pl.ds(row, rows), :], sems.at[n]
            )
            for n, (x, row) in enumerate(self.spots)
        ]

    def start(self, refs, target, sems):
        for c in self.copies(refs, target, sems):
            c.start()

    def finish(self, refs, target, sems, x):
        @pl.when(pl.program_id(0) == 0)
        def _():
            for (half, _), c in zip(self.spots, self.copies(refs, target, sems)):
                if half == x:
                    c.wait()


def fold_sums(chain, arrays, wanted):
    inputs = [v for group in arrays for v in group]
    first = [sum(len(group) for group in arrays[:n]) for n in range(len(arrays))]
    outs = []
    for rows, dtype in wanted:
        which, index = rows[0]
        shape = jax.eval_shape(lambda v: v[index], arrays[which][0]).shape
        outs.append((shape if len(rows) == 1 else (len(rows), *shape), dtype))

    def body(*refs):
        for out, (rows, dtype) in zip(refs[len(inputs) :], wanted):
            for n, (which, index) in enumerate(rows):
                group = refs[first[which] : first[which] + len(arrays[which])]
                total = sum(ref[index].astype(f32) for ref in group).astype(dtype)
                if len(rows) == 1:
                    out[...] = total
                else:
                    out[n] = total

    return chain.call(
        body,
        inputs,
        [VMEM] * len(inputs),
        outs,
        [VMEM] * len(outs),
        flops=sum(v.size for v in inputs),
        vmem=12,
    )


class Scatter:
    def __init__(self, chain, links, parts):
        self.chain = chain
        self.links = links
        self.routes = [route for _, _, route in parts]
        self.depth = parts[0][0].shape[1] // links.nz
        if links.routed:
            self.sums = [[keep, links.swap(send, route[0])] for keep, send, route in parts]
        else:
            self.sums = [links.scatter(*part) for part in parts]

    def second(self):
        if not self.links.routed:
            return
        wanted = [([(n, (i,))], bf16 if i else f32) for n in range(len(self.routes)) for i in range(2)]
        made = fold_sums(self.chain, self.sums, wanted)
        self.sums = [
            [made[2 * n], self.links.swap(made[2 * n + 1], route[1])]
            for n, route in enumerate(self.routes)
        ]

    def third(self):
        links = self.links
        if not links.routed:
            return
        depth = self.depth
        count = len(self.sums)
        columns = self.sums[0][0].shape[1]

        def body(turn, *refs):
            ins, (keep, send) = refs[: 2 * count], refs[2 * count :]
            for n in range(count):
                held, got = ins[2 * n : 2 * n + 2]
                for i in range(2):
                    at = slice(2 * i * depth, (2 * i + 1) * depth)
                    keep[i, n] = held[at].astype(f32) + got[at].astype(f32)
                    at = pl.ds(pl.multiple_of(turn[i] * depth, 32), depth)
                    send[i, n] = (held[at].astype(f32) + got[at].astype(f32)).astype(bf16)

        shape = (2, count, depth, columns)
        keep, send = self.chain.call(
            body,
            [links.turn(), *self.sums[0], *self.sums[1]],
            [pl.BlockSpec(memory_space=pltpu.SMEM)] + [VMEM] * (2 * count),
            [(shape, f32), (shape, bf16)],
            [VMEM] * 2,
            flops=10**6,
            vmem=12,
        )
        self.sums = [keep, links.across(send, 1)]

    def fourth(self):
        if not self.links.routed:
            return
        wanted = [([(0, (i,))], bf16 if i else f32) for i in range(2)]
        keep, send = fold_sums(self.chain, [self.sums], wanted)
        self.sums = [keep, self.links.across(send, 2)]

    def finish(self):
        if not self.links.routed:
            return self.sums
        wanted = [([(0, (n,))], f32) for n in range(len(self.routes))]
        return fold_sums(self.chain, [self.sums], wanted)


def centered(rows):
    center = rows - jnp.mean(rows, axis=-1, keepdims=True)
    scale = lax.rsqrt(jnp.mean(center * center, axis=-1, keepdims=True) + epsilon)
    return center * scale, scale


def norm_back(rows, gain, grad):
    unit, scale = centered(rows)
    inner = grad * gain
    first = jnp.mean(inner, axis=-1, keepdims=True)
    second = jnp.mean(inner * unit, axis=-1, keepdims=True)
    back = scale * (inner - first - unit * second)
    return back, jnp.sum(grad * unit, axis=0, keepdims=True), jnp.sum(grad, axis=0, keepdims=True)


def gelu_pair(u):
    root = 0.7978845608028654
    square = u * u
    t = jnp.tanh(root * u * (1.0 + 0.044715 * square))
    half = 0.5 * (1.0 + t)
    slope = half + (0.5 * root) * u * (1.0 - t * t) * (1.0 + (3 * 0.044715) * square)
    return u * half, slope


def bias_block(tiles, head, half):
    rows = []
    for key in range(SEQ // TILE):
        row = []
        for query in range(2 * half, 2 * half + 2):
            row.append(tiles[head, min(max(key - query, -2), 2) + 2])
        rows.append(jnp.concatenate(row, axis=1))
    return jnp.concatenate(rows, axis=0)


def split_heads(block, count):
    return [block[:, HEAD * n : HEAD * (n + 1)] for n in range(count)]


def attn_forward(weight, later, refs):
    n = len(weight.arrays)
    refs = list(refs)
    if later:
        h1_ref, own_ref, other_ref, prm_ref = refs[:4]
        refs = refs[4:]
    else:
        x_ref = refs.pop(0)
    pieces, refs = refs[:n], refs[n:]
    qv_ref, tiles_ref, mask_ref = refs[:3]
    refs = refs[3:]
    if later:
        h_ref, x_ref = refs[:2]
        refs = refs[2:]
    part_ref, q_ref, k_ref, v_ref, o_ref, lse_ref, w_ref, mixed_ref = refs
    rows = 2 * SEQ
    if later:
        gain, shift, bias = prm_ref[3:4], prm_ref[4:5], prm_ref[5:6]

        def norm(i, carry):
            at = pl.ds(pl.multiple_of(i * 128, 128), 128)
            value = h1_ref[at] + own_ref[at].astype(f32) + other_ref[at].astype(f32) + bias
            unit, scale = centered(value)
            result = unit * gain + shift
            h_ref[at] = result
            x_ref[at] = result.astype(bf16)
            return carry

        lax.fori_loop(0, rows // 128, norm, 0)
    weight.start(pieces, w_ref, None)
    heads = k_ref.shape[0]
    per = heads // 2
    part = per * HEAD
    for x in range(2):
        for stream in range(2):
            block = x_ref[stream * SEQ : (stream + 1) * SEQ]
            width = w_ref.shape[2] if stream == 0 else 256
            result = nn(block, w_ref[x, :, :width])
            query = (result[:, :part] + qv_ref[x, 0:1, :part]).astype(bf16).astype(f32) * 0.125
            for j, one in enumerate(split_heads(query.astype(bf16), per)):
                q_ref[stream * heads + x * per + j] = one
            if stream == 0:
                key = result[:, part : 2 * part].astype(bf16)
                value = (result[:, 2 * part : 3 * part] + qv_ref[x, 1:2, :part]).astype(bf16)
                for j, one in enumerate(split_heads(key, per)):
                    k_ref[x * per + j] = one
                for j, one in enumerate(split_heads(value, per)):
                    v_ref[x * per + j] = one

    def one_head(head, carry):
        key, value = k_ref[head], v_ref[head]
        for half in range(2):
            at = slice(half * 256, half * 256 + 256)
            bias = bias_block(tiles_ref, head, half)
            for stream in range(2):
                query = q_ref[stream * heads + head, at]
                score = nt(key, query) + (bias + mask_ref[stream, :, at])
                top = jnp.max(score, axis=0, keepdims=True)
                raised = jnp.exp(score - top)
                total = jnp.sum(raised, axis=0, keepdims=True)
                mixed = tn(value, raised.astype(bf16)) * (1.0 / total)
                mixed_ref[stream * heads + head, at] = mixed.T.astype(bf16)
                lse_ref[stream * heads + head, :, at] = top + jnp.log(total)
        return carry

    lax.fori_loop(0, heads, one_head, 0)
    for stream in range(2):
        total = None
        for x in range(2):
            blocks = [jnp.zeros((SEQ, HEAD), bf16)]
            blocks += [mixed_ref[stream * heads + x * per + j] for j in range(per)]
            block = jnp.concatenate(blocks, axis=1)
            o_ref[x, stream * SEQ : (stream + 1) * SEQ] = block
            term = nt(block, w_ref[x, :, 512:768])
            total = term if total is None else total + term
        part_ref[stream * SEQ : (stream + 1) * SEQ] = total.astype(bf16)


def run_attn_forward(chain, entering, weight, qv, tiles, mask, after):
    later = len(entering) == 4
    heads = tiles.shape[0]
    width = entering[0].shape[1]
    rows = entering[0].shape[0]
    columns = weight.width
    inputs = [*entering, *weight.arrays, qv, tiles, mask]
    specs = [VMEM] * len(entering) + weight.specs(False) + [VMEM] * 3
    outs = [((rows, width), f32), ((rows, width), bf16)] if later else []
    outs += [
        ((rows, width), bf16),
        ((2 * heads, SEQ, HEAD), bf16),
        ((heads, SEQ, HEAD), bf16),
        ((heads, SEQ, HEAD), bf16),
        ((2, rows, 256), bf16),
        ((2 * heads, 1, SEQ), f32),
    ]
    return chain.call(
        lambda *refs: attn_forward(weight, later, refs),
        inputs,
        specs,
        outs,
        [VMEM] * len(outs),
        flops=14 * 10**9,
        vmem=36,
        scratch=[
            pltpu.VMEM((2, width, weight.width), bf16),
            pltpu.VMEM((2 * heads, SEQ, HEAD), bf16),
        ],
        after=after,
    )


def ffn_forward(up, down, refs):
    h_ref, own_ref, other_ref, prm_ref, bias_ref = refs[:5]
    refs = refs[5:]
    up_pieces, refs = refs[: len(up.arrays)], refs[len(up.arrays) :]
    down_pieces, refs = refs[: len(down.arrays)], refs[len(down.arrays) :]
    ah_ref, h1_ref, fed_ref, act_ref, slope_ref, part_ref = refs[:6]
    up_ref, down_ref, up_sems, down_sems = refs[6:]

    @pl.when(pl.program_id(0) == 0)
    def _():
        up.start(up_pieces, up_ref, up_sems)
        down.start(down_pieces, down_ref, down_sems)

    gain, shift, bias = prm_ref[0:1], prm_ref[1:2], prm_ref[2:3]
    before = h_ref[...].astype(f32) + own_ref[...].astype(f32) + other_ref[...].astype(f32) + bias
    ah_ref[...] = before
    unit, scale = centered(before)
    normed = unit * gain + shift
    h1_ref[...] = normed
    fed = normed.astype(bf16)
    fed_ref[...] = fed

    total = None
    for x in range(2):
        up.finish(up_pieces, up_ref, up_sems, x)
        inner = nn(fed, up_ref[x]) + bias_ref[x]
        act, slope = gelu_pair(inner)
        act = act.astype(bf16)
        act_ref[x] = act
        slope_ref[x] = slope.astype(bf16)
        down.finish(down_pieces, down_ref, down_sems, x)
        term = nt(act, down_ref[x])
        total = term if total is None else total + term
    part_ref[...] = total.astype(bf16)


def by_rows(rows, width):
    return pl.BlockSpec((rows, width), lambda i: (i, 0))


def by_rows_pair(rows, width):
    return pl.BlockSpec((2, rows, width), lambda i: (0, i, 0))


def fixed(*shape):
    return pl.BlockSpec(shape, lambda i: (0,) * len(shape))


def run_ffn_forward(chain, entering, params, bias, up, down):
    rows, width = entering[0].shape
    step = 256
    units = up.width
    inputs = [*entering, params, bias, *up.arrays, *down.arrays]
    specs = [by_rows(step, width)] * 3 + [fixed(8, width), fixed(2, 1, units)]
    specs += up.specs(True) + down.specs(True)
    outs = [
        ((rows, width), f32),
        ((rows, width), f32),
        ((rows, width), bf16),
        ((2, rows, units), bf16),
        ((2, rows, units), bf16),
        ((rows, width), bf16),
    ]
    out_specs = [by_rows(step, width)] * 3 + [by_rows_pair(step, units)] * 2
    out_specs += [by_rows(step, width)]
    return chain.call(
        lambda *refs: ffn_forward(up, down, refs),
        inputs,
        specs,
        outs,
        out_specs,
        flops=8 * rows * width * units,
        vmem=30,
        grid=(rows // step,),
        scratch=[
            pltpu.VMEM((2, width, units), bf16),
            pltpu.VMEM((2, width, units), bf16),
            pltpu.SemaphoreType.DMA((16,)),
            pltpu.SemaphoreType.DMA((16,)),
        ],
    )


def ffn_backward(up, down, grads, last, refs):
    grad_refs, refs = refs[:grads], refs[grads:]
    h1_ref, own_ref, other_ref, prm_ref, slope_ref = refs[:5]
    refs = refs[5:]
    up_pieces, refs = refs[: len(up.arrays)], refs[len(up.arrays) :]
    down_pieces, refs = refs[: len(down.arrays)], refs[len(down.arrays) :]
    dz_ref, dbh_ref, du_ref, part_ref, sums_ref, up_sums_ref = refs[:6]
    refs = refs[6:]
    if last:
        out_ref, refs = refs[0], refs[1:]
    up_ref, down_ref, up_sems, down_sems = refs

    @pl.when(pl.program_id(0) == 0)
    def _():
        down.start(down_pieces, down_ref, down_sems)
        up.start(up_pieces, up_ref, up_sems)
        sums_ref[...] = jnp.zeros_like(sums_ref)
        up_sums_ref[...] = jnp.zeros_like(up_sums_ref)

    gain, shift, bias = prm_ref[3:4], prm_ref[4:5], prm_ref[5:6]
    grad = sum(ref[...].astype(f32) for ref in grad_refs)
    after = h1_ref[...] + own_ref[...].astype(f32) + other_ref[...].astype(f32) + bias
    if last:
        unit, scale = centered(after)
        out_ref[...] = (unit * gain + shift).astype(bf16)
    back, gain_sum, shift_sum = norm_back(after, gain, grad)
    dbh_ref[...] = back
    sums_ref[0:1] += gain_sum
    sums_ref[1:2] += shift_sum
    sums_ref[2:3] += jnp.sum(back, axis=0, keepdims=True)
    dz = back.astype(bf16)
    dz_ref[...] = dz

    total = None
    for x in range(2):
        down.finish(down_pieces, down_ref, down_sems, x)
        du = (nn(dz, down_ref[x]) * slope_ref[x].astype(f32)).astype(bf16)
        du_ref[x] = du
        up_sums_ref[x] += jnp.sum(du.astype(f32), axis=0, keepdims=True)
        up.finish(up_pieces, up_ref, up_sems, x)
        term = nt(du, up_ref[x])
        total = term if total is None else total + term
    part_ref[...] = total.astype(bf16)


def run_ffn_backward(chain, grads, entering, params, slope, up, down, last):
    rows, width = entering[0].shape
    step = 256
    units = up.width
    inputs = [*grads, *entering, params, slope, *up.arrays, *down.arrays]
    specs = [by_rows(step, width)] * (len(grads) + 3)
    specs += [fixed(8, width), by_rows_pair(step, units)]
    specs += up.specs(True) + down.specs(True)
    outs = [
        ((rows, width), bf16),
        ((rows, width), f32),
        ((2, rows, units), bf16),
        ((rows, width), bf16),
        ((8, width), f32),
        ((2, 1, units), f32),
    ]
    out_specs = [by_rows(step, width)] * 2 + [by_rows_pair(step, units), by_rows(step, width)]
    out_specs += [fixed(8, width), fixed(2, 1, units)]
    if last:
        outs.append(((rows, width), bf16))
        out_specs.append(by_rows(step, width))
    return chain.call(
        lambda *refs: ffn_backward(up, down, len(grads), last, refs),
        inputs,
        specs,
        outs,
        out_specs,
        flops=8 * rows * width * units,
        vmem=30,
        grid=(rows // step,),
        scratch=[
            pltpu.VMEM((2, width, units), bf16),
            pltpu.VMEM((2, width, units), bf16),
            pltpu.SemaphoreType.DMA((16,)),
            pltpu.SemaphoreType.DMA((16,)),
        ],
    )


def fold(near):
    within = lax.broadcasted_iota(jnp.int32, (8, TILE), 0)
    lane = lax.broadcasted_iota(jnp.int32, (8, TILE), 1)
    zero = jnp.zeros((8, TILE), f32)

    def aligned(rows, at):
        rows = pltpu.roll(rows, (TILE - at) % TILE, 1)
        for bit in (1, 2, 4):
            rows = jnp.where((within & bit) != 0, pltpu.roll(rows, TILE - bit, 1), rows)
        return rows

    same = after = far_before = far_after = zero
    for at in range(0, TILE, 8):
        upper = within + lane < TILE - at
        one, two, three = (aligned(near[i][at : at + 8], at) for i in (1, 2, 3))
        same += jnp.where(upper, two, one)
        after += jnp.where(upper, three, two)
        far_before += near[0][at : at + 8] + jnp.where(upper, one, zero)
        far_after += near[4][at : at + 8] + jnp.where(upper, zero, three)
    sums = [jnp.sum(v, axis=0, keepdims=True) for v in (same, after, far_before, far_after)]
    return jnp.concatenate([*sums, jnp.zeros((4, TILE), f32)])


def attn_backward(weight, refs):
    n = len(weight.arrays)
    dbh_ref, own_ref, other_ref, ah_ref, prm_ref = refs[:5]
    pieces, refs = refs[5 : 5 + n], refs[5 + n :]
    q_ref, k_ref, v_ref, lse_ref, tiles_ref, mask_ref = refs[:6]
    refs = refs[6:]
    dah_ref, dy_ref, dcat_ref, dqg_ref, part_ref, near_ref, sums_ref, col_ref = refs[:8]
    w_ref, do_ref, dq_ref, dk_ref, dv_ref = refs[8:]
    rows = 2 * SEQ
    gain = prm_ref[0:1]
    sums_ref[...] = jnp.zeros_like(sums_ref)

    def norm(i, carry):
        at = pl.ds(pl.multiple_of(i * 128, 128), 128)
        grad = dbh_ref[at] + own_ref[at].astype(f32) + other_ref[at].astype(f32)
        back, gain_sum, shift_sum = norm_back(ah_ref[at], gain, grad)
        dah_ref[at] = back
        dy_ref[at] = back.astype(bf16)
        sums_ref[0:1] += gain_sum
        sums_ref[1:2] += shift_sum
        sums_ref[2:3] += jnp.sum(back, axis=0, keepdims=True)
        return carry

    lax.fori_loop(0, rows // 128, norm, 0)
    weight.start(pieces, w_ref, None)
    heads = k_ref.shape[0]
    per = heads // 2
    for stream in range(2):
        at = slice(stream * SEQ, (stream + 1) * SEQ)
        for x in range(2):
            block = nn(dy_ref[at], w_ref[x, :, 512:768]).astype(bf16)
            for j in range(per):
                do_ref[stream * heads + x * per + j] = block[:, HEAD * (1 + j) : HEAD * (2 + j)]

    def one_head(head, carry):
        key, value = k_ref[head], v_ref[head]
        grad_key = jnp.zeros((SEQ, HEAD), f32)
        grad_value = jnp.zeros((SEQ, HEAD), f32)
        near = [jnp.zeros((TILE, TILE), f32) for _ in range(NEAR)]
        for half in range(2):
            at = slice(half * 256, half * 256 + 256)
            bias = bias_block(tiles_ref, head, half)
            for stream in range(2):
                spot = stream * heads + head
                query, grad_out = q_ref[spot, at], do_ref[spot, at]
                score = nt(key, query) + (bias + mask_ref[stream, :, at])
                prob = jnp.exp(score - lse_ref[spot, :, at])
                both = prob * nt(value, grad_out)
                inner = jnp.sum(both, axis=0, keepdims=True)
                grad_score = (both - prob * inner).astype(bf16)
                grad_value += nn(prob.astype(bf16), grad_out)
                grad_key += nn(grad_score, query)
                dq_ref[spot, at] = (tn(key, grad_score) * 0.125).T.astype(bf16)
                wide = grad_score.astype(f32)
                for k in range(SEQ // TILE):
                    for q in range(2):
                        which = min(max(k - (2 * half + q), -2), 2) + 2
                        near[which] += wide[
                            k * TILE : (k + 1) * TILE, q * TILE : (q + 1) * TILE
                        ]
        near_ref[head] = fold(near)
        dk_ref[head] = grad_key.astype(bf16)
        dv_ref[head] = grad_value.astype(bf16)
        return carry

    lax.fori_loop(0, heads, one_head, 0)
    total_h = total_g = None
    for x in range(2):
        near = range(x * per, (x + 1) * per)
        blocks = [dq_ref[j] for j in near] + [dk_ref[j] for j in near] + [dv_ref[j] for j in near]
        blocks += [jnp.zeros((SEQ, HEAD), bf16)] * per
        block = jnp.concatenate(blocks, axis=1)
        dcat_ref[x] = block
        term = nt(block, w_ref[x])
        total_h = term if total_h is None else total_h + term
        col_ref[x, 0:1] = jnp.sum(block.astype(f32), axis=0, keepdims=True)
        blocks = [dq_ref[heads + j] for j in near] + [jnp.zeros((SEQ, HEAD), bf16)]
        block = jnp.concatenate(blocks, axis=1)
        dqg_ref[x] = block
        term = nt(block, w_ref[x, :, :256])
        total_g = term if total_g is None else total_g + term
        col_ref[x, 1:2, :256] = jnp.sum(block.astype(f32), axis=0, keepdims=True)
    part_ref[:SEQ] = total_h.astype(bf16)
    part_ref[SEQ:] = total_g.astype(bf16)


def run_attn_backward(chain, entering, params, weight, saved, tiles, mask):
    rows, width = entering[0].shape
    heads = tiles.shape[0]
    columns = weight.width
    q, k, v, _, lse = saved
    inputs = [*entering, params, *weight.arrays, q, k, v, lse, tiles, mask]
    specs = [VMEM] * 5 + weight.specs(False) + [VMEM] * 6
    outs = [
        ((rows, width), f32),
        ((rows, width), bf16),
        ((2, SEQ, columns), bf16),
        ((2, SEQ, 256), bf16),
        ((rows, width), bf16),
        ((heads, 8, TILE), f32),
        ((8, width), f32),
        ((2, 8, columns), f32),
    ]
    return chain.call(
        lambda *refs: attn_backward(weight, refs),
        inputs,
        specs,
        outs,
        [VMEM] * len(outs),
        flops=20 * 10**9,
        vmem=40,
        scratch=[
            pltpu.VMEM((2, width, weight.width), bf16),
            pltpu.VMEM((2 * heads, SEQ, HEAD), bf16),
            pltpu.VMEM((2 * heads, SEQ, HEAD), bf16),
            pltpu.VMEM((heads, SEQ, HEAD), bf16),
            pltpu.VMEM((heads, SEQ, HEAD), bf16),
        ],
    )


def quarters(part, first):
    return [(part, x) for x in range(2)] if first == "y" else [(y, part) for y in range(2)]


def ffn_grads(chain, fed, du, dz, act, part, up_first, down_first):
    rows, width = fed.shape
    units = du.shape[2]
    half = width // 2

    def body(fed_ref, du_ref, dz_ref, act_ref, up_ref, down_ref):
        for left, right, out, first in (
            (fed_ref, du_ref, up_ref, up_first),
            (dz_ref, act_ref, down_ref, down_first),
        ):
            for n, (y, x) in enumerate(quarters(part, first)):
                out[n] = tn(left[:, y * half : (y + 1) * half], right[x]).astype(bf16)

    return chain.call(
        body,
        [fed, du, dz, act],
        [VMEM] * 4,
        [((2, half, units), bf16)] * 2,
        [VMEM] * 2,
        flops=8 * rows * half * units,
        vmem=20,
    )


def attn_grads(chain, x, dcat, dqg, dy, o, part, firsts):
    rows, width = x.shape
    half = width // 2
    columns = dcat.shape[2]
    span = columns // len(firsts)

    def body(x_ref, dcat_ref, dqg_ref, dy_ref, o_ref, *outs):
        for y in range(2):
            at = slice(y * half, (y + 1) * half)
            for n, first in enumerate(firsts):
                for place, (want, other) in enumerate(quarters(part, first)):
                    if want != y:
                        continue
                    low, high = n * span, (n + 1) * span
                    total = tn(x_ref[:SEQ, at], dcat_ref[other, :, low:high])
                    outs[n][place] = total.astype(bf16)
                    if n == 0:
                        query = total[:, :256] + tn(x_ref[SEQ:, at], dqg_ref[other])
                        outs[n][place, :, :256] = query.astype(bf16)
                    if n == len(firsts) - 1:
                        out = total[:, span - 256 :] + tn(dy_ref[:, at], o_ref[other])
                        outs[n][place, :, span - 256 :] = out.astype(bf16)

    return chain.call(
        body,
        [x, dcat, dqg, dy, o],
        [VMEM] * 5,
        [((2, half, span), bf16)] * len(firsts),
        [VMEM] * len(firsts),
        flops=6 * rows * half * columns,
        vmem=20,
    )


def exact(rows, right, product):
    total = None
    for _ in range(3):
        top = rows.astype(bf16)
        rows = rows - top.astype(f32)
        term = product(top, right)
        total = term if total is None else total + term
    return total


SMALL = 8


def finish_rows(chain, core, swapper, fold_hot, groups, smalls):
    rows, width = groups[0][0].shape
    own = rows // 4
    flat = [v for group in groups for v in group]
    counts = [len(group) for group in groups]
    layers = len(smalls) // 5
    heads = smalls[0].shape[0]
    per = heads // 2

    def body(core_ref, swapper_ref, hot_ref, *refs):
        ins, small_ins = refs[: len(flat)], refs[len(flat) : len(flat) + len(smalls)]
        outs = refs[len(flat) + len(smalls) :]
        at = pl.multiple_of(core_ref[0] * own, own)
        first = 0
        for count, out in zip(counts, outs):
            for stream in range(2):
                total = sum(
                    ref[pl.ds(at + stream * SEQ, own)].astype(f32)
                    for ref in ins[first : first + count]
                )
                out[stream] = nt(total.astype(bf16), swapper_ref[...]).astype(bf16)
            first += count
        sides = outs[len(counts) :]
        edge = layers * SMALL
        for layer in range(layers):
            near, cols, one, two, up = small_ins[5 * layer : 5 * layer + 5]
            for x, side in enumerate(sides):
                base = layer * SMALL
                side[base : base + SMALL] = jnp.zeros((SMALL, width), f32)
                side[base : base + 1] = cols[x, 0:1]
                side[base : base + 1, :256] = cols[x, 0:1, :256] + cols[x, 1:2, :256]
                side[base + 1 : base + 2] = up[x]
                for j in range(per):
                    table = None
                    for n in range(4):
                        hot = hot_ref[n * TILE : (n + 1) * TILE]
                        term = exact(near[x * per + j], hot, nn)[n : n + 1]
                        table = term if table is None else table + term
                    side[base + 2 + j : base + 3 + j, :TILE] = table
            sums = jnp.concatenate([one[...], two[...]])
            back = exact(sums, swapper_ref[...], nt)
            for side in sides:
                base = edge + layer * SMALL
                for n in range(3):
                    side[base + 2 * n : base + 2 * n + 1] = back[n : n + 1]
                    side[base + 2 * n + 1 : base + 2 * n + 2] = back[SMALL + n : SMALL + n + 1]
                side[base + 6 : base + 8] = jnp.zeros((2, width), f32)

    shape = ((2 * layers * SMALL, width), f32)
    made = chain.call(
        body,
        [core, swapper, fold_hot, *flat, *smalls],
        [pl.BlockSpec(memory_space=pltpu.SMEM)] + [VMEM] * (2 + len(flat) + len(smalls)),
        [((2, own, width), bf16)] * len(groups) + [shape] * 2,
        [VMEM] * (len(groups) + 2),
        flops=4 * own * width * width * len(groups),
        vmem=24,
    )
    return made[: len(groups)], made[len(groups)], made[len(groups) + 1]


def small_grads(value, part, per):
    layers = value.shape[0] // (2 * SMALL)
    base = [layer * SMALL for layer in range(layers)]
    far = [layers * SMALL + b for b in base]
    return [
        [value[b : b + 1, :part] for b in base],
        [value[b : b + 1, 2 * part : 3 * part] for b in base],
        [value[b + 1 : b + 2] for b in base],
        [value[b + 2 : b + 2 + per, :BUCKETS] for b in base],
        *[[value[b + 2 * n : b + 2 * n + 2] for b in far] for n in range(3)],
    ]


def add_pair(chain, a, b):
    def body(one, two, out):
        out[...] = one[...] + two[...]

    return chain.call(body, [a, b], [VMEM] * 2, [(a.shape, f32)], [VMEM], flops=10**5, vmem=4)[0]


def all_grads(chain, part, per, attn_sums, attn_old, ffn_sums, ffn_old, small):
    groups = [*attn_sums, *ffn_sums]
    depth, units = ffn_old[0].shape
    width = small[0].shape[1]
    layers = 2

    def body(*refs):
        ins, outs = refs[: len(groups) + 6], refs[len(groups) + 6 :]
        attn_refs, rest = ins[: len(attn_sums)], ins[len(attn_sums) :]
        ffn_refs, (low, high, up, down, *more) = rest[: len(ffn_sums)], rest[len(ffn_sums) :]

        def total(of, n):
            return sum(ref[n].astype(f32) for ref in of)

        for layer in range(layers):
            if layer == 0:
                attn = [total(attn_refs, n) for n in range(2)]
                ffn = [total(ffn_refs, n) for n in range(2)]
            else:
                attn, ffn = [low[...], high[...]], [up[...], down[...]]
            outs[0][layer] = attn[0][:, :part]
            outs[1][layer] = attn[0][:, part:]
            outs[2][layer] = attn[1][:, :part]
            outs[3][layer] = attn[1][:, part:].T
            outs[4][layer] = ffn[0]
            outs[5][layer] = ffn[1].T
        one, two = more
        made = small_grads(one[...] + two[...], part, per)
        for n, values in enumerate(made):
            for layer in range(layers):
                if n < 3:
                    outs[6 + n][layer : layer + 1] = values[layer]
                else:
                    outs[6 + n][layer] = values[layer]

    shapes = [(layers, depth, part)] * 3 + [(layers, part, depth), (layers, depth, units)]
    shapes += [(layers, units, depth), (layers, part), (layers, part), (layers, units)]
    shapes += [(layers, per, BUCKETS)] + [(layers, 2, width)] * 3
    return chain.call(
        body,
        [*groups, *attn_old, *ffn_old, *small],
        [VMEM] * (len(groups) + 6),
        [(shape, f32) for shape in shapes],
        [VMEM] * len(shapes),
        flops=10**6,
        vmem=16,
    )


def local(links, *arguments):
    (
        h_in,
        g_in,
        lengths,
        order,
        predicted,
        w_query,
        w_key,
        w_value,
        w_out,
        w_up,
        w_down,
        q_bias,
        v_bias,
        up_bias,
        rel_table,
        norm_gain,
        norm_shift,
        out_bias,
        h_cot,
        g_cot,
    ) = arguments
    rows_own, model = h_in.shape
    part = w_query.shape[2]
    units = w_up.shape[2]
    heads = 2 * rel_table.shape[1]
    table_size = rel_table.shape[1] * BUCKETS
    slot = lax.axis_index("x")
    core = lax.axis_index("core")

    chain = Chain()
    gathered = []
    for layer in range(LAYERS):
        attn = jnp.concatenate(
            [w_query[layer], w_key[layer], w_value[layer], w_out[layer].T], axis=1
        )
        blocks = (attn, w_up[layer], w_down[layer].T)
        if layer < LAYERS - 1:
            gathered.append([links.gather(b, r) for b, r in zip(blocks, GATHER)])
            continue
        gathered.append([links.gather(attn, "zyx"), *links.gather_far(blocks[1:])])

    def pick(v):
        return lax.dynamic_index_in_dim(v, slot, 0, keepdims=False)

    mask = slot_masks(pick(lengths), pick(order), pick(predicted))
    onehot = (
        jnp.arange(BUCKETS, dtype=jnp.int32)[:, None] == tile_buckets().reshape(1, -1)
    ).astype(f32)

    lanes = jnp.arange(TILE, dtype=jnp.int32)
    edge = jnp.full_like(lanes, TILE)
    fold_buckets = bucket_of(jnp.concatenate([-lanes, TILE - lanes, -edge, edge]))
    fold_hot = (fold_buckets[:, None] == lanes[None, :]).astype(bf16)

    small = links.pair(
        jnp.concatenate(
            [q_bias, v_bias, up_bias, rel_table.reshape(LAYERS, table_size)], axis=1
        )
    )
    tables = small[:, :, 2 * part + units :].transpose(1, 0, 2).reshape(LAYERS * heads, BUCKETS)
    tiles = jnp.dot(tables, onehot, precision=highest).reshape(LAYERS, heads, NEAR, TILE, TILE)
    qv = jnp.stack([small[:, :, :part], small[:, :, part : 2 * part]], axis=2)
    qv = jnp.pad(qv, ((0, 0), (0, 0), (0, 6), (0, 256 - part)))
    bias_up = small[:, :, None, 2 * part : 2 * part + units]

    features = links.feature_order(model)
    swapper = (jnp.arange(model, dtype=jnp.int32)[:, None] == features[None, :]).astype(bf16)
    swapper32 = swapper.astype(f32)
    params = jnp.dot(
        jnp.stack([norm_gain, norm_shift, out_bias], axis=2).reshape(-1, model),
        swapper32,
        precision=highest,
    ).reshape(LAYERS, 6, model)
    params = jnp.pad(params, ((0, 0), (0, 2), (0, 0)))

    def ordered(first, second):
        rows = links.both_rows(jnp.concatenate([first, second], axis=1))
        both = jnp.concatenate([rows[:, :model], rows[:, model:]], axis=0)
        return nn(both, swapper).astype(bf16)

    entering = ordered(h_in, g_in)
    kept = []
    for layer in range(LAYERS):
        attn, up, down = gathered[layer]
        if layer == 0:
            x = stream = entering
            before = (entering,)
            after = []
            if links.routed:
                after = [v for w in (up, down, gathered[1][0]) for v in w.arrays]
        else:
            before = (h1, part_own, part_other, params[layer - 1])
            after = []
        made = run_attn_forward(chain, before, attn, qv[:, layer], tiles[layer], mask, after)
        if layer > 0:
            stream, x = made[:2]
            made = made[2:]
        mixed_own, q, k, v, o, lse = made
        ah, h1, fed, act, slope, part_own = run_ffn_forward(
            chain, (stream, mixed_own, links.pc(mixed_own)), params[layer], bias_up[:, layer], up, down
        )
        part_other = links.pc(part_own)
        kept.append((x, (q, k, v, o, lse), ah, (h1, part_own, part_other), fed, act, slope))
    grads = (ordered(h_cot, g_cot),)
    smalls = []
    for layer in range(LAYERS - 1, -1, -1):
        attn, up, down = gathered[layer]
        firsts = [r[0] for r in SCATTER]
        x, saved, ah, second, fed, act, slope = kept[layer]
        last = layer == LAYERS - 1
        made = run_ffn_backward(chain, grads, second, params[layer], slope, up, down, last)
        dz, dbh, du, part_own, sums_two, up_sums = made[:6]
        if last:
            result = made[6]
        part_other = links.pc(part_own)
        if not last:
            ffn_way.third()
            attn_way.second()
        sent = ffn_grads(chain, fed, du, dz, act, 1, *firsts)
        held = ffn_grads(chain, fed, du, dz, act, 0, *firsts)
        if not last:
            ffn_way.fourth()
            attn_way.third()
            old_ffn, old_attn = ffn_way, attn_way
        ffn_way = Scatter(chain, links, list(zip(held, sent, SCATTER)))
        dah, dy, dcat, dqg, part_own, near, sums_one, cols = run_attn_backward(
            chain, (dbh, part_own, part_other, ah), params[layer], attn, saved, tiles[layer], mask
        )
        part_other = links.pc(part_own)
        if not last:
            done_ffn = old_ffn.finish()
            old_attn.fourth()
        ffn_way.second()
        sent = attn_grads(chain, x, dcat, dqg, dy, saved[3], 1, firsts)
        held = attn_grads(chain, x, dcat, dqg, dy, saved[3], 0, firsts)
        attn_way = Scatter(chain, links, list(zip(held, sent, SCATTER)))
        smalls += [near, cols, sums_one, sums_two, up_sums]
        grads = (dah, part_own, part_other)
    smalls = smalls[5:] + smalls[:5]
    final, kept_small, sent_small = finish_rows(
        chain, jnp.full((1,), core, jnp.int32), swapper, fold_hot, [(result,), grads], smalls
    )
    per = heads // 2
    if links.routed:
        other = links.swap(sent_small, "x")
        ffn_way.third()
        attn_way.second()
        value = add_pair(chain, kept_small, other)
        other = links.swap(value, "y")
        ffn_way.fourth()
        attn_way.third()
        value = add_pair(chain, value, other)
        other = links.across(value, 1)
        done_attn = old_attn.finish()
        attn_way.fourth()
        value = add_pair(chain, value, other)
        small = (value, links.across(value, 2))
        owned = all_grads(chain, part, per, attn_way.sums, done_attn, ffn_way.sums, done_ffn, small)
    else:
        done_attn = old_attn.finish()
        attn_sum = jnp.stack([jnp.concatenate(v, axis=1) for v in (attn_way.sums, done_attn)])
        up_sum, down_sum = (jnp.stack([ffn_way.sums[n], done_ffn[n]]) for n in range(2))
        owned = [attn_sum[:, :, n * part : (n + 1) * part] for n in range(4)] + [up_sum, down_sum]
        owned[3] = owned[3].transpose(0, 2, 1)
        owned[5] = owned[5].transpose(0, 2, 1)
        edge = LAYERS * SMALL
        split = lax.psum_scatter(jnp.stack([kept_small[:edge], sent_small[:edge]]), "x")
        value = jnp.concatenate(
            [lax.psum(split, ("z", "y")), lax.psum(kept_small[edge:], ("z", "y", "x"))]
        )
        for n, values in enumerate(small_grads(value, part, per)):
            owned.append(jnp.concatenate(values) if n < 3 else jnp.stack(values))
    return (
        final[0][0],
        final[0][1],
        final[1][0],
        final[1][1],
        *owned,
    )


def solution(mesh):
    links = Links(mesh)
    rows = P(("z", "y", "x", "core"), None)
    by_dp = P(("z", "y"), None)
    wide = P(None, ("z", "y"), ("x", "core"))
    tall = P(None, ("x", "core"), ("z", "y"))
    by_tensor = P(None, ("x", "core"))
    table = P(None, ("x", "core"), None)
    weights = (wide, wide, wide, tall, wide, tall)
    owned = (by_tensor, by_tensor, by_tensor, table, P(), P(), P())
    return jax.shard_map(
        functools.partial(local, links),
        mesh=links.mesh,
        in_specs=(rows, rows, by_dp, by_dp, by_dp) + weights + owned + (rows, rows),
        out_specs=(rows, rows, rows, rows) + weights + owned,
        check_vma=False,
    )
```
